128 devices in a mesh: slab: 8 (over y, core), row: 16 (over x, z).
Axes of the slice: x: 4, y: 4, z: 4, core: 2. Of those that a mesh axis runs over, the one named last changes fastest.
Arguments:
- state_start: float32 [32, 16, 128, 128], P(None, 'slab', 'row'), may hold values from -6 to 6
- viscosity: float32 [16, 128, 128], P('slab', 'row'), may hold values from 0.5 to 2
- forcing: bfloat16 [8, 32, 16, 128, 128], P(None, None, 'slab', 'row'), may hold values from -6 to 6
- target: int32 [8, 16, 2048, 1], P('slab', 'row'), may hold values from 0 to 15; in each aligned block of 2048 rows (0 to 2047, 2048 to 4095, ..., all dimensions but the last counted through in order) at most 256 rows name the same one
Outputs:
- final_state: float32 [32, 16, 128, 128], P(None, 'slab', 'row')
- r_factor: float32 [256, 256], replicated
- basis: float32 [524288, 256], P(('slab', 'row'))
The draws below stay inside these ranges and needn't reach their ends.
Inputs may be any that keep to these rules, and one draw needn't show every extreme that they name: `target`: at most 256 cells of one source device have the same row owner, and in every draw some source device gives exactly 256 cells to one owner.
All inputs are finite; a program needn't handle non-finite values.
Results may differ from the reference program's by a relative error of at most 0.0003.
Values sent between devices are 32-bit elements; how exact they have to be, the bound alone decides.
No kernel may reach another device: no remote copies, remote signals or barrier semaphores. Data moves between devices by JAX's collectives and lax.ppermute only.
A program may use at most 128 MiB of HBM per device.

```python
import math
import jax
import jax.numpy as jnp
import numpy as np

FIELDS = 32
SNAPS = 8
STEPS = 2
CX = 2
CY = 8
NZ = 128
COLS = 256
CELLS_DEV = 2048
CAP = 256
NX = 16
NY = 128
SLOTS = 524288
N_SLAB = 8
N_ROW = 16


def shard_levels(key, shape, shards, low, largest):
    def one(axis_at, blocks):
        steps = jax.random.uniform(jax.random.fold_in(jax.random.fold_in(key, 6), axis_at), (blocks,), jnp.float32, low / len(shards), largest / len(shards))
        return jnp.repeat(jnp.exp(steps), shape[axis_at] // blocks).reshape((-1,) + (1,) * (len(shape) - axis_at - 1))

    factor_of = one(*shards[0])
    for cut in shards[1:]:
        factor_of = factor_of * one(*cut)
    return factor_of


def deal_out(own_key, own, number, rows, count, top, most, slope):
    ranking = jax.random.permutation(own_key, count)
    crowded, common = load_shares(count, rows * top, most, slope, True), load_shares(count, rows * top, most, slope, False)
    places = jnp.arange(count)

    def named(lengths, rotation):
        used = int((lengths > 0).sum())
        fixed = max(1, used // 4)
        moved = fixed + (places - fixed + rotation * (used - fixed)) % max(1, count - fixed)
        return jnp.zeros((count,), jnp.int32).at[ranking[jnp.where(places < fixed, places, moved)]].set(jnp.asarray(lengths, jnp.int32))

    lengths = jnp.where(number % 4 == 0, named(crowded, number // 4), named(common, number - number // 4 - 1))
    mixed = jax.random.permutation(jax.random.fold_in(own, 3), count)
    giver, sink = mixed[0:count // 2 * 2:2], mixed[1:count // 2 * 2:2]
    room = jnp.minimum(lengths[giver] - 1, most - lengths[sink]) // 2
    room = jnp.where((giver == ranking[0]) | (sink == ranking[0]) | (lengths[sink] == 0), 0, jnp.maximum(room, 0))
    moved = jax.random.randint(jax.random.fold_in(own, 4), (count // 2,), 0, 1 << 20) % (room + 1)
    lengths = lengths.at[giver].add(-moved).at[sink].add(moved)
    labels = jnp.searchsorted(jnp.cumsum(lengths), jnp.arange(rows * top), side="right").astype(jnp.int32)
    listing = labels.reshape(top, rows).T
    listing = listing[jax.random.permutation(jax.random.fold_in(own, 1), rows)]
    rotation = jax.random.randint(jax.random.fold_in(own, 2), (rows, 1), 0, top)
    return jnp.take_along_axis(listing, (jnp.arange(top)[None, :] + rotation) % top, axis=1)


def load_shares(number_of, total, limit, lean, full):
    loads = [(1 << 20) // math.isqrt(standing ** lean) + 1 for standing in range(1, number_of + 1)]
    largest = limit if full else min(limit, max(-(-total // number_of), total * loads[0] // sum(loads)))
    least = 1 if total - largest >= number_of - 1 else 0
    given, spare = [largest] + [least] * (number_of - 1), total - largest - least * (number_of - 1)
    while spare > 0:
        movable = [i for i in range(1, number_of) if given[i] < largest] or [i for i in range(1, number_of) if given[i] < limit]
        whole, remaining = sum([loads[i] for i in movable]), spare
        for i in movable:
            addition = min(limit - given[i], max(1, remaining * loads[i] // whole), spare)
            given[i] = given[i] + addition
            spare = spare - addition
    return np.array(given)


def noise(rng, dims, scale, limit, cuts=(), kind=jnp.bfloat16):
    gain = shard_levels(rng, dims, cuts, -0.22, 0.18) if cuts else 1.0
    array = jax.random.normal(rng, dims, jnp.float32) * scale * gain
    return jnp.minimum(jnp.maximum(array, -limit), limit).astype(kind)


def setup_inputs(seed: int = 0) -> dict:
    streams_of = jax.random.split(jax.random.key(seed), 5)
    state_start = noise(streams_of[0], (FIELDS, NX, NY, NZ), 1.0, 6.0, ((1, 8), (2, 16)), jnp.float32)
    viscosity = jnp.clip(jnp.exp(math.log(2.0) - 1.3862944 * jax.random.uniform(streams_of[1], (NX, NY, NZ), jnp.float32) ** shard_levels(streams_of[1], (NX, NY, NZ), ((0, 8), (1, 16)), -0.2, 0.2)), 0.5, 2.0)
    forcing = noise(streams_of[2], (SNAPS, FIELDS, NX, NY, NZ), 1.0, 6.0, ((2, 8), (3, 16)))
    target_keys = jax.random.split(jax.random.fold_in(streams_of[3], 1), N_SLAB * N_ROW * CELLS_DEV // CELLS_DEV)
    target_turns = jax.random.permutation(jax.random.fold_in(streams_of[3], 3), N_SLAB * N_ROW * CELLS_DEV // CELLS_DEV)
    target = jax.vmap(lambda own, number: deal_out(jax.random.fold_in(streams_of[3], 2), own, number, CELLS_DEV, N_ROW, 1, CAP, 2))(target_keys, target_turns).reshape((N_SLAB, N_ROW, CELLS_DEV, 1))
    return {"state_start": state_start, "viscosity": viscosity, "forcing": forcing, "target": target}


step_size = 0.08

def advance(padded, visc_padded):
    center = padded[:, 1:-1, 1:-1]
    visc_mid = visc_padded[1:-1, 1:-1]
    flux_total = 0.5 * (visc_mid + visc_padded[2:, 1:-1]) * (padded[:, 2:, 1:-1] - center)
    flux_total = flux_total + 0.5 * (visc_mid + visc_padded[:-2, 1:-1]) * (padded[:, :-2, 1:-1] - center)
    flux_total = flux_total + 0.5 * (visc_mid + visc_padded[1:-1, 2:]) * (padded[:, 1:-1, 2:] - center)
    flux_total = flux_total + 0.5 * (visc_mid + visc_padded[1:-1, :-2]) * (padded[:, 1:-1, :-2] - center)
    flux_total = flux_total + 0.5 * (visc_mid + jnp.roll(visc_mid, -1, 2)) * (jnp.roll(center, -1, 3) - center)
    flux_total = flux_total + 0.5 * (visc_mid + jnp.roll(visc_mid, 1, 2)) * (jnp.roll(center, 1, 3) - center)
    return center + step_size * flux_total

def reference(state_start, viscosity, forcing, target):
    visc_padded = jnp.pad(viscosity, ((1, 1), (1, 1), (0, 0)))
    fields_now = state_start
    records = []
    for snapshot in range(SNAPS):
        fields_now = fields_now + forcing[snapshot].astype(fields_now.dtype)
        for substep in range(STEPS):
            fields_now = advance(jnp.pad(fields_now, ((0, 0), (1, 1), (1, 1), (0, 0))), visc_padded)
        records.append(fields_now)
    stacked = jnp.stack(records, 0)
    stacked = stacked.reshape(SNAPS, FIELDS, N_SLAB, CX, N_ROW, CY, NZ)
    snapshot_rows = stacked.transpose(2, 4, 3, 5, 6, 0, 1).reshape(N_SLAB * N_ROW * CELLS_DEV, COLS)
    upper = jnp.linalg.qr(snapshot_rows, mode='r')
    diag_signs = jnp.where(jnp.diagonal(upper) < 0, -1.0, 1.0).astype(upper.dtype)
    upper = upper * diag_signs[:, None]
    ortho = jax.scipy.linalg.solve_triangular(upper, snapshot_rows.T, trans=1, lower=False).T
    owners = target[..., 0]
    matches = (owners[..., None] == jnp.arange(N_ROW, dtype=jnp.int32)).astype(jnp.int32)
    earlier = jnp.sum((jnp.cumsum(matches, axis=2) - 1) * matches, axis=-1)
    slab_index = jnp.arange(N_SLAB, dtype=jnp.int32)[:, None, None]
    row_index = jnp.arange(N_ROW, dtype=jnp.int32)[None, :, None]
    slot_rows = ((slab_index * N_ROW + owners) * N_ROW + row_index) * CAP + earlier
    basis = jnp.zeros((SLOTS, COLS), ortho.dtype).at[slot_rows.reshape(-1)].set(ortho)
    return (fields_now, upper, basis)
```

```python
import functools

import jax
import jax.numpy as jnp
from jax import lax
from jax.experimental import pallas as pl
from jax.experimental.pallas import tpu as pltpu
from jax.sharding import Mesh, PartitionSpec as P

SNAPS = 8
STEPS = 2
HALF = SNAPS // 2
DEEP = HALF * STEPS
step_size = 0.08
F32 = jnp.float32
BF16 = jnp.bfloat16
NT = (((1,), (1,)), ((), ()))
NN = (((1,), (0,)), ((), ()))
TN = (((0,), (0,)), ((), ()))


def split(value):
    high = value.astype(BF16)
    return high, (value - high.astype(F32)).astype(BF16)


def exact_dot(left, right, dims):
    return lax.dot_general(
        left, right, dims, precision=lax.Precision.HIGHEST, preferred_element_type=F32
    )


def bf_dot(left, right, dims):
    return lax.dot_general(left, right, dims, preferred_element_type=F32)


def lane_next(value):
    return pltpu.roll(value, value.shape[-1] - 1, value.ndim - 1)


def lane_prev(value):
    return pltpu.roll(value, 1, value.ndim - 1)


def make_coefs(visc, coefs, rows):
    half = 0.5 * step_size
    slab = lax.broadcasted_iota(jnp.int32, (8, 128), 0)

    def row_body(y, carry):
        v0, v1 = visc[y, 0], visc[y, 1]
        pair = half * (v0 + v1)
        up = jnp.where(slab < 7, pltpu.roll(v0, 7, 0), 0.0)
        cross_up = half * (v1 + up)
        down = jnp.where(slab > 0, pltpu.roll(v1, 1, 0), 0.0)
        cross_down = half * (v0 + down)
        for i, v, cross in ((0, v0, cross_down), (1, v1, cross_up)):
            nxt, prv = visc[y + 1, i], visc[y - 1, i]
            z_next = half * (v + lane_next(v))
            z_prev = lane_prev(z_next)
            to_next = half * (v + nxt)
            to_prev = half * (v + prv)
            total = to_next + to_prev + pair + cross + z_next + z_prev
            inside = v > 0.0
            coefs[0, y, i] = jnp.where(inside, 1.0 - total, 0.0)
            coefs[1, y, i] = jnp.where(inside & (nxt > 0.0), to_next, 0.0)
            coefs[2, y, i] = jnp.where(inside, pair, 0.0)
            wall = (slab == 0) if i == 0 else (slab == 7)
            coefs[3, y, i] = jnp.where(inside & ~wall, cross, 0.0)
            coefs[4, y, i] = jnp.where(inside, z_next, 0.0)
            coefs[5, y, i] = jnp.where(inside, z_prev, 0.0)
        return carry

    v0, v1 = visc[0, 0], visc[0, 1]
    for i, v in ((0, v0), (1, v1)):
        nxt = visc[1, i]
        coefs[1, 0, i] = jnp.where((v > 0.0) & (nxt > 0.0), half * (v + nxt), 0.0)
    lax.fori_loop(1, rows - 1, row_body, 0)


def diffuse(source, dest, coefs, low, high):
    def row_body(y, carry):
        u0, u1 = source[y, 0], source[y, 1]
        for i, mine, other in ((0, u0, u1), (1, u1, u0)):
            cross = pltpu.roll(other, 1 if i == 0 else 7, 0)
            total = coefs[0, y, i] * mine + coefs[2, y, i] * other
            total = total + coefs[3, y, i] * cross
            total = total + coefs[1, y, i] * source[y + 1, i]
            total = total + coefs[1, y - 1, i] * source[y - 1, i]
            total = total + coefs[4, y, i] * lane_next(mine)
            total = total + coefs[5, y, i] * lane_prev(mine)
            dest[y, i] = total
        return carry

    lax.fori_loop(low, high, row_body, 0, unroll=2)


def run_steps(fields, forcing, coefs, pieces, own, snaps, records, last):
    rows = own + 2 * snaps * STEPS
    side = snaps * STEPS
    done = 0
    for k in range(snaps):
        first = fields[0]
        if k:

            def add_body(y, carry):
                first[y, 0] = first[y, 0] + forcing[k - 1, y, 0]
                first[y, 1] = first[y, 1] + forcing[k - 1, y, 1]
                return carry

            lax.fori_loop(done, rows - done, add_body, 0, unroll=2)
        for step in range(STEPS):
            done += 1
            diffuse(fields[step % 2], fields[(step + 1) % 2], coefs, done, rows - done)
        for y in range(own):
            z, j = divmod(y, 8)
            for i in range(2):
                value = first[side + y, i]
                records[pl.ds((z * snaps + k) * 16 + i * 8 + j, 8, stride=pieces * snaps * 16), :] = value
                if k == snaps - 1:
                    last[y, i] = value


def collect(main, low, high, blocks, pieces, block, store):
    for i in range(2):
        for j in range(8):
            at = block * 16 + i * 8 + j
            store(j, i, low[pl.ds(at, 8, stride=blocks * 16), :])
            store(8 + 8 * pieces + j, i, high[pl.ds(at, 8, stride=blocks * 16), :])
            for z in range(pieces):
                start = (z * blocks + block) * 16 + i * 8 + j
                store(8 + 8 * z + j, i, main[pl.ds(start, 8, stride=pieces * blocks * 16), :])


def first_kernel(pieces, snaps, edge, main, low, high, records, last, visc_out, buf0, buf1, forcing, coefs):
    own = 8 * pieces
    rows = own + 2 * snaps * STEPS
    blocks = snaps + 1
    has_low = jnp.where(edge[0] > 0, 1.0, 0.0)
    has_high = jnp.where(edge[1] > 0, 1.0, 0.0)

    def put_visc(y, i, value):
        if y < 8:
            value = value * has_low
        elif y >= 8 + own:
            value = value * has_high
        visc_out[y, i] = value

    collect(main, low, high, blocks, pieces, 0, put_visc)

    def put_start(y, i, value):
        buf0[y, i] = value

    collect(main, low, high, blocks, pieces, 1, put_start)
    for k in range(1, snaps):

        def put_force(y, i, value, k=k):
            forcing[k - 1, y, i] = value

        collect(main, low, high, blocks, pieces, k + 1, put_force)
    make_coefs(visc_out, coefs, rows)
    run_steps((buf0, buf1), forcing, coefs, pieces, own, snaps, records, last)


def second_kernel(pieces, snaps, main, low, high, start, start_low, start_high, visc, records, last, buf0, buf1, forcing, coefs):
    own = 8 * pieces
    rows = own + 2 * snaps * STEPS
    blocks = snaps

    def put_start(y, i, value):
        if y < 8:
            buf0[y, i] = value + start_low[y, i]
        elif y >= 8 + own:
            buf0[y, i] = value + start_high[y - 8 - own, i]
        else:
            buf0[y, i] = value + start[y - 8, i]

    collect(main, low, high, blocks, pieces, 0, put_start)
    for k in range(1, snaps):

        def put_force(y, i, value, k=k):
            forcing[k - 1, y, i] = value

        collect(main, low, high, blocks, pieces, k, put_force)
    make_coefs(visc, coefs, rows)
    run_steps((buf0, buf1), forcing, coefs, pieces, own, snaps, records, last)


VMEM = pl.BlockSpec(memory_space=pltpu.VMEM)
SMEM = pl.BlockSpec(memory_space=pltpu.SMEM)


def params(size=48):
    return pltpu.CompilerParams(vmem_limit_bytes=size * 1024 * 1024)


def step_scratch(rows, snaps):
    return [
        pltpu.VMEM((rows, 2, 8, 128), F32),
        pltpu.VMEM((rows, 2, 8, 128), F32),
        pltpu.VMEM((snaps - 1, rows, 2, 8, 128), F32),
        pltpu.VMEM((6, rows, 2, 8, 128), F32),
    ]


def first_half(edge, main, low, high, pieces, snaps):
    rows = 8 * pieces + 2 * snaps * STEPS
    return pl.pallas_call(
        functools.partial(first_kernel, pieces, snaps),
        out_shape=(
            jax.ShapeDtypeStruct((8 * pieces * snaps * 16, 128), F32),
            jax.ShapeDtypeStruct((8 * pieces, 2, 8, 128), F32),
            jax.ShapeDtypeStruct((rows, 2, 8, 128), F32),
        ),
        in_specs=[SMEM, VMEM, VMEM, VMEM],
        out_specs=(VMEM, VMEM, VMEM),
        scratch_shapes=step_scratch(rows, snaps),
        compiler_params=params(),
        name="diffuse_first",
    )(edge, main, low, high)


def second_half(main, low, high, start, start_low, start_high, visc, pieces, snaps):
    rows = 8 * pieces + 2 * snaps * STEPS
    return pl.pallas_call(
        functools.partial(second_kernel, pieces, snaps),
        out_shape=(
            jax.ShapeDtypeStruct((8 * pieces * snaps * 16, 128), F32),
            jax.ShapeDtypeStruct((8 * pieces, 2, 8, 128), F32),
        ),
        in_specs=[VMEM] * 7,
        out_specs=(VMEM, VMEM),
        scratch_shapes=step_scratch(rows, snaps),
        compiler_params=params(),
        name="diffuse_second",
    )(main, low, high, start, start_low, start_high, visc)


def prep_kernel(fields, snaps, count, *refs):
    rec = refs[0]
    before = refs[1 : 1 + 2 * count]
    high_out, low_out = refs[1 + 2 * count : 3 + 2 * count]
    gram = refs[3 + 2 * count]
    for cell_row in range(16):
        for s in range(snaps):
            for f in range(0, fields, 16):
                parts = [
                    rec[pl.ds(((f + g) * snaps + s) * 16 + cell_row, 8, stride=snaps * 16), :]
                    for g in (0, 8)
                ]
                high, low = split(jnp.concatenate(parts, 0))
                at = (slice(s * fields + f, s * fields + f + 16), slice(cell_row * 128, cell_row * 128 + 128))
                high_out[at] = high
                low_out[at] = low
    high, low = high_out[...], low_out[...]
    width = fields * snaps
    pairs = [(before[2 * c], before[2 * c + 1]) for c in range(count)] + [(high_out, low_out)]
    for c, (other_high, other_low) in enumerate(pairs):
        oh, ol = other_high[...], other_low[...]
        block = bf_dot(high, oh, NT) + (bf_dot(high, ol, NT) + bf_dot(low, oh, NT))
        gram[:, c * width : (c + 1) * width] = block


def prep(rec, before, fields, snaps):
    width = fields * snaps
    cells = 2048
    return pl.pallas_call(
        functools.partial(prep_kernel, fields, snaps, len(before) // 2),
        out_shape=(
            jax.ShapeDtypeStruct((width, cells), BF16),
            jax.ShapeDtypeStruct((width, cells), BF16),
            jax.ShapeDtypeStruct((width, width * (len(before) // 2 + 1)), F32),
        ),
        in_specs=[VMEM] * (1 + len(before)),
        out_specs=(VMEM,) * 3,
        compiler_params=params(),
        name="gram_blocks",
    )(rec, *before)


def rank_kernel(owner_count, owners, hot):
    own = owners[...]
    rows = own.shape[0]
    total = owner_count * rows
    stacked = jnp.concatenate(
        [jnp.where(own == o, 1.0, 0.0).astype(F32) for o in range(owner_count)], 0
    )
    ones = stacked.astype(BF16)
    before = lax.broadcasted_iota(jnp.int32, (128, 128), 0) < lax.broadcasted_iota(jnp.int32, (128, 128), 1)
    inner = bf_dot(ones, jnp.where(before, 1.0, 0.0).astype(BF16), NN)
    sums = bf_dot(ones, jnp.ones((128, 128), BF16), NN).astype(BF16)
    at = lax.broadcasted_iota(jnp.int32, (total, total), 0)
    of = lax.broadcasted_iota(jnp.int32, (total, total), 1)
    lower = (of < at) & (of // rows == at // rows)
    offset = bf_dot(jnp.where(lower, 1.0, 0.0).astype(BF16), sums, NN)
    picked = stacked * (inner + offset)
    rank = picked[0:rows]
    for o in range(1, owner_count):
        rank = rank + picked[o * rows : (o + 1) * rows]
    rank = rank.astype(jnp.int32)
    slot = lax.broadcasted_iota(jnp.int32, (hot.shape[0], 128), 0)
    for r in range(rows):
        hot[:, r * 128 : (r + 1) * 128] = jnp.where(slot == rank[r : r + 1, :], 1.0, 0.0).astype(BF16)


def rank_hot(owners, owner_count, capacity):
    return pl.pallas_call(
        functools.partial(rank_kernel, owner_count),
        out_shape=jax.ShapeDtypeStruct((capacity, owners.size), BF16),
        in_specs=[VMEM],
        out_specs=VMEM,
        compiler_params=params(),
        name="slot_ranks",
    )(owners)


GROUP = 4


def pack_kernel(owners, hot, high, low, out, picked):
    width = high.shape[0]
    base = pl.program_id(0) * GROUP
    own = owners[...]
    rows = own.shape[0]
    for part, source in enumerate((high, low)):
        for g in range(GROUP):
            mask = jnp.where(own == base + g, 1.0, 0.0)
            for r in range(rows):
                cols = slice(r * 128, (r + 1) * 128)
                keep = jnp.broadcast_to(mask[r : r + 1, :], (width, 128)).astype(BF16)
                picked[part, g * width : (g + 1) * width, cols] = source[:, cols] * keep
    sums = bf_dot(picked[0], hot[...], NT) + bf_dot(picked[1], hot[...], NT)
    for g in range(GROUP):
        out[g] = sums[g * width : (g + 1) * width]


def pack(owners, hot, high, low, owner_count):
    width, cells = high.shape
    capacity = hot.shape[0]
    return pl.pallas_call(
        pack_kernel,
        grid=(owner_count // GROUP,),
        out_shape=jax.ShapeDtypeStruct((owner_count, width, capacity), F32),
        in_specs=[VMEM] * 4,
        out_specs=pl.BlockSpec((GROUP, width, capacity), lambda g: (g, 0, 0)),
        scratch_shapes=[pltpu.VMEM((2, GROUP * width, cells), BF16)],
        compiler_params=params(),
        name="pack_slots",
    )(owners, hot, high, low)


BLOCK = 32


def factor_kernel(gram, r_out, inv_out, work):
    order = gram.shape[0]
    work[:, 0:order] = gram[...]
    eye = lax.broadcasted_iota(jnp.int32, (order, order), 0) == lax.broadcasted_iota(jnp.int32, (order, order), 1)
    work[:, order:] = jnp.where(eye, 1.0, 0.0)
    row_at = lax.broadcasted_iota(jnp.int32, (BLOCK, 128), 0)
    lane_at = lax.broadcasted_iota(jnp.int32, (BLOCK, 128), 1)
    for first in range(0, order, BLOCK):
        tile, inner = divmod(first, 128)
        tile *= 128
        on_diag = lane_at == row_at + inner
        part = work[first : first + BLOCK, tile : tile + 128]
        unit = jnp.where(on_diag, 1.0, 0.0)
        for k in range(BLOCK):
            column = part[:, inner + k : inner + k + 1]
            factor = jnp.where(row_at > k, column / part[k : k + 1, inner + k : inner + k + 1], 0.0)
            unit = unit - factor * unit[k : k + 1, :]
            part = part - factor * part[k : k + 1, :]
        pivots = jnp.sum(jnp.where(on_diag, part, 0.0), axis=1, keepdims=True)
        unit = unit / jnp.sqrt(pivots)
        solved = exact_dot(unit, work[tile : tile + 128, :], NN)
        work[first : first + BLOCK, :] = solved
        if first + BLOCK < order:
            change = exact_dot(solved[:, 0:order], solved, TN)
            work[first + BLOCK :, :] = work[first + BLOCK :, :] - change[first + BLOCK :, :]
    keep = lax.broadcasted_iota(jnp.int32, (order, order), 0) <= lax.broadcasted_iota(jnp.int32, (order, order), 1)
    r_out[...] = jnp.where(keep, work[:, 0:order], 0.0)
    inv_out[...] = work[:, order:]


def factor(gram):
    order = gram.shape[0]
    return pl.pallas_call(
        factor_kernel,
        out_shape=(jax.ShapeDtypeStruct((order, order), F32),) * 2,
        in_specs=[VMEM],
        out_specs=(VMEM,) * 2,
        scratch_shapes=[pltpu.VMEM((order, 2 * order), F32)],
        compiler_params=params(),
        name="factor_upper",
    )(gram)


def basis_kernel(inverse, *refs):
    out = refs[-1]
    panel = jnp.concatenate([ref[0] for ref in refs[:-1]], 0).T
    high, low = split(panel)
    inv_high, inv_low = split(inverse[...])
    out[...] = bf_dot(high, inv_high, NT) + (bf_dot(high, inv_low, NT) + bf_dot(low, inv_high, NT))


def basis_of(inverse, panels):
    sources, width, capacity = panels[0].shape
    order = inverse.shape[0]
    return pl.pallas_call(
        basis_kernel,
        grid=(sources,),
        out_shape=jax.ShapeDtypeStruct((sources * capacity, order), F32),
        in_specs=[pl.BlockSpec((order, order), lambda b: (0, 0))]
        + [pl.BlockSpec((1, width, capacity), lambda b: (b, 0, 0)) for _ in panels],
        out_specs=pl.BlockSpec((capacity, order), lambda b: (b, 0)),
        compiler_params=params(),
        name="basis_rows",
    )(inverse, *panels)


def ring(size, shift):
    return [(i, (i + shift) % size) for i in range(size)]


def reduced(value):
    for axis in ("slab", "z", "x"):
        size = lax.axis_size(axis)
        for level in range(size.bit_length() - 1):
            value = value + lax.ppermute(value, axis, [(i, i ^ 1 << level) for i in range(size)])
    return value


def on_device(state_start, viscosity, forcing, target):
    fields, wide, deep, lanes = state_start.shape
    x_size, pieces = lax.axis_size("x"), lax.axis_size("z")
    owner_count = x_size * pieces
    plane = ("slab", "z")
    capacity = 2 * viscosity.size // owner_count
    owners = target.reshape(wide * deep, lanes)

    def swap(value):
        return lax.all_to_all(value, plane, split_axis=0, concat_axis=0, tiled=True)

    start = state_start + forcing[0].astype(F32)
    visc_blocks = jnp.broadcast_to(viscosity[None, None], (fields, 1, wide, deep, lanes))
    later = jnp.transpose(forcing, (1, 0, 2, 3, 4))
    one = swap(jnp.concatenate([visc_blocks, start[:, None], later[:, 1:HALF].astype(F32)], 1))
    two = swap(later[:, HALF:].astype(F32))
    slabs = fields // pieces

    def edges(value):
        by_row = value.reshape((slabs, pieces) + value.shape[1:])
        low = lax.ppermute(by_row[:, pieces - 1], "x", ring(x_size, 1))
        high = lax.ppermute(by_row[:, 0], "x", ring(x_size, -1))
        return low.reshape(-1, lanes), high.reshape(-1, lanes)

    x_at = lax.axis_index("x")
    edge = jnp.stack([x_at > 0, x_at < x_size - 1]).astype(jnp.int32)
    low_one, high_one = edges(one)
    records_one, middle, visc = first_half(edge, one.reshape(-1, lanes), low_one, high_one, pieces, HALF)
    low_two, high_two = edges(two)
    middle_low = lax.ppermute(middle[-deep:], "x", ring(x_size, 1))
    middle_high = lax.ppermute(middle[:deep], "x", ring(x_size, -1))
    records_two, _ = second_half(
        two.reshape(-1, lanes), low_two, high_two, middle, middle_low, middle_high, visc, pieces, HALF
    )
    block = (fields, HALF, wide, deep, lanes)
    home_one = swap(records_one.reshape(block))
    home_two = swap(records_two.reshape(block))
    hot = rank_hot(owners, owner_count, capacity)
    high_a, low_a, gram_a = prep(home_one.reshape(-1, lanes), (), fields, HALF)
    high_b, low_b, gram_b = prep(home_two.reshape(-1, lanes), (high_a, low_a), fields, HALF)
    panels = [
        lax.all_to_all(pack(owners, hot, high, low, owner_count), ("x", "z"), split_axis=0, concat_axis=0, tiled=True)
        for high, low in ((high_a, low_a), (high_b, low_b))
    ]
    width = fields * HALF
    gram = jnp.concatenate([jnp.concatenate([gram_a, gram_b[:, :width].T], 1), gram_b], 0)
    r_factor, inverse = factor(reduced(gram))
    basis = basis_of(inverse, panels)
    return home_two[:, HALF - 1], r_factor, basis


def solution(mesh):
    slab_size, row_size = mesh.shape["slab"], mesh.shape["row"]
    z_size = 4
    cut = Mesh(mesh.devices.reshape(slab_size, row_size // z_size, z_size), ("slab", "x", "z"))
    row = ("x", "z")
    placed = (
        P(None, "slab", row, None),
        P("slab", row, None),
        P(None, None, "slab", row, None),
        P("slab", row, None, None),
    )
    return jax.shard_map(
        on_device,
        mesh=cut,
        in_specs=placed,
        out_specs=(P(None, "slab", row, None), P(), P(("slab",) + row, None)),
        check_vma=False,
    )
```

```python
import functools

import jax
import jax.numpy as jnp
from jax import lax
from jax.experimental import pallas as pl
from jax.experimental.pallas import tpu as pltpu
from jax.sharding import Mesh, PartitionSpec as P

SNAPS = 8
STEPS = 2
HALF = SNAPS // 2
DEEP = HALF * STEPS
ROWS = 8
step_size = 0.08
F32 = jnp.float32
BF16 = jnp.bfloat16
NT = (((1,), (1,)), ((), ()))
NN = (((1,), (0,)), ((), ()))
TN = (((0,), (0,)), ((), ()))


def split(value):
    high = value.astype(BF16)
    return high, (value - high.astype(F32)).astype(BF16)


def exact_dot(left, right, dims):
    return lax.dot_general(
        left, right, dims, precision=lax.Precision.HIGHEST, preferred_element_type=F32
    )


def bf_dot(left, right, dims):
    return lax.dot_general(left, right, dims, preferred_element_type=F32)


def lane_next(value):
    return pltpu.roll(value, value.shape[-1] - 1, value.ndim - 1)


def lane_prev(value):
    return pltpu.roll(value, 1, value.ndim - 1)


def make_coefs(visc, coefs, rows):
    half = 0.5 * step_size
    slab = lax.broadcasted_iota(jnp.int32, (8, 128), 0)

    def row_body(y, carry):
        v0, v1 = visc[y, 0], visc[y, 1]
        pair = half * (v0 + v1)
        up = jnp.where(slab < 7, pltpu.roll(v0, 7, 0), 0.0)
        cross_up = half * (v1 + up)
        down = jnp.where(slab > 0, pltpu.roll(v1, 1, 0), 0.0)
        cross_down = half * (v0 + down)
        for i, v, cross in ((0, v0, cross_down), (1, v1, cross_up)):
            nxt, prv = visc[y + 1, i], visc[y - 1, i]
            z_next = half * (v + lane_next(v))
            z_prev = lane_prev(z_next)
            to_next = half * (v + nxt)
            to_prev = half * (v + prv)
            total = to_next + to_prev + pair + cross + z_next + z_prev
            inside = v > 0.0
            coefs[0, y, i] = jnp.where(inside, 1.0 - total, 0.0)
            coefs[1, y, i] = jnp.where(inside & (nxt > 0.0), to_next, 0.0)
            coefs[2, y, i] = jnp.where(inside, pair, 0.0)
            wall = (slab == 0) if i == 0 else (slab == 7)
            coefs[3, y, i] = jnp.where(inside & ~wall, cross, 0.0)
            coefs[4, y, i] = jnp.where(inside, z_next, 0.0)
            coefs[5, y, i] = jnp.where(inside, z_prev, 0.0)
        return carry

    v0, v1 = visc[0, 0], visc[0, 1]
    for i, v in ((0, v0), (1, v1)):
        nxt = visc[1, i]
        coefs[1, 0, i] = jnp.where((v > 0.0) & (nxt > 0.0), half * (v + nxt), 0.0)
    lax.fori_loop(1, rows - 1, row_body, 0, unroll=6)


def diffuse(source, dest, coefs, low, high, plus=None):
    def block_body(block, carry):
        base = low + block * ROWS
        u = [[source[base - 1 + r, i] for i in range(2)] for r in range(ROWS + 2)]
        face = [[coefs[1, base - 1 + r, i] for i in range(2)] for r in range(ROWS + 1)]
        for r in range(1, ROWS + 1):
            y = base - 1 + r
            for i in range(2):
                mine, other = u[r][i], u[r][1 - i]
                cross = pltpu.roll(other, 1 if i == 0 else 7, 0)
                total = (coefs[0, y, i] * mine + coefs[2, y, i] * other) + (
                    face[r][i] * u[r + 1][i] + face[r - 1][i] * u[r - 1][i]
                )
                total = total + (
                    (coefs[4, y, i] * lane_next(mine) + coefs[5, y, i] * lane_prev(mine))
                    + coefs[3, y, i] * cross
                )
                dest[y, i] = total
        return carry

    lax.fori_loop(0, (high - low + ROWS - 1) // ROWS, block_body, 0, unroll=True)


def run_steps(fields, forcing, coefs, pieces, own, snaps, records, last):
    rows = own + 2 * snaps * STEPS
    side = snaps * STEPS
    done = 0
    for k in range(snaps):
        first = fields[0]
        if k:

            def add_body(y, carry):
                first[y, 0] = first[y, 0] + forcing[k - 1, y, 0]
                first[y, 1] = first[y, 1] + forcing[k - 1, y, 1]
                return carry

            lax.fori_loop(done, rows - done, add_body, 0, unroll=4)
        for step in range(STEPS):
            done += 1
            diffuse(fields[step % 2], fields[(step + 1) % 2], coefs, done, rows - done)
        for y in range(own):
            z, j = divmod(y, 8)
            for i in range(2):
                value = first[side + y, i]
                records[pl.ds((z * snaps + k) * 16 + i * 8 + j, 8, stride=pieces * snaps * 16), :] = value
                if k == snaps - 1:
                    last[y, i] = value


def collect(main, low, high, blocks, pieces, block, store):
    for i in range(2):
        for j in range(8):
            at = block * 16 + i * 8 + j
            store(j, i, low[pl.ds(at, 8, stride=blocks * 16), :])
            store(8 + 8 * pieces + j, i, high[pl.ds(at, 8, stride=blocks * 16), :])
            for z in range(pieces):
                start = (z * blocks + block) * 16 + i * 8 + j
                store(8 + 8 * z + j, i, main[pl.ds(start, 8, stride=pieces * blocks * 16), :])


def first_kernel(pieces, snaps, edge, main, low, high, records, last, visc_out, buf0, buf1, forcing, coefs):
    own = 8 * pieces
    rows = own + 2 * snaps * STEPS
    blocks = snaps + 1
    has_low = jnp.where(edge[0] > 0, 1.0, 0.0)
    has_high = jnp.where(edge[1] > 0, 1.0, 0.0)

    def put_visc(y, i, value):
        if y < 8:
            value = value * has_low
        elif y >= 8 + own:
            value = value * has_high
        visc_out[y, i] = value

    collect(main, low, high, blocks, pieces, 0, put_visc)

    def put_start(y, i, value):
        buf0[y, i] = value

    collect(main, low, high, blocks, pieces, 1, put_start)
    for k in range(1, snaps):

        def put_force(y, i, value, k=k):
            forcing[k - 1, y, i] = value

        collect(main, low, high, blocks, pieces, k + 1, put_force)
    make_coefs(visc_out, coefs, rows)
    run_steps((buf0, buf1), forcing, coefs, pieces, own, snaps, records, last)


def second_kernel(pieces, snaps, main, low, high, start, start_low, start_high, visc, records, last, buf0, buf1, forcing, coefs):
    own = 8 * pieces
    rows = own + 2 * snaps * STEPS
    blocks = snaps

    def put_start(y, i, value):
        if y < 8:
            buf0[y, i] = value + start_low[y, i]
        elif y >= 8 + own:
            buf0[y, i] = value + start_high[y - 8 - own, i]
        else:
            buf0[y, i] = value + start[y - 8, i]

    collect(main, low, high, blocks, pieces, 0, put_start)
    for k in range(1, snaps):

        def put_force(y, i, value, k=k):
            forcing[k - 1, y, i] = value

        collect(main, low, high, blocks, pieces, k, put_force)
    make_coefs(visc, coefs, rows)
    run_steps((buf0, buf1), forcing, coefs, pieces, own, snaps, records, last)


VMEM = pl.BlockSpec(memory_space=pltpu.VMEM)
SMEM = pl.BlockSpec(memory_space=pltpu.SMEM)


def params(size=48):
    return pltpu.CompilerParams(vmem_limit_bytes=size * 1024 * 1024)


def step_scratch(rows, snaps):
    padded = rows + ROWS
    return [
        pltpu.VMEM((padded, 2, 8, 128), F32),
        pltpu.VMEM((padded, 2, 8, 128), F32),
        pltpu.VMEM((snaps - 1, rows, 2, 8, 128), F32),
        pltpu.VMEM((6, padded, 2, 8, 128), F32),
    ]


def first_half(edge, main, low, high, pieces, snaps):
    rows = 8 * pieces + 2 * snaps * STEPS
    return pl.pallas_call(
        functools.partial(first_kernel, pieces, snaps),
        out_shape=(
            jax.ShapeDtypeStruct((8 * pieces * snaps * 16, 128), F32),
            jax.ShapeDtypeStruct((8 * pieces, 2, 8, 128), F32),
            jax.ShapeDtypeStruct((rows, 2, 8, 128), F32),
        ),
        in_specs=[SMEM, VMEM, VMEM, VMEM],
        out_specs=(VMEM, VMEM, VMEM),
        scratch_shapes=step_scratch(rows, snaps),
        compiler_params=params(),
        name="diffuse_first",
    )(edge, main, low, high)


def second_half(main, low, high, start, start_low, start_high, visc, pieces, snaps):
    rows = 8 * pieces + 2 * snaps * STEPS
    return pl.pallas_call(
        functools.partial(second_kernel, pieces, snaps),
        out_shape=(
            jax.ShapeDtypeStruct((8 * pieces * snaps * 16, 128), F32),
            jax.ShapeDtypeStruct((8 * pieces, 2, 8, 128), F32),
        ),
        in_specs=[VMEM] * 7,
        out_specs=(VMEM, VMEM),
        scratch_shapes=step_scratch(rows, snaps),
        compiler_params=params(),
        name="diffuse_second",
    )(main, low, high, start, start_low, start_high, visc)


def prep_kernel(fields, snaps, count, *refs):
    rec = refs[0]
    before = refs[1 : 1 + 2 * count]
    high_out, low_out = refs[1 + 2 * count : 3 + 2 * count]
    gram = refs[3 + 2 * count]
    for cell_row in range(16):
        for s in range(snaps):
            for f in range(0, fields, 16):
                parts = [
                    rec[pl.ds(((f + g) * snaps + s) * 16 + cell_row, 8, stride=snaps * 16), :]
                    for g in (0, 8)
                ]
                high, low = split(jnp.concatenate(parts, 0))
                at = (slice(s * fields + f, s * fields + f + 16), slice(cell_row * 128, cell_row * 128 + 128))
                high_out[at] = high
                low_out[at] = low
    high, low = high_out[...], low_out[...]
    width = fields * snaps
    pairs = [(before[2 * c], before[2 * c + 1]) for c in range(count)] + [(high_out, low_out)]
    for c, (other_high, other_low) in enumerate(pairs):
        oh, ol = other_high[...], other_low[...]
        block = bf_dot(high, oh, NT) + (bf_dot(high, ol, NT) + bf_dot(low, oh, NT))
        gram[:, c * width : (c + 1) * width] = block


def prep(rec, before, fields, snaps):
    width = fields * snaps
    cells = 2048
    return pl.pallas_call(
        functools.partial(prep_kernel, fields, snaps, len(before) // 2),
        out_shape=(
            jax.ShapeDtypeStruct((width, cells), BF16),
            jax.ShapeDtypeStruct((width, cells), BF16),
            jax.ShapeDtypeStruct((width, width * (len(before) // 2 + 1)), F32),
        ),
        in_specs=[VMEM] * (1 + len(before)),
        out_specs=(VMEM,) * 3,
        compiler_params=params(),
        name="gram_blocks",
    )(rec, *before)


def rank_kernel(owner_count, owners, hot):
    own = owners[...]
    rows = own.shape[0]
    total = owner_count * rows
    stacked = jnp.concatenate(
        [jnp.where(own == o, 1.0, 0.0).astype(F32) for o in range(owner_count)], 0
    )
    ones = stacked.astype(BF16)
    before = lax.broadcasted_iota(jnp.int32, (128, 128), 0) < lax.broadcasted_iota(jnp.int32, (128, 128), 1)
    inner = bf_dot(ones, jnp.where(before, 1.0, 0.0).astype(BF16), NN)
    sums = bf_dot(ones, jnp.ones((128, 128), BF16), NN).astype(BF16)
    at = lax.broadcasted_iota(jnp.int32, (total, total), 0)
    of = lax.broadcasted_iota(jnp.int32, (total, total), 1)
    lower = (of < at) & (of // rows == at // rows)
    offset = bf_dot(jnp.where(lower, 1.0, 0.0).astype(BF16), sums, NN)
    picked = stacked * (inner + offset)
    rank = picked[0:rows]
    for o in range(1, owner_count):
        rank = rank + picked[o * rows : (o + 1) * rows]
    rank = rank.astype(jnp.int32)
    slot = lax.broadcasted_iota(jnp.int32, (hot.shape[0], 128), 0)
    for r in range(rows):
        hot[:, r * 128 : (r + 1) * 128] = jnp.where(slot == rank[r : r + 1, :], 1.0, 0.0).astype(BF16)


def rank_hot(owners, owner_count, capacity):
    return pl.pallas_call(
        functools.partial(rank_kernel, owner_count),
        out_shape=jax.ShapeDtypeStruct((capacity, owners.size), BF16),
        in_specs=[VMEM],
        out_specs=VMEM,
        compiler_params=params(),
        name="slot_ranks",
    )(owners)


GROUP = 4


def pack_kernel(owners, hot, high, low, out, picked):
    width = high.shape[0]
    base = pl.program_id(0) * GROUP
    own = owners[...]
    rows = own.shape[0]
    for part, source in enumerate((high, low)):
        for g in range(GROUP):
            mask = jnp.where(own == base + g, 1.0, 0.0)
            for r in range(rows):
                cols = slice(r * 128, (r + 1) * 128)
                keep = jnp.broadcast_to(mask[r : r + 1, :], (width, 128)).astype(BF16)
                picked[part, g * width : (g + 1) * width, cols] = source[:, cols] * keep
    sums = bf_dot(hot[...], picked[0], NT) + bf_dot(hot[...], picked[1], NT)
    for g in range(GROUP):
        out[g] = sums[:, g * width : (g + 1) * width]


def pack(owners, hot, high, low, owner_count):
    width, cells = high.shape
    capacity = hot.shape[0]
    return pl.pallas_call(
        pack_kernel,
        grid=(owner_count // GROUP,),
        out_shape=jax.ShapeDtypeStruct((owner_count, capacity, width), F32),
        in_specs=[VMEM] * 4,
        out_specs=pl.BlockSpec((GROUP, capacity, width), lambda g: (g, 0, 0)),
        scratch_shapes=[pltpu.VMEM((2, GROUP * width, cells), BF16)],
        compiler_params=params(),
        name="pack_slots",
    )(owners, hot, high, low)


BLOCK = 32


def eliminate(work, order):
    row_at = lax.broadcasted_iota(jnp.int32, (BLOCK, 128), 0)
    lane_at = lax.broadcasted_iota(jnp.int32, (BLOCK, 128), 1)
    for first in range(0, order, BLOCK):
        tile, inner = divmod(first, 128)
        tile *= 128
        on_diag = lane_at == row_at + inner
        part = work[first : first + BLOCK, tile : tile + 128]
        unit = jnp.where(on_diag, 1.0, 0.0)
        for k in range(BLOCK):
            column = part[:, inner + k : inner + k + 1]
            factor = jnp.where(row_at > k, column * (1.0 / part[k : k + 1, inner + k : inner + k + 1]), 0.0)
            unit = unit - factor * unit[k : k + 1, :]
            part = part - factor * part[k : k + 1, :]
        pivots = jnp.sum(jnp.where(on_diag, part, 0.0), axis=1, keepdims=True)
        unit = unit / jnp.sqrt(pivots)
        solved = exact_dot(unit, work[tile : tile + 128, :], NN)
        work[first : first + BLOCK, :] = solved
        if first + BLOCK < order:
            change = exact_dot(solved[:, 0:order], solved, TN)
            work[first + BLOCK :, :] = work[first + BLOCK :, :] - change[first + BLOCK :, :]


def identity(order):
    at = lax.broadcasted_iota(jnp.int32, (order, order), 0)
    return jnp.where(at == lax.broadcasted_iota(jnp.int32, (order, order), 1), 1.0, 0.0)


def upper(value):
    at = lax.broadcasted_iota(jnp.int32, value.shape, 0)
    return jnp.where(at <= lax.broadcasted_iota(jnp.int32, value.shape, 1), value, 0.0)


def lead_kernel(gram, r_out, inv_out, work):
    order = gram.shape[0]
    work[:, 0:order] = gram[...]
    work[:, order:] = identity(order)
    eliminate(work, order)
    r_out[...] = upper(work[:, 0:order])
    inv_out[...] = work[:, order:]


def trail_kernel(gram, lead, lead_inv, r_out, inv_out, work):
    order = lead.shape[0]
    inverse = lead_inv[...]
    cross = exact_dot(inverse, gram[:, 0:order], NT)
    work[:, 0:order] = gram[:, order:] - exact_dot(cross, cross, TN)
    work[:, order:] = identity(order)
    eliminate(work, order)
    zeros = jnp.zeros((order, order), F32)
    own = work[:, order:]
    r_out[0:order, 0:order] = lead[...]
    r_out[0:order, order:] = cross
    r_out[order:, 0:order] = zeros
    r_out[order:, order:] = upper(work[:, 0:order])
    inv_out[0:order, 0:order] = inverse
    inv_out[0:order, order:] = zeros
    inv_out[order:, 0:order] = -exact_dot(own, exact_dot(cross, inverse, TN), NN)
    inv_out[order:, order:] = own


def factor_lead(gram):
    order = gram.shape[0]
    return pl.pallas_call(
        lead_kernel,
        out_shape=(jax.ShapeDtypeStruct((order, order), F32),) * 2,
        in_specs=[VMEM],
        out_specs=(VMEM,) * 2,
        scratch_shapes=[pltpu.VMEM((order, 2 * order), F32)],
        compiler_params=params(),
        name="factor_lead",
    )(gram)


def factor_trail(gram, lead, lead_inv):
    order = lead.shape[0]
    return pl.pallas_call(
        trail_kernel,
        out_shape=(jax.ShapeDtypeStruct((2 * order, 2 * order), F32),) * 2,
        in_specs=[VMEM] * 3,
        out_specs=(VMEM,) * 2,
        scratch_shapes=[pltpu.VMEM((order, 2 * order), F32)],
        compiler_params=params(),
        name="factor_trail",
    )(gram, lead, lead_inv)


SOURCES = 2


def basis_kernel(inverse, *refs):
    out = refs[-1]
    inv_high, inv_low = split(inverse[...])
    for b in range(SOURCES):
        high, low = split(jnp.concatenate([ref[b] for ref in refs[:-1]], 1))
        rows = high.shape[0]
        out[b * rows : (b + 1) * rows, :] = bf_dot(high, inv_high, NT) + (
            bf_dot(high, inv_low, NT) + bf_dot(low, inv_high, NT)
        )


def basis_of(inverse, panels):
    sources, capacity, width = panels[0].shape
    order = inverse.shape[0]
    return pl.pallas_call(
        basis_kernel,
        grid=(sources // SOURCES,),
        out_shape=jax.ShapeDtypeStruct((sources * capacity, order), F32),
        in_specs=[pl.BlockSpec((order, order), lambda b: (0, 0))]
        + [pl.BlockSpec((SOURCES, capacity, width), lambda b: (b, 0, 0)) for _ in panels],
        out_specs=pl.BlockSpec((SOURCES * capacity, order), lambda b: (b, 0)),
        compiler_params=params(),
        name="basis_rows",
    )(inverse, *panels)


def ring(size, shift):
    return [(i, (i + shift) % size) for i in range(size)]


def reduced(value):
    for axis in ("slab", "z", "x"):
        size = lax.axis_size(axis)
        for level in range(size.bit_length() - 1):
            value = value + lax.ppermute(value, axis, [(i, i ^ 1 << level) for i in range(size)])
    return value


def on_device(state_start, viscosity, forcing, target):
    fields, wide, deep, lanes = state_start.shape
    x_size, pieces = lax.axis_size("x"), lax.axis_size("z")
    owner_count = x_size * pieces
    plane = ("slab", "z")
    capacity = 2 * viscosity.size // owner_count
    owners = target.reshape(wide * deep, lanes)

    def swap(value):
        return lax.all_to_all(value, plane, split_axis=0, concat_axis=0, tiled=True)

    start = state_start + forcing[0].astype(F32)
    visc_blocks = jnp.broadcast_to(viscosity[None, None], (fields, 1, wide, deep, lanes))
    later = jnp.transpose(forcing, (1, 0, 2, 3, 4))
    one = swap(jnp.concatenate([visc_blocks, start[:, None], later[:, 1:HALF].astype(F32)], 1))
    two = swap(later[:, HALF:].astype(F32))
    slabs = fields // pieces

    def edges(value):
        by_row = value.reshape((slabs, pieces) + value.shape[1:])
        low = lax.ppermute(by_row[:, pieces - 1], "x", ring(x_size, 1))
        high = lax.ppermute(by_row[:, 0], "x", ring(x_size, -1))
        return low.reshape(-1, lanes), high.reshape(-1, lanes)

    x_at = lax.axis_index("x")
    edge = jnp.stack([x_at > 0, x_at < x_size - 1]).astype(jnp.int32)
    low_one, high_one = edges(one)
    records_one, middle, visc = first_half(edge, one.reshape(-1, lanes), low_one, high_one, pieces, HALF)
    low_two, high_two = edges(two)
    middle_low = lax.ppermute(middle[-deep:], "x", ring(x_size, 1))
    middle_high = lax.ppermute(middle[:deep], "x", ring(x_size, -1))
    records_two, _ = second_half(
        two.reshape(-1, lanes), low_two, high_two, middle, middle_low, middle_high, visc, pieces, HALF
    )
    block = (fields, HALF, wide, deep, lanes)
    home_one = swap(records_one.reshape(block))
    home_two = swap(records_two.reshape(block))
    hot = rank_hot(owners, owner_count, capacity)
    high_a, low_a, gram_a = prep(home_one.reshape(-1, lanes), (), fields, HALF)
    high_b, low_b, gram_b = prep(home_two.reshape(-1, lanes), (high_a, low_a), fields, HALF)
    panels = [
        lax.all_to_all(pack(owners, hot, high, low, owner_count), ("x", "z"), split_axis=0, concat_axis=0, tiled=True)
        for high, low in ((high_a, low_a), (high_b, low_b))
    ]
    lead, lead_inv = factor_lead(reduced(gram_a))
    r_factor, inverse = factor_trail(reduced(gram_b), lead, lead_inv)
    basis = basis_of(inverse, panels)
    return home_two[:, HALF - 1], r_factor, basis


def solution(mesh):
    slab_size, row_size = mesh.shape["slab"], mesh.shape["row"]
    z_size = 4
    cut = Mesh(mesh.devices.reshape(slab_size, row_size // z_size, z_size), ("slab", "x", "z"))
    row = ("x", "z")
    placed = (
        P(None, "slab", row, None),
        P("slab", row, None),
        P(None, None, "slab", row, None),
        P("slab", row, None, None),
    )
    return jax.shard_map(
        on_device,
        mesh=cut,
        in_specs=placed,
        out_specs=(P(None, "slab", row, None), P(), P(("slab",) + row, None)),
        check_vma=False,
    )
```

```python
import functools

import jax
import jax.numpy as jnp
from jax import lax
from jax.experimental import pallas as pl
from jax.experimental.pallas import tpu as pltpu
from jax.sharding import Mesh, PartitionSpec as P

SNAPS = 8
STEPS = 2
HALF = SNAPS // 2
DEEP = HALF * STEPS
ROWS = 8
step_size = 0.08
F32 = jnp.float32
BF16 = jnp.bfloat16
NT = (((1,), (1,)), ((), ()))
NN = (((1,), (0,)), ((), ()))
TN = (((0,), (0,)), ((), ()))


def split(value):
    high = value.astype(BF16)
    return high, (value - high.astype(F32)).astype(BF16)


def exact_dot(left, right, dims):
    return lax.dot_general(
        left, right, dims, precision=lax.Precision.HIGHEST, preferred_element_type=F32
    )


def bf_dot(left, right, dims):
    return lax.dot_general(left, right, dims, preferred_element_type=F32)


def lane_next(value):
    return pltpu.roll(value, value.shape[-1] - 1, value.ndim - 1)


def lane_prev(value):
    return pltpu.roll(value, 1, value.ndim - 1)


def make_coefs(visc, coefs, rows):
    half = 0.5 * step_size
    slab = lax.broadcasted_iota(jnp.int32, (8, 128), 0)

    def row_body(y, carry):
        v0, v1 = visc[y, 0], visc[y, 1]
        pair = half * (v0 + v1)
        up = jnp.where(slab < 7, pltpu.roll(v0, 7, 0), 0.0)
        cross_up = half * (v1 + up)
        down = jnp.where(slab > 0, pltpu.roll(v1, 1, 0), 0.0)
        cross_down = half * (v0 + down)
        for i, v, cross in ((0, v0, cross_down), (1, v1, cross_up)):
            nxt, prv = visc[y + 1, i], visc[y - 1, i]
            z_next = half * (v + lane_next(v))
            z_prev = lane_prev(z_next)
            to_next = half * (v + nxt)
            to_prev = half * (v + prv)
            total = to_next + to_prev + pair + cross + z_next + z_prev
            inside = v > 0.0
            coefs[0, y, i] = jnp.where(inside, 1.0 - total, 0.0)
            coefs[1, y, i] = jnp.where(inside & (nxt > 0.0), to_next, 0.0)
            coefs[2, y, i] = jnp.where(inside, pair, 0.0)
            wall = (slab == 0) if i == 0 else (slab == 7)
            coefs[3, y, i] = jnp.where(inside & ~wall, cross, 0.0)
            coefs[4, y, i] = jnp.where(inside, z_next, 0.0)
            coefs[5, y, i] = jnp.where(inside, z_prev, 0.0)
        return carry

    v0, v1 = visc[0, 0], visc[0, 1]
    for i, v in ((0, v0), (1, v1)):
        nxt = visc[1, i]
        coefs[1, 0, i] = jnp.where((v > 0.0) & (nxt > 0.0), half * (v + nxt), 0.0)
    lax.fori_loop(1, rows - 1, row_body, 0, unroll=6)


def diffuse(source, dest, coefs, low, high, plus=None):
    def block_body(block, carry):
        base = low + block * ROWS
        u = [[source[base - 1 + r, i] for i in range(2)] for r in range(ROWS + 2)]
        face = [[coefs[1, base - 1 + r, i] for i in range(2)] for r in range(ROWS + 1)]
        for r in range(1, ROWS + 1):
            y = base - 1 + r
            for i in range(2):
                mine, other = u[r][i], u[r][1 - i]
                cross = pltpu.roll(other, 1 if i == 0 else 7, 0)
                total = (coefs[0, y, i] * mine + coefs[2, y, i] * other) + (
                    face[r][i] * u[r + 1][i] + face[r - 1][i] * u[r - 1][i]
                )
                total = total + (
                    (coefs[4, y, i] * lane_next(mine) + coefs[5, y, i] * lane_prev(mine))
                    + coefs[3, y, i] * cross
                )
                dest[y, i] = total
        return carry

    lax.fori_loop(0, (high - low + ROWS - 1) // ROWS, block_body, 0, unroll=True)


def run_steps(fields, forcing, coefs, pieces, own, snaps, records, last):
    rows = own + 2 * snaps * STEPS
    side = snaps * STEPS
    done = 0
    for k in range(snaps):
        first = fields[0]
        if k:

            def add_body(y, carry):
                first[y, 0] = first[y, 0] + forcing[k - 1, y, 0]
                first[y, 1] = first[y, 1] + forcing[k - 1, y, 1]
                return carry

            lax.fori_loop(done, rows - done, add_body, 0, unroll=4)
        for step in range(STEPS):
            done += 1
            diffuse(fields[step % 2], fields[(step + 1) % 2], coefs, done, rows - done)
        for y in range(own):
            z, j = divmod(y, 8)
            for i in range(2):
                value = first[side + y, i]
                records[pl.ds((z * snaps + k) * 16 + i * 8 + j, 8, stride=pieces * snaps * 16), :] = value
                if k == snaps - 1:
                    last[y, i] = value


def collect(main, low, high, blocks, pieces, block, store):
    for i in range(2):
        for j in range(8):
            at = block * 16 + i * 8 + j
            store(j, i, low[pl.ds(at, 8, stride=blocks * 16), :])
            store(8 + 8 * pieces + j, i, high[pl.ds(at, 8, stride=blocks * 16), :])
            for z in range(pieces):
                start = (z * blocks + block) * 16 + i * 8 + j
                store(8 + 8 * z + j, i, main[pl.ds(start, 8, stride=pieces * blocks * 16), :])


def first_kernel(pieces, snaps, edge, main, low, high, records, last, visc_out, buf0, buf1, forcing, coefs):
    own = 8 * pieces
    rows = own + 2 * snaps * STEPS
    blocks = snaps + 1
    has_low = jnp.where(edge[0] > 0, 1.0, 0.0)
    has_high = jnp.where(edge[1] > 0, 1.0, 0.0)

    def put_visc(y, i, value):
        if y < 8:
            value = value * has_low
        elif y >= 8 + own:
            value = value * has_high
        visc_out[y, i] = value

    collect(main, low, high, blocks, pieces, 0, put_visc)

    def put_start(y, i, value):
        buf0[y, i] = value

    collect(main, low, high, blocks, pieces, 1, put_start)
    for k in range(1, snaps):

        def put_force(y, i, value, k=k):
            forcing[k - 1, y, i] = value

        collect(main, low, high, blocks, pieces, k + 1, put_force)
    make_coefs(visc_out, coefs, rows)
    run_steps((buf0, buf1), forcing, coefs, pieces, own, snaps, records, last)


def second_kernel(pieces, snaps, main, low, high, start, start_low, start_high, visc, records, last, buf0, buf1, forcing, coefs):
    own = 8 * pieces
    rows = own + 2 * snaps * STEPS
    blocks = snaps

    def put_start(y, i, value):
        if y < 8:
            buf0[y, i] = value + start_low[y, i]
        elif y >= 8 + own:
            buf0[y, i] = value + start_high[y - 8 - own, i]
        else:
            buf0[y, i] = value + start[y - 8, i]

    collect(main, low, high, blocks, pieces, 0, put_start)
    for k in range(1, snaps):

        def put_force(y, i, value, k=k):
            forcing[k - 1, y, i] = value

        collect(main, low, high, blocks, pieces, k, put_force)
    make_coefs(visc, coefs, rows)
    run_steps((buf0, buf1), forcing, coefs, pieces, own, snaps, records, last)


VMEM = pl.BlockSpec(memory_space=pltpu.VMEM)
SMEM = pl.BlockSpec(memory_space=pltpu.SMEM)


def params(size=48):
    return pltpu.CompilerParams(vmem_limit_bytes=size * 1024 * 1024)


def step_scratch(rows, snaps):
    padded = rows + ROWS
    return [
        pltpu.VMEM((padded, 2, 8, 128), F32),
        pltpu.VMEM((padded, 2, 8, 128), F32),
        pltpu.VMEM((snaps - 1, rows, 2, 8, 128), F32),
        pltpu.VMEM((6, padded, 2, 8, 128), F32),
    ]


def first_half(edge, main, low, high, pieces, snaps):
    rows = 8 * pieces + 2 * snaps * STEPS
    return pl.pallas_call(
        functools.partial(first_kernel, pieces, snaps),
        out_shape=(
            jax.ShapeDtypeStruct((8 * pieces * snaps * 16, 128), F32),
            jax.ShapeDtypeStruct((8 * pieces, 2, 8, 128), F32),
            jax.ShapeDtypeStruct((rows, 2, 8, 128), F32),
        ),
        in_specs=[SMEM, VMEM, VMEM, VMEM],
        out_specs=(VMEM, VMEM, VMEM),
        scratch_shapes=step_scratch(rows, snaps),
        compiler_params=params(),
        name="diffuse_first",
    )(edge, main, low, high)


def second_half(main, low, high, start, start_low, start_high, visc, pieces, snaps):
    rows = 8 * pieces + 2 * snaps * STEPS
    return pl.pallas_call(
        functools.partial(second_kernel, pieces, snaps),
        out_shape=(
            jax.ShapeDtypeStruct((8 * pieces * snaps * 16, 128), F32),
            jax.ShapeDtypeStruct((8 * pieces, 2, 8, 128), F32),
        ),
        in_specs=[VMEM] * 7,
        out_specs=(VMEM, VMEM),
        scratch_shapes=step_scratch(rows, snaps),
        compiler_params=params(),
        name="diffuse_second",
    )(main, low, high, start, start_low, start_high, visc)


def prep_kernel(fields, snaps, count, *refs):
    rec = refs[0]
    before = refs[1 : 1 + 2 * count]
    high_out, low_out, gram = refs[-3:]
    for cell_row in range(16):
        for s in range(snaps):
            for f in range(0, fields, 16):
                parts = [
                    rec[pl.ds(((f + g) * snaps + s) * 16 + cell_row, 8, stride=snaps * 16), :]
                    for g in (0, 8)
                ]
                high, low = split(jnp.concatenate(parts, 0))
                at = (slice(s * fields + f, s * fields + f + 16), slice(cell_row * 128, cell_row * 128 + 128))
                high_out[at] = high
                low_out[at] = low
    high, low = high_out[...], low_out[...]
    width = fields * snaps
    pairs = [(before[2 * c], before[2 * c + 1]) for c in range(count)] + [(high_out, low_out)]
    for c, (other_high, other_low) in enumerate(pairs):
        oh, ol = other_high[...], other_low[...]
        block = bf_dot(high, oh, NT) + (bf_dot(high, ol, NT) + bf_dot(low, oh, NT))
        gram[:, c * width : (c + 1) * width] = block


def prep(rec, before, fields, snaps, after=()):
    width = fields * snaps
    cells = 2048
    return pl.pallas_call(
        functools.partial(prep_kernel, fields, snaps, len(before) // 2),
        out_shape=(
            jax.ShapeDtypeStruct((width, cells), BF16),
            jax.ShapeDtypeStruct((width, cells), BF16),
            jax.ShapeDtypeStruct((width, width * (len(before) // 2 + 1)), F32),
        ),
        in_specs=[VMEM] * (1 + len(before)) + [pl.BlockSpec(memory_space=pl.ANY)] * len(after),
        out_specs=(VMEM,) * 3,
        compiler_params=params(),
        name="gram_blocks",
    )(rec, *before, *after)


def rank_kernel(owner_count, owners, hot):
    own = owners[...]
    rows = own.shape[0]
    total = owner_count * rows
    stacked = jnp.concatenate(
        [jnp.where(own == o, 1.0, 0.0).astype(F32) for o in range(owner_count)], 0
    )
    ones = stacked.astype(BF16)
    before = lax.broadcasted_iota(jnp.int32, (128, 128), 0) < lax.broadcasted_iota(jnp.int32, (128, 128), 1)
    inner = bf_dot(ones, jnp.where(before, 1.0, 0.0).astype(BF16), NN)
    sums = bf_dot(ones, jnp.ones((128, 128), BF16), NN).astype(BF16)
    at = lax.broadcasted_iota(jnp.int32, (total, total), 0)
    of = lax.broadcasted_iota(jnp.int32, (total, total), 1)
    lower = (of < at) & (of // rows == at // rows)
    offset = bf_dot(jnp.where(lower, 1.0, 0.0).astype(BF16), sums, NN)
    picked = stacked * (inner + offset)
    rank = picked[0:rows]
    for o in range(1, owner_count):
        rank = rank + picked[o * rows : (o + 1) * rows]
    rank = rank.astype(jnp.int32)
    slot = lax.broadcasted_iota(jnp.int32, (hot.shape[0], 128), 0)
    for r in range(rows):
        hot[:, r * 128 : (r + 1) * 128] = jnp.where(slot == rank[r : r + 1, :], 1.0, 0.0).astype(BF16)


def rank_hot(owners, owner_count, capacity):
    return pl.pallas_call(
        functools.partial(rank_kernel, owner_count),
        out_shape=jax.ShapeDtypeStruct((capacity, owners.size), BF16),
        in_specs=[VMEM],
        out_specs=VMEM,
        compiler_params=params(),
        name="slot_ranks",
    )(owners)


GROUP = 4


def pack_kernel(owners, hot, high, low, *refs):
    out, picked = refs[-2:]
    width = high.shape[0]
    base = pl.program_id(0) * GROUP
    own = owners[...]
    rows = own.shape[0]
    for part, source in enumerate((high, low)):
        for g in range(GROUP):
            mask = jnp.where(own == base + g, 1.0, 0.0)
            for r in range(rows):
                cols = slice(r * 128, (r + 1) * 128)
                keep = jnp.broadcast_to(mask[r : r + 1, :], (width, 128)).astype(BF16)
                picked[part, g * width : (g + 1) * width, cols] = source[:, cols] * keep
    sums = bf_dot(hot[...], picked[0], NT) + bf_dot(hot[...], picked[1], NT)
    for g in range(GROUP):
        out[g] = sums[:, g * width : (g + 1) * width]


def pack(owners, hot, high, low, owner_count, half, slots=None):
    width, cells = high.shape
    capacity = hot.shape[0]
    more = (slots,) if half else ()
    return pl.pallas_call(
        pack_kernel,
        grid=(owner_count // GROUP,),
        out_shape=jax.ShapeDtypeStruct((owner_count, capacity, 2 * width), F32),
        in_specs=[VMEM] * 4 + [pl.BlockSpec(memory_space=pl.ANY)] * len(more),
        out_specs=pl.BlockSpec((GROUP, capacity, width), lambda g: (g, 0, half)),
        scratch_shapes=[pltpu.VMEM((2, GROUP * width, cells), BF16)],
        input_output_aliases={4: 0} if half else {},
        compiler_params=params(),
        cost_estimate=pl.CostEstimate(
            flops=4 * owner_count * capacity * width * cells, bytes_accessed=4 * owner_count * capacity * width, transcendentals=0
        ),
        name="pack_slots",
    )(owners, hot, high, low, *more)


BLOCK = 32


def eliminate(work, order):
    row_at = lax.broadcasted_iota(jnp.int32, (BLOCK, 128), 0)
    lane_at = lax.broadcasted_iota(jnp.int32, (BLOCK, 128), 1)
    for first in range(0, order, BLOCK):
        tile, inner = divmod(first, 128)
        tile *= 128
        on_diag = lane_at == row_at + inner
        part = work[first : first + BLOCK, tile : tile + 128]
        unit = jnp.where(on_diag, 1.0, 0.0)
        for k in range(BLOCK):
            column = part[:, inner + k : inner + k + 1]
            factor = jnp.where(row_at > k, column * (1.0 / part[k : k + 1, inner + k : inner + k + 1]), 0.0)
            unit = unit - factor * unit[k : k + 1, :]
            part = part - factor * part[k : k + 1, :]
        pivots = jnp.sum(jnp.where(on_diag, part, 0.0), axis=1, keepdims=True)
        unit = unit / jnp.sqrt(pivots)
        solved = exact_dot(unit, work[tile : tile + 128, :], NN)
        work[first : first + BLOCK, :] = solved
        if first + BLOCK < order:
            change = exact_dot(solved[:, 0:order], solved, TN)
            work[first + BLOCK :, :] = work[first + BLOCK :, :] - change[first + BLOCK :, :]


def identity(order):
    at = lax.broadcasted_iota(jnp.int32, (order, order), 0)
    return jnp.where(at == lax.broadcasted_iota(jnp.int32, (order, order), 1), 1.0, 0.0)


def upper(value):
    at = lax.broadcasted_iota(jnp.int32, value.shape, 0)
    return jnp.where(at <= lax.broadcasted_iota(jnp.int32, value.shape, 1), value, 0.0)


def lead_kernel(gram, r_out, inv_out, work):
    order = gram.shape[0]
    work[:, 0:order] = gram[...]
    work[:, order:] = identity(order)
    eliminate(work, order)
    r_out[...] = upper(work[:, 0:order])
    inv_out[...] = work[:, order:]


def trail_kernel(gram, lead, lead_inv, r_out, inv_out, work):
    order = lead.shape[0]
    inverse = lead_inv[...]
    cross = exact_dot(inverse, gram[:, 0:order], NT)
    work[:, 0:order] = gram[:, order:] - exact_dot(cross, cross, TN)
    work[:, order:] = identity(order)
    eliminate(work, order)
    zeros = jnp.zeros((order, order), F32)
    own = work[:, order:]
    r_out[0:order, 0:order] = lead[...]
    r_out[0:order, order:] = cross
    r_out[order:, 0:order] = zeros
    r_out[order:, order:] = upper(work[:, 0:order])
    inv_out[0:order, 0:order] = inverse
    inv_out[0:order, order:] = zeros
    inv_out[order:, 0:order] = -exact_dot(own, exact_dot(cross, inverse, TN), NN)
    inv_out[order:, order:] = own


def factor_lead(gram):
    order = gram.shape[0]
    return pl.pallas_call(
        lead_kernel,
        out_shape=(jax.ShapeDtypeStruct((order, order), F32),) * 2,
        in_specs=[VMEM],
        out_specs=(VMEM,) * 2,
        scratch_shapes=[pltpu.VMEM((order, 2 * order), F32)],
        compiler_params=params(),
        name="factor_lead",
    )(gram)


def factor_trail(gram, lead, lead_inv):
    order = lead.shape[0]
    return pl.pallas_call(
        trail_kernel,
        out_shape=(jax.ShapeDtypeStruct((2 * order, 2 * order), F32),) * 2,
        in_specs=[VMEM] * 3,
        out_specs=(VMEM,) * 2,
        scratch_shapes=[pltpu.VMEM((order, 2 * order), F32)],
        compiler_params=params(),
        name="factor_trail",
    )(gram, lead, lead_inv)


SOURCES = 2


def basis_kernel(inverse, panel, out):
    inv_high, inv_low = split(inverse[...])
    for b in range(SOURCES):
        high, low = split(panel[b])
        rows = high.shape[0]
        out[b * rows : (b + 1) * rows, :] = bf_dot(high, inv_high, NT) + (
            bf_dot(high, inv_low, NT) + bf_dot(low, inv_high, NT)
        )


def basis_of(inverse, panel):
    sources, capacity, order = panel.shape
    return pl.pallas_call(
        basis_kernel,
        grid=(sources // SOURCES,),
        out_shape=jax.ShapeDtypeStruct((sources * capacity, order), F32),
        in_specs=[
            pl.BlockSpec((order, order), lambda b: (0, 0)),
            pl.BlockSpec((SOURCES, capacity, order), lambda b: (b, 0, 0)),
        ],
        out_specs=pl.BlockSpec((SOURCES * capacity, order), lambda b: (b, 0)),
        compiler_params=params(),
        name="basis_rows",
    )(inverse, panel)


def ring(size, shift):
    return [(i, (i + shift) % size) for i in range(size)]


def summed(value, *axes):
    for axis in axes:
        size = lax.axis_size(axis)
        for level in range(size.bit_length() - 1):
            value = value + lax.ppermute(value, axis, [(i, i ^ 1 << level) for i in range(size)])
    return value


def on_device(state_start, viscosity, forcing, target):
    fields, wide, deep, lanes = state_start.shape
    x_size, pieces = lax.axis_size("x"), lax.axis_size("z")
    owner_count = x_size * pieces
    plane = ("slab", "z")
    capacity = 2 * viscosity.size // owner_count
    owners = target.reshape(wide * deep, lanes)

    def swap(value):
        return lax.all_to_all(value, plane, split_axis=0, concat_axis=0, tiled=True)

    start = state_start + forcing[0].astype(F32)
    visc_blocks = jnp.broadcast_to(viscosity[None, None], (fields, 1, wide, deep, lanes))
    later = jnp.transpose(forcing, (1, 0, 2, 3, 4))
    one = swap(jnp.concatenate([visc_blocks, start[:, None], later[:, 1:HALF].astype(F32)], 1))
    two = swap(later[:, HALF:].astype(F32))
    slabs = fields // pieces

    def edges(value):
        by_row = value.reshape((slabs, pieces) + value.shape[1:])
        low = lax.ppermute(by_row[:, pieces - 1], "x", ring(x_size, 1))
        high = lax.ppermute(by_row[:, 0], "x", ring(x_size, -1))
        return low.reshape(-1, lanes), high.reshape(-1, lanes)

    x_at = lax.axis_index("x")
    edge = jnp.stack([x_at > 0, x_at < x_size - 1]).astype(jnp.int32)
    low_one, high_one = edges(one)
    records_one, middle, visc = first_half(edge, one.reshape(-1, lanes), low_one, high_one, pieces, HALF)
    low_two, high_two = edges(two)
    middle_low = lax.ppermute(middle[-deep:], "x", ring(x_size, 1))
    middle_high = lax.ppermute(middle[:deep], "x", ring(x_size, -1))
    records_two, _ = second_half(
        two.reshape(-1, lanes), low_two, high_two, middle, middle_low, middle_high, visc, pieces, HALF
    )
    block = (fields, HALF, wide, deep, lanes)
    home_one = swap(records_one.reshape(block))
    home_two = swap(records_two.reshape(block))
    hot = rank_hot(owners, owner_count, capacity)
    high_a, low_a, gram_a = prep(home_one.reshape(-1, lanes), (), fields, HALF)
    part_a = summed(gram_a, "x")
    slots = pack(owners, hot, high_a, low_a, owner_count, 0)
    high_b, low_b, gram_b = prep(home_two.reshape(-1, lanes), (high_a, low_a), fields, HALF, (slots, part_a))
    part_a = summed(part_a, "z")
    part_b = summed(gram_b, "x")
    slots = pack(owners, hot, high_b, low_b, owner_count, 1, slots)
    slots, part_b = lax.optimization_barrier((slots, part_b))
    part_b = summed(part_b, "z")
    slots, part_a, part_b = lax.optimization_barrier((slots, part_a, part_b))
    panel = lax.all_to_all(slots, ("x", "z"), split_axis=0, concat_axis=0, tiled=True)
    lead, lead_inv = factor_lead(summed(part_a, "slab"))
    r_factor, inverse = factor_trail(summed(part_b, "slab"), lead, lead_inv)
    basis = basis_of(inverse, panel)
    return home_two[:, HALF - 1], r_factor, basis


def solution(mesh):
    slab_size, row_size = mesh.shape["slab"], mesh.shape["row"]
    z_size = 4
    cut = Mesh(mesh.devices.reshape(slab_size, row_size // z_size, z_size), ("slab", "x", "z"))
    row = ("x", "z")
    placed = (
        P(None, "slab", row, None),
        P("slab", row, None),
        P(None, None, "slab", row, None),
        P("slab", row, None, None),
    )
    return jax.shard_map(
        on_device,
        mesh=cut,
        in_specs=placed,
        out_specs=(P(None, "slab", row, None), P(), P(("slab",) + row, None)),
        check_vma=False,
    )
```

```python
import functools

import jax
import jax.numpy as jnp
from jax import lax
from jax.experimental import pallas as pl
from jax.experimental.pallas import tpu as pltpu
from jax.sharding import Mesh, PartitionSpec as P

SNAPS = 8
STEPS = 2
HALF = SNAPS // 2
DEEP = HALF * STEPS
ROWS = 8
step_size = 0.08
F32 = jnp.float32
BF16 = jnp.bfloat16
NT = (((1,), (1,)), ((), ()))
NN = (((1,), (0,)), ((), ()))
TN = (((0,), (0,)), ((), ()))


def split(value):
    high = value.astype(BF16)
    return high, (value - high.astype(F32)).astype(BF16)


def exact_dot(left, right, dims):
    return lax.dot_general(
        left, right, dims, precision=lax.Precision.HIGHEST, preferred_element_type=F32
    )


def bf_dot(left, right, dims):
    return lax.dot_general(left, right, dims, preferred_element_type=F32)


def lane_next(value):
    return pltpu.roll(value, value.shape[-1] - 1, value.ndim - 1)


def lane_prev(value):
    return pltpu.roll(value, 1, value.ndim - 1)


def make_coefs(visc, coefs, rows):
    half = 0.5 * step_size
    slab = lax.broadcasted_iota(jnp.int32, (8, 128), 0)

    def row_body(y, carry):
        v0, v1 = visc[y, 0], visc[y, 1]
        pair = half * (v0 + v1)
        up = jnp.where(slab < 7, pltpu.roll(v0, 7, 0), 0.0)
        cross_up = half * (v1 + up)
        down = jnp.where(slab > 0, pltpu.roll(v1, 1, 0), 0.0)
        cross_down = half * (v0 + down)
        for i, v, cross in ((0, v0, cross_down), (1, v1, cross_up)):
            nxt, prv = visc[y + 1, i], visc[y - 1, i]
            z_next = half * (v + lane_next(v))
            z_prev = lane_prev(z_next)
            to_next = half * (v + nxt)
            to_prev = half * (v + prv)
            total = to_next + to_prev + pair + cross + z_next + z_prev
            inside = v > 0.0
            coefs[0, y, i] = jnp.where(inside, 1.0 - total, 0.0)
            coefs[1, y, i] = jnp.where(inside & (nxt > 0.0), to_next, 0.0)
            coefs[2, y, i] = jnp.where(inside, pair, 0.0)
            wall = (slab == 0) if i == 0 else (slab == 7)
            coefs[3, y, i] = jnp.where(inside & ~wall, cross, 0.0)
            coefs[4, y, i] = jnp.where(inside, z_next, 0.0)
            coefs[5, y, i] = jnp.where(inside, z_prev, 0.0)
        return carry

    v0, v1 = visc[0, 0], visc[0, 1]
    for i, v in ((0, v0), (1, v1)):
        nxt = visc[1, i]
        coefs[1, 0, i] = jnp.where((v > 0.0) & (nxt > 0.0), half * (v + nxt), 0.0)
    lax.fori_loop(1, rows - 1, row_body, 0, unroll=6)


def diffuse(source, dest, coefs, low, high, plus=None):
    def block_body(block, carry):
        base = low + block * ROWS
        u = [[source[base - 1 + r, i] for i in range(2)] for r in range(ROWS + 2)]
        face = [[coefs[1, base - 1 + r, i] for i in range(2)] for r in range(ROWS + 1)]
        for r in range(1, ROWS + 1):
            y = base - 1 + r
            for i in range(2):
                mine, other = u[r][i], u[r][1 - i]
                cross = pltpu.roll(other, 1 if i == 0 else 7, 0)
                total = (coefs[0, y, i] * mine + coefs[2, y, i] * other) + (
                    face[r][i] * u[r + 1][i] + face[r - 1][i] * u[r - 1][i]
                )
                total = total + (
                    (coefs[4, y, i] * lane_next(mine) + coefs[5, y, i] * lane_prev(mine))
                    + coefs[3, y, i] * cross
                )
                dest[y, i] = total
        return carry

    lax.fori_loop(0, (high - low + ROWS - 1) // ROWS, block_body, 0, unroll=True)


def run_steps(fields, forcing, coefs, pieces, own, snaps, records, last):
    rows = own + 2 * snaps * STEPS
    side = snaps * STEPS
    done = 0
    for k in range(snaps):
        first = fields[0]
        if k:

            def add_body(y, carry):
                first[y, 0] = first[y, 0] + forcing[k - 1, y, 0]
                first[y, 1] = first[y, 1] + forcing[k - 1, y, 1]
                return carry

            lax.fori_loop(done, rows - done, add_body, 0, unroll=4)
        for step in range(STEPS):
            done += 1
            diffuse(fields[step % 2], fields[(step + 1) % 2], coefs, done, rows - done)
        for y in range(own):
            z, j = divmod(y, 8)
            for i in range(2):
                value = first[side + y, i]
                records[pl.ds((z * snaps + k) * 16 + i * 8 + j, 8, stride=pieces * snaps * 16), :] = value
                if k == snaps - 1:
                    last[y, i] = value


def collect(main, low, high, blocks, pieces, block, store):
    for i in range(2):
        for j in range(8):
            at = block * 16 + i * 8 + j
            store(j, i, low[pl.ds(at, 8, stride=blocks * 16), :])
            store(8 + 8 * pieces + j, i, high[pl.ds(at, 8, stride=blocks * 16), :])
            for z in range(pieces):
                start = (z * blocks + block) * 16 + i * 8 + j
                store(8 + 8 * z + j, i, main[pl.ds(start, 8, stride=pieces * blocks * 16), :])


def first_kernel(pieces, snaps, edge, main, low, high, records, last, visc_out, buf0, buf1, forcing, coefs):
    own = 8 * pieces
    rows = own + 2 * snaps * STEPS
    blocks = snaps + 1
    has_low = jnp.where(edge[0] > 0, 1.0, 0.0)
    has_high = jnp.where(edge[1] > 0, 1.0, 0.0)

    def put_visc(y, i, value):
        if y < 8:
            value = value * has_low
        elif y >= 8 + own:
            value = value * has_high
        visc_out[y, i] = value

    collect(main, low, high, blocks, pieces, 0, put_visc)

    def put_start(y, i, value):
        buf0[y, i] = value

    collect(main, low, high, blocks, pieces, 1, put_start)
    for k in range(1, snaps):

        def put_force(y, i, value, k=k):
            forcing[k - 1, y, i] = value

        collect(main, low, high, blocks, pieces, k + 1, put_force)
    make_coefs(visc_out, coefs, rows)
    run_steps((buf0, buf1), forcing, coefs, pieces, own, snaps, records, last)


def second_kernel(pieces, snaps, main, low, high, start, start_low, start_high, visc, records, last, buf0, buf1, forcing, coefs):
    own = 8 * pieces
    rows = own + 2 * snaps * STEPS
    blocks = snaps

    def put_start(y, i, value):
        if y < 8:
            buf0[y, i] = value + start_low[y, i]
        elif y >= 8 + own:
            buf0[y, i] = value + start_high[y - 8 - own, i]
        else:
            buf0[y, i] = value + start[y - 8, i]

    collect(main, low, high, blocks, pieces, 0, put_start)
    for k in range(1, snaps):

        def put_force(y, i, value, k=k):
            forcing[k - 1, y, i] = value

        collect(main, low, high, blocks, pieces, k, put_force)
    make_coefs(visc, coefs, rows)
    run_steps((buf0, buf1), forcing, coefs, pieces, own, snaps, records, last)


VMEM = pl.BlockSpec(memory_space=pltpu.VMEM)
SMEM = pl.BlockSpec(memory_space=pltpu.SMEM)


def params(size=48):
    return pltpu.CompilerParams(vmem_limit_bytes=size * 1024 * 1024)


def step_scratch(rows, snaps):
    padded = rows + ROWS
    return [
        pltpu.VMEM((padded, 2, 8, 128), F32),
        pltpu.VMEM((padded, 2, 8, 128), F32),
        pltpu.VMEM((snaps - 1, rows, 2, 8, 128), F32),
        pltpu.VMEM((6, padded, 2, 8, 128), F32),
    ]


def first_half(edge, main, low, high, pieces, snaps):
    rows = 8 * pieces + 2 * snaps * STEPS
    return pl.pallas_call(
        functools.partial(first_kernel, pieces, snaps),
        out_shape=(
            jax.ShapeDtypeStruct((8 * pieces * snaps * 16, 128), F32),
            jax.ShapeDtypeStruct((8 * pieces, 2, 8, 128), F32),
            jax.ShapeDtypeStruct((rows, 2, 8, 128), F32),
        ),
        in_specs=[SMEM, VMEM, VMEM, VMEM],
        out_specs=(VMEM, VMEM, VMEM),
        scratch_shapes=step_scratch(rows, snaps),
        compiler_params=params(),
        name="diffuse_first",
    )(edge, main, low, high)


def second_half(main, low, high, start, start_low, start_high, visc, pieces, snaps):
    rows = 8 * pieces + 2 * snaps * STEPS
    return pl.pallas_call(
        functools.partial(second_kernel, pieces, snaps),
        out_shape=(
            jax.ShapeDtypeStruct((8 * pieces * snaps * 16, 128), F32),
            jax.ShapeDtypeStruct((8 * pieces, 2, 8, 128), F32),
        ),
        in_specs=[VMEM] * 7,
        out_specs=(VMEM, VMEM),
        scratch_shapes=step_scratch(rows, snaps),
        compiler_params=params(),
        name="diffuse_second",
    )(main, low, high, start, start_low, start_high, visc)


def prep_kernel(fields, snaps, count, core, *refs):
    rec = refs[0]
    before = refs[1 : 1 + 2 * count]
    high_out, low_out, keep, send, gram = refs[-5:]
    for cell_row in range(16):
        for s in range(snaps):
            for f in range(0, fields, 16):
                parts = [
                    rec[pl.ds(((f + g) * snaps + s) * 16 + cell_row, 8, stride=snaps * 16), :]
                    for g in (0, 8)
                ]
                high, low = split(jnp.concatenate(parts, 0))
                at = (slice(s * fields + f, s * fields + f + 16), slice(cell_row * 128, cell_row * 128 + 128))
                high_out[at] = high
                low_out[at] = low
    high, low = high_out[...], low_out[...]
    width = fields * snaps
    pairs = [(before[2 * c], before[2 * c + 1]) for c in range(count)] + [(high_out, low_out)]
    for c, (other_high, other_low) in enumerate(pairs):
        oh, ol = other_high[...], other_low[...]
        block = bf_dot(high, oh, NT) + (bf_dot(high, ol, NT) + bf_dot(low, oh, NT))
        gram[:, c * width : (c + 1) * width] = block
    half = width // 2
    mine = core[0]
    keep[...] = gram[pl.ds(mine * half, half), :]
    send[...] = gram[pl.ds((1 - mine) * half, half), :]


def prep(core, rec, before, fields, snaps, after=()):
    width = fields * snaps
    cells = 2048
    return pl.pallas_call(
        functools.partial(prep_kernel, fields, snaps, len(before) // 2),
        out_shape=(
            jax.ShapeDtypeStruct((width, cells), BF16),
            jax.ShapeDtypeStruct((width, cells), BF16),
        )
        + (jax.ShapeDtypeStruct((width // 2, width * (len(before) // 2 + 1)), F32),) * 2,
        in_specs=[SMEM] + [VMEM] * (1 + len(before)) + [pl.BlockSpec(memory_space=pl.ANY)] * len(after),
        out_specs=(VMEM,) * 4,
        scratch_shapes=[pltpu.VMEM((width, width * (len(before) // 2 + 1)), F32)],
        compiler_params=params(),
        name="gram_blocks",
    )(core, rec, *before, *after)


def rank_kernel(owner_count, owners, hot):
    own = owners[...]
    rows = own.shape[0]
    total = owner_count * rows
    stacked = jnp.concatenate(
        [jnp.where(own == o, 1.0, 0.0).astype(F32) for o in range(owner_count)], 0
    )
    ones = stacked.astype(BF16)
    before = lax.broadcasted_iota(jnp.int32, (128, 128), 0) < lax.broadcasted_iota(jnp.int32, (128, 128), 1)
    inner = bf_dot(ones, jnp.where(before, 1.0, 0.0).astype(BF16), NN)
    sums = bf_dot(ones, jnp.ones((128, 128), BF16), NN).astype(BF16)
    at = lax.broadcasted_iota(jnp.int32, (total, total), 0)
    of = lax.broadcasted_iota(jnp.int32, (total, total), 1)
    lower = (of < at) & (of // rows == at // rows)
    offset = bf_dot(jnp.where(lower, 1.0, 0.0).astype(BF16), sums, NN)
    picked = stacked * (inner + offset)
    rank = picked[0:rows]
    for o in range(1, owner_count):
        rank = rank + picked[o * rows : (o + 1) * rows]
    rank = rank.astype(jnp.int32)
    slot = lax.broadcasted_iota(jnp.int32, (hot.shape[0], 128), 0)
    for r in range(rows):
        hot[:, r * 128 : (r + 1) * 128] = jnp.where(slot == rank[r : r + 1, :], 1.0, 0.0).astype(BF16)


def rank_hot(owners, owner_count, capacity):
    return pl.pallas_call(
        functools.partial(rank_kernel, owner_count),
        out_shape=jax.ShapeDtypeStruct((capacity, owners.size), BF16),
        in_specs=[VMEM],
        out_specs=VMEM,
        compiler_params=params(),
        name="slot_ranks",
    )(owners)


GROUP = 4


def pack_kernel(first, owners, hot, high, low, *refs):
    out, picked = refs[-2:]
    width = high.shape[0]
    base = (first + pl.program_id(0)) * GROUP
    own = owners[...]
    rows = own.shape[0]
    for part, source in enumerate((high, low)):
        for g in range(GROUP):
            mask = jnp.where(own == base + g, 1.0, 0.0)
            for r in range(rows):
                cols = slice(r * 128, (r + 1) * 128)
                keep = jnp.broadcast_to(mask[r : r + 1, :], (width, 128)).astype(BF16)
                picked[part, g * width : (g + 1) * width, cols] = source[:, cols] * keep
    sums = bf_dot(hot[...], picked[0], NT) + bf_dot(hot[...], picked[1], NT)
    for g in range(GROUP):
        out[g] = sums[:, g * width : (g + 1) * width]


def pack(owners, hot, high, low, owner_count, half, slots=None, part=0, parts=1):
    width, cells = high.shape
    capacity = hot.shape[0]
    more = () if slots is None else (slots,)
    groups = owner_count // GROUP // parts
    first = part * groups
    return pl.pallas_call(
        functools.partial(pack_kernel, first),
        grid=(groups,),
        out_shape=jax.ShapeDtypeStruct((owner_count, capacity, 2 * width), F32),
        in_specs=[VMEM] * 4 + [pl.BlockSpec(memory_space=pl.ANY)] * len(more),
        out_specs=pl.BlockSpec((GROUP, capacity, width), lambda g: (first + g, 0, half)),
        scratch_shapes=[pltpu.VMEM((2, GROUP * width, cells), BF16)],
        input_output_aliases={4: 0} if more else {},
        compiler_params=params(),
        cost_estimate=pl.CostEstimate(
            flops=4 * GROUP * groups * capacity * width * cells,
            bytes_accessed=4 * GROUP * groups * capacity * width,
            transcendentals=0,
        ),
        name="pack_slots",
    )(owners, hot, high, low, *more)


BLOCK = 32


def eliminate(work, order):
    row_at = lax.broadcasted_iota(jnp.int32, (BLOCK, 128), 0)
    lane_at = lax.broadcasted_iota(jnp.int32, (BLOCK, 128), 1)
    for first in range(0, order, BLOCK):
        tile, inner = divmod(first, 128)
        tile *= 128
        on_diag = lane_at == row_at + inner
        part = work[first : first + BLOCK, tile : tile + 128]
        unit = jnp.where(on_diag, 1.0, 0.0)
        for k in range(BLOCK):
            column = part[:, inner + k : inner + k + 1]
            factor = jnp.where(row_at > k, column * (1.0 / part[k : k + 1, inner + k : inner + k + 1]), 0.0)
            unit = unit - factor * unit[k : k + 1, :]
            part = part - factor * part[k : k + 1, :]
        pivots = jnp.sum(jnp.where(on_diag, part, 0.0), axis=1, keepdims=True)
        unit = unit / jnp.sqrt(pivots)
        solved = exact_dot(unit, work[tile : tile + 128, :], NN)
        work[first : first + BLOCK, :] = solved
        if first + BLOCK < order:
            change = exact_dot(solved[:, 0:order], solved, TN)
            work[first + BLOCK :, :] = work[first + BLOCK :, :] - change[first + BLOCK :, :]


def identity(order):
    at = lax.broadcasted_iota(jnp.int32, (order, order), 0)
    return jnp.where(at == lax.broadcasted_iota(jnp.int32, (order, order), 1), 1.0, 0.0)


def upper(value):
    at = lax.broadcasted_iota(jnp.int32, value.shape, 0)
    return jnp.where(at <= lax.broadcasted_iota(jnp.int32, value.shape, 1), value, 0.0)


def joined(core, own, other, whole, width):
    half = own.shape[0]
    mine = core[0]
    whole[pl.ds(mine * half, half), 0:width] = own[...]
    whole[pl.ds((1 - mine) * half, half), 0:width] = other[...]


def lead_kernel(core, own, other, r_out, inv_out, work):
    order = 2 * own.shape[0]
    joined(core, own, other, work, order)
    work[:, order:] = identity(order)
    eliminate(work, order)
    r_out[...] = upper(work[:, 0:order])
    inv_out[...] = work[:, order:]


def trail_kernel(core, own_half, other_half, lead, lead_inv, r_out, inv_out, work, gram):
    order = lead.shape[0]
    joined(core, own_half, other_half, gram, 2 * order)
    inverse = lead_inv[...]
    cross = exact_dot(inverse, gram[:, 0:order], NT)
    work[:, 0:order] = gram[:, order:] - exact_dot(cross, cross, TN)
    work[:, order:] = identity(order)
    eliminate(work, order)
    zeros = jnp.zeros((order, order), F32)
    own = work[:, order:]
    r_out[0:order, 0:order] = lead[...]
    r_out[0:order, order:] = cross
    r_out[order:, 0:order] = zeros
    r_out[order:, order:] = upper(work[:, 0:order])
    inv_out[0:order, 0:order] = inverse
    inv_out[0:order, order:] = zeros
    inv_out[order:, 0:order] = -exact_dot(own, exact_dot(cross, inverse, TN), NN)
    inv_out[order:, order:] = own


def factor_lead(core, own, other):
    order = 2 * own.shape[0]
    return pl.pallas_call(
        lead_kernel,
        out_shape=(jax.ShapeDtypeStruct((order, order), F32),) * 2,
        in_specs=[SMEM, VMEM, VMEM],
        out_specs=(VMEM,) * 2,
        scratch_shapes=[pltpu.VMEM((order, 2 * order), F32)],
        compiler_params=params(),
        name="factor_lead",
    )(core, own, other)


def factor_trail(core, own, other, lead, lead_inv):
    order = lead.shape[0]
    return pl.pallas_call(
        trail_kernel,
        out_shape=(jax.ShapeDtypeStruct((2 * order, 2 * order), F32),) * 2,
        in_specs=[SMEM] + [VMEM] * 4,
        out_specs=(VMEM,) * 2,
        scratch_shapes=[pltpu.VMEM((order, 2 * order), F32)] * 2,
        compiler_params=params(),
        name="factor_trail",
    )(core, own, other, lead, lead_inv)


SOURCES = 8


def basis_kernel(inverse, panel, out):
    inv_high, inv_low = split(inverse[...])
    for b in range(SOURCES):
        high, low = split(panel[b])
        rows = high.shape[0]
        out[b * rows : (b + 1) * rows, :] = bf_dot(high, inv_high, NT) + (
            bf_dot(high, inv_low, NT) + bf_dot(low, inv_high, NT)
        )


def basis_of(inverse, panel):
    sources, capacity, order = panel.shape
    return pl.pallas_call(
        basis_kernel,
        grid=(sources // SOURCES,),
        out_shape=jax.ShapeDtypeStruct((sources * capacity, order), F32),
        in_specs=[
            pl.BlockSpec((order, order), lambda b: (0, 0)),
            pl.BlockSpec((SOURCES, capacity, order), lambda b: (b, 0, 0)),
        ],
        out_specs=pl.BlockSpec((SOURCES * capacity, order), lambda b: (b, 0)),
        compiler_params=params(),
        name="basis_rows",
    )(inverse, panel)


def ring(size, shift):
    return [(i, (i + shift) % size) for i in range(size)]


def swapped(value):
    return lax.ppermute(value, "core", [(0, 1), (1, 0)])


def summed(value, axis, levels):
    size = lax.axis_size(axis)
    for level in levels:
        value = value + lax.ppermute(value, axis, [(i, i ^ 1 << level) for i in range(size)])
    return value


def on_device(state_start, viscosity, forcing, target):
    fields, wide, deep, lanes = state_start.shape
    x_size, pieces = lax.axis_size("x"), lax.axis_size("z")
    owner_count = x_size * pieces
    plane = ("y", "core", "z")
    capacity = 2 * viscosity.size // owner_count
    owners = target.reshape(wide * deep, lanes)

    def swap(value):
        return lax.all_to_all(value, plane, split_axis=0, concat_axis=0, tiled=True)

    start = state_start + forcing[0].astype(F32)
    visc_blocks = jnp.broadcast_to(viscosity[None, None], (fields, 1, wide, deep, lanes))
    later = jnp.transpose(forcing, (1, 0, 2, 3, 4))
    one = swap(jnp.concatenate([visc_blocks, start[:, None], later[:, 1:HALF].astype(F32)], 1))
    two = swap(later[:, HALF:].astype(F32))
    slabs = fields // pieces

    def edges(value):
        by_row = value.reshape((slabs, pieces) + value.shape[1:])
        low = lax.ppermute(by_row[:, pieces - 1], "x", ring(x_size, 1))
        high = lax.ppermute(by_row[:, 0], "x", ring(x_size, -1))
        return low.reshape(-1, lanes), high.reshape(-1, lanes)

    x_at = lax.axis_index("x")
    edge = jnp.stack([x_at > 0, x_at < x_size - 1]).astype(jnp.int32)
    low_one, high_one = edges(one)
    records_one, middle, visc = first_half(edge, one.reshape(-1, lanes), low_one, high_one, pieces, HALF)
    low_two, high_two = edges(two)
    middle_low = lax.ppermute(middle[-deep:], "x", ring(x_size, 1))
    middle_high = lax.ppermute(middle[:deep], "x", ring(x_size, -1))
    records_two, _ = second_half(
        two.reshape(-1, lanes), low_two, high_two, middle, middle_low, middle_high, visc, pieces, HALF
    )
    block = (fields, HALF, wide, deep, lanes)
    home_one = swap(records_one.reshape(block))
    home_two = swap(records_two.reshape(block))
    hot = rank_hot(owners, owner_count, capacity)
    core = lax.axis_index("core").astype(jnp.int32).reshape(1)
    both = (0, 1)
    high_a, low_a, keep_a, send_a = prep(core, home_one.reshape(-1, lanes), (), fields, HALF)
    part_a = summed(keep_a + swapped(send_a), "x", both)
    slots = pack(owners, hot, high_a, low_a, owner_count, 0)
    high_b, low_b, keep_b, send_b = prep(
        core, home_two.reshape(-1, lanes), (high_a, low_a), fields, HALF, (slots, part_a)
    )
    part_b = summed(keep_b + swapped(send_b), "x", (0,))
    slots = pack(owners, hot, high_b, low_b, owner_count, 1, slots, 0, 2)
    slots, part_b = lax.optimization_barrier((slots, part_b))
    part_b = summed(part_b, "x", (1,))
    slots = pack(owners, hot, high_b, low_b, owner_count, 1, slots, 1, 2)
    slots, part_b, part_a = lax.optimization_barrier((slots, part_b, part_a))
    part = summed(jnp.concatenate([part_a, part_b], 1), "z", (0,))
    part = summed(part, "z", (1,))
    slots, part = lax.optimization_barrier((slots, part))
    panel = lax.all_to_all(slots, ("x", "z"), split_axis=0, concat_axis=0, tiled=True)
    part = summed(part, "y", both)
    other = swapped(part)
    width = fields * HALF
    lead, lead_inv = factor_lead(core, part[:, :width], other[:, :width])
    r_factor, inverse = factor_trail(core, part[:, width:], other[:, width:], lead, lead_inv)
    basis = basis_of(inverse, panel)
    return home_two[:, HALF - 1], r_factor, basis


def solution(mesh):
    slab_size, row_size = mesh.shape["slab"], mesh.shape["row"]
    cores, z_size = 2, 4
    axes = (slab_size // cores, cores, row_size // z_size, z_size)
    cut = Mesh(mesh.devices.reshape(axes), ("y", "core", "x", "z"))
    slab, row = ("y", "core"), ("x", "z")
    placed = (
        P(None, slab, row, None),
        P(slab, row, None),
        P(None, None, slab, row, None),
        P(slab, row, None, None),
    )
    return jax.shard_map(
        on_device,
        mesh=cut,
        in_specs=placed,
        out_specs=(P(None, slab, row, None), P(), P(slab + row, None)),
        check_vma=False,
    )
```

```python
import functools

import jax
import jax.numpy as jnp
from jax import lax
from jax.experimental import pallas as pl
from jax.experimental.pallas import tpu as pltpu
from jax.sharding import Mesh, PartitionSpec as P

SNAPS = 8
STEPS = 2
HALF = SNAPS // 2
ROWS = 8
step_size = 0.08
F32 = jnp.float32
BF16 = jnp.bfloat16
NT = (((1,), (1,)), ((), ()))
NN = (((1,), (0,)), ((), ()))
TN = (((0,), (0,)), ((), ()))


def split(value):
    high = value.astype(BF16)
    return high, (value - high.astype(F32)).astype(BF16)


def exact_dot(left, right, dims):
    return lax.dot_general(
        left, right, dims, precision=lax.Precision.HIGHEST, preferred_element_type=F32
    )


def bf_dot(left, right, dims):
    return lax.dot_general(left, right, dims, preferred_element_type=F32)


SIDE = HALF * STEPS
VMEM = pl.BlockSpec(memory_space=pltpu.VMEM)
SMEM = pl.BlockSpec(memory_space=pltpu.SMEM)
HBM = pl.BlockSpec(memory_space=pltpu.HBM)


def params(size=8):
    return pltpu.CompilerParams(vmem_limit_bytes=size * 1024 * 1024)


def lane_next(value):
    return pltpu.roll(value, value.shape[-1] - 1, value.ndim - 1)


def lane_prev(value):
    return pltpu.roll(value, 1, value.ndim - 1)


def reader(main, low, high, heights, pieces):
    blocks = len(heights)
    rows = sum(heights)
    own = 8 * pieces

    def read(block, y, i):
        y -= SIDE
        if 0 <= y < own:
            z, j = divmod(y, 8)
            start = (z * blocks + block) * 16 + i * 8 + j
            return main[pl.ds(start, 8, stride=pieces * blocks * 16), :]
        first = i * rows + sum(heights[:block])
        if y < 0:
            return low[pl.ds(first + heights[block] + y, 8, stride=2 * rows), :]
        return high[pl.ds(first + y - own, 8, stride=2 * rows), :]

    return read


def row_coefs(visc, y, with_rest, store):
    half = 0.5 * step_size
    slab = lax.broadcasted_iota(jnp.int32, (8, 128), 0)
    here = [visc(y, 0), visc(y, 1)]
    if with_rest:
        pair = half * (here[0] + here[1])
        up = jnp.where(slab < 7, pltpu.roll(here[0], 7, 0), 0.0)
        down = jnp.where(slab > 0, pltpu.roll(here[1], 1, 0), 0.0)
        crosses = (half * (here[0] + down), half * (here[1] + up))
    for i in range(2):
        v, nxt = here[i], visc(y + 1, i)
        inside = v > 0.0
        to_next = half * (v + nxt)
        store(1, y, i, jnp.where(inside & (nxt > 0.0), to_next, 0.0))
        if with_rest:
            z_next = half * (v + lane_next(v))
            z_prev = lane_prev(z_next)
            total = to_next + half * (v + visc(y - 1, i)) + pair + crosses[i] + z_next + z_prev
            wall = slab == (0 if i == 0 else 7)
            store(0, y, i, jnp.where(inside, 1.0 - total, 0.0))
            store(2, y, i, jnp.where(inside, pair, 0.0))
            store(3, y, i, jnp.where(inside & ~wall, crosses[i], 0.0))
            store(4, y, i, jnp.where(inside, z_next, 0.0))
            store(5, y, i, jnp.where(inside, z_prev, 0.0))


def own_coefs_kernel(pieces, blocks, main, coefs):
    own = 8 * pieces
    read = reader(main, None, None, (0,) * blocks, pieces)
    cache = {}

    def visc(y, i):
        if (y, i) not in cache:
            cache[y, i] = read(0, y, i)
        return cache[y, i]

    def store(c, y, i, value):
        coefs[c, y - SIDE, i] = value

    for y in range(SIDE + 1, SIDE + own - 1):
        row_coefs(visc, y, True, store)


def edge_coefs(edge_visc, pieces, edge):
    own = 8 * pieces
    cache = {}

    def visc(y, i):
        if (y, i) not in cache:
            cache[y, i] = edge_visc[y if y <= SIDE + 1 else y - own + 4, i]
        return cache[y, i]

    def store(c, y, i, value):
        edge[c, y if y <= SIDE else y - own + 2, i] = value

    for y in range(0, SIDE + 1):
        row_coefs(visc, y, y > 0, store)
    for y in range(SIDE + own - 1, 2 * SIDE + own - 1):
        row_coefs(visc, y, True, store)


def run_steps(read, blocks, fields, own_coefs, edge, pieces, snaps, records, last, kept, sems):
    own = 8 * pieces
    rows = own + 2 * SIDE

    def coef(c, y, i):
        if SIDE < y < SIDE + own - 1:
            return own_coefs[c, y - SIDE, i]
        return edge[c, y if y <= SIDE else y - own + 2, i]

    def diffuse(source, dest, low, high):
        for base in range(low, high, ROWS):
            top = min(base + ROWS, high)
            u = {(y, i): source[y, i] for y in range(base - 1, top + 1) for i in range(2)}
            face = {(y, i): coef(1, y, i) for y in range(base - 1, top) for i in range(2)}
            for y in range(base, top):
                for i in range(2):
                    mine, other = u[y, i], u[y, 1 - i]
                    cross = pltpu.roll(other, 1 if i == 0 else 7, 0)
                    total = (coef(0, y, i) * mine + coef(2, y, i) * other) + (
                        face[y, i] * u[y + 1, i] + face[y - 1, i] * u[y - 1, i]
                    )
                    total = total + (
                        (coef(4, y, i) * lane_next(mine) + coef(5, y, i) * lane_prev(mine))
                        + coef(3, y, i) * cross
                    )
                    dest[y, i] = total

    done = 0
    copies = []
    for k in range(snaps):
        first = fields[0]
        if k:
            for y in range(done, rows - done):
                for i in range(2):
                    first[y, i] = first[y, i] + read(blocks[k], y, i)
        for step in range(STEPS):
            done += 1
            diffuse(fields[step % 2], fields[(step + 1) % 2], done, rows - done)
        for y in range(own):
            z, j = divmod(y, 8)
            for i in range(2):
                value = first[SIDE + y, i]
                kept[pl.ds((z * snaps + k) * 16 + i * 8 + j, 8, stride=pieces * snaps * 16), :] = value
                if last is not None and k == snaps - 1:
                    last[y, i] = value
        blocks_of = (8 * pieces, snaps, 16, 128)
        copies.append(
            pltpu.make_async_copy(
                kept.reshape(*blocks_of).at[:, k], records.at[:, k], sems.at[k]
            )
        )
        copies[-1].start()
    for copy in copies:
        copy.wait()


def first_kernel(
    pieces, heights, around, main, low_from, high_from, own_coefs, records, last, edge_visc, buf0, buf1, kept, sems, edge, low, high, edge_sems
):
    arriving = [
        pltpu.make_async_copy(low_from, low, edge_sems.at[0]),
        pltpu.make_async_copy(high_from, high, edge_sems.at[1]),
    ]
    for copy in arriving:
        copy.start()
    read = reader(main, low, high, heights, pieces)
    has_low = jnp.where(around[0] > 0, 1.0, 0.0)
    has_high = jnp.where(around[1] > 0, 1.0, 0.0)
    own = 8 * pieces
    for y in range(SIDE, SIDE + own):
        for i in range(2):
            buf0[y, i] = read(1, y, i)
    for copy in arriving:
        copy.wait()
    for y in list(range(SIDE)) + list(range(SIDE + own, own + 2 * SIDE)):
        for i in range(2):
            buf0[y, i] = read(1, y, i)
    for y in list(range(SIDE + 2)) + list(range(SIDE + own - 2, own + 2 * SIDE)):
        for i in range(2):
            value = read(0, y, i)
            if y < SIDE:
                value = value * has_low
            elif y >= SIDE + own:
                value = value * has_high
            edge_visc[y if y <= SIDE + 1 else y - own + 4, i] = value
    edge_coefs(edge_visc, pieces, edge)
    snaps = len(heights) - 1
    run_steps(read, range(1, snaps + 1), (buf0, buf1), own_coefs, edge, pieces, snaps, records, last, kept, sems)


def second_kernel(pieces, heights, main, low, high, start, start_low, start_high, own_coefs, edge_visc, records, buf0, buf1, kept, sems, edge):
    read = reader(main, low, high, heights, pieces)
    own = 8 * pieces
    for y in range(own + 2 * SIDE):
        for i in range(2):
            if y < SIDE:
                before = start_low[y, i]
            elif y >= SIDE + own:
                before = start_high[y - SIDE - own, i]
            else:
                before = start[y - SIDE, i]
            buf0[y, i] = before + read(0, y, i)
    edge_coefs(edge_visc, pieces, edge)
    snaps = len(heights)
    run_steps(read, range(snaps), (buf0, buf1), own_coefs, edge, pieces, snaps, records, None, kept, sems)


def own_coefs_of(main, pieces, blocks):
    return pl.pallas_call(
        functools.partial(own_coefs_kernel, pieces, blocks),
        out_shape=jax.ShapeDtypeStruct((6, 8 * pieces, 2, 8, 128), F32),
        in_specs=[VMEM],
        out_specs=VMEM,
        compiler_params=params(4),
        name="own_coefficients",
    )(main)


def buffers(pieces, snaps):
    return [pltpu.VMEM((8 * pieces + 2 * SIDE, 2, 8, 128), F32)] * 2 + [
        pltpu.VMEM((8 * pieces * snaps * 16, 128), F32),
        pltpu.SemaphoreType.DMA((snaps,)),
        pltpu.VMEM((6, 2 * SIDE + 2, 2, 8, 128), F32),
    ]


def first_half(around, main, low, high, own_coefs, pieces, heights):
    snaps = len(heights) - 1
    return pl.pallas_call(
        functools.partial(first_kernel, pieces, heights),
        out_shape=(
            jax.ShapeDtypeStruct((8 * pieces, snaps, 16, 128), F32),
            jax.ShapeDtypeStruct((8 * pieces, 2, 8, 128), F32),
            jax.ShapeDtypeStruct((2 * SIDE + 4, 2, 8, 128), F32),
        ),
        in_specs=[SMEM, VMEM, HBM, HBM, VMEM],
        out_specs=(HBM, VMEM, VMEM),
        scratch_shapes=buffers(pieces, snaps)
        + [pltpu.VMEM(low.shape, F32), pltpu.VMEM(high.shape, F32), pltpu.SemaphoreType.DMA((2,))],
        compiler_params=params(6),
        name="diffuse_first",
    )(around, main, low, high, own_coefs)


def second_half(main, low, high, start, start_low, start_high, own_coefs, edge, pieces, heights):
    snaps = len(heights)
    return pl.pallas_call(
        functools.partial(second_kernel, pieces, heights),
        out_shape=jax.ShapeDtypeStruct((8 * pieces, snaps, 16, 128), F32),
        in_specs=[VMEM] * 8,
        out_specs=HBM,
        scratch_shapes=buffers(pieces, snaps),
        compiler_params=params(6),
        name="diffuse_second",
    )(main, low, high, start, start_low, start_high, own_coefs, edge)


def edge_kernel(pieces, heights, main, last_rows, first_rows):
    blocks, rows = len(heights), sum(heights)
    for a in range(8):
        for i in range(2):
            at = (a * 2 + i) * rows
            for k, height in enumerate(heights):
                first = (a * pieces * blocks + k) * 16 + i * 8
                last = first + (pieces - 1) * blocks * 16
                first_rows[at : at + height, :] = main[first : first + height, :]
                last_rows[at : at + height, :] = main[last + 8 - height : last + 8, :]
                at += height


def edges_of(main, pieces, heights):
    return pl.pallas_call(
        functools.partial(edge_kernel, pieces, heights),
        out_shape=(jax.ShapeDtypeStruct((16 * sum(heights), 128), F32),) * 2,
        in_specs=[VMEM],
        out_specs=(VMEM,) * 2,
        compiler_params=params(4),
        name="edge_rows",
    )(main)


def opening_kernel(visc_from, start_from, forcing_from, out_to, visc, start, forcing, out, in_sems, out_sems):
    snaps, fields = forcing.shape[:2]
    arriving = [
        pltpu.make_async_copy(visc_from, visc, in_sems.at[snaps + 1]),
        pltpu.make_async_copy(start_from, start, in_sems.at[snaps]),
    ]
    arriving += [pltpu.make_async_copy(forcing_from.at[k], forcing.at[k], in_sems.at[k]) for k in range(snaps)]
    for copy in arriving:
        copy.start()
    leaving = [
        pltpu.make_async_copy(out.at[:, k], out_to.at[:, k], out_sems.at[k]) for k in range(snaps + 1)
    ]
    arriving[0].wait()
    value = visc[...]
    for f in range(fields):
        out[f, 0] = value
    leaving[0].start()
    arriving[1].wait()
    for k in range(snaps):
        arriving[2 + k].wait()
        for f in range(fields):
            value = forcing[k, f].astype(F32)
            out[f, k + 1] = value + start[f] if k == 0 else value
        leaving[k + 1].start()
    for copy in leaving:
        copy.wait()


def opening(visc, start, forcing, snaps):
    fields = start.shape[0]
    cells = start.shape[1:]
    return pl.pallas_call(
        opening_kernel,
        out_shape=jax.ShapeDtypeStruct((fields, snaps + 1) + cells, F32),
        in_specs=[HBM] * 3,
        out_specs=HBM,
        scratch_shapes=[
            pltpu.VMEM(cells, F32),
            pltpu.VMEM(start.shape, F32),
            pltpu.VMEM((snaps,) + forcing.shape[1:], forcing.dtype),
            pltpu.VMEM((fields, snaps + 1) + cells, F32),
            pltpu.SemaphoreType.DMA((snaps + 2,)),
            pltpu.SemaphoreType.DMA((snaps + 1,)),
        ],
        compiler_params=params(60),
        name="opening_blocks",
    )(visc, start, forcing)


def prep_kernel(fields, snaps, count, core, *refs):
    rec = refs[0]
    before = refs[1 : 1 + 2 * count]
    high_out, low_out, keep, send, gram = refs[-5:]
    for cell_row in range(16):
        for s in range(snaps):
            for f in range(0, fields, 16):
                parts = [
                    rec[pl.ds(((f + g) * snaps + s) * 16 + cell_row, 8, stride=snaps * 16), :]
                    for g in (0, 8)
                ]
                high, low = split(jnp.concatenate(parts, 0))
                at = (slice(s * fields + f, s * fields + f + 16), slice(cell_row * 128, cell_row * 128 + 128))
                high_out[at] = high
                low_out[at] = low
    high, low = high_out[...], low_out[...]
    width = fields * snaps
    pairs = [(before[2 * c], before[2 * c + 1]) for c in range(count)] + [(high_out, low_out)]
    for c, (other_high, other_low) in enumerate(pairs):
        oh, ol = other_high[...], other_low[...]
        block = bf_dot(high, oh, NT) + (bf_dot(high, ol, NT) + bf_dot(low, oh, NT))
        gram[:, c * width : (c + 1) * width] = block
    half = width // 2
    mine = core[0]
    keep[...] = gram[pl.ds(mine * half, half), :]
    send[...] = gram[pl.ds((1 - mine) * half, half), :]


def prep(core, rec, before, fields, snaps):
    width = fields * snaps
    cells = 2048
    return pl.pallas_call(
        functools.partial(prep_kernel, fields, snaps, len(before) // 2),
        out_shape=(
            jax.ShapeDtypeStruct((width, cells), BF16),
            jax.ShapeDtypeStruct((width, cells), BF16),
        )
        + (jax.ShapeDtypeStruct((width // 2, width * (len(before) // 2 + 1)), F32),) * 2,
        in_specs=[SMEM] + [VMEM] * (1 + len(before)),
        out_specs=(VMEM,) * 4,
        scratch_shapes=[pltpu.VMEM((width, width * (len(before) // 2 + 1)), F32)],
        compiler_params=params(),
        name="gram_blocks",
    )(core, rec, *before)


def rank_kernel(owner_count, owners, hot):
    own = owners[...]
    rows = own.shape[0]
    total = owner_count * rows
    stacked = jnp.concatenate(
        [jnp.where(own == o, 1.0, 0.0).astype(F32) for o in range(owner_count)], 0
    )
    ones = stacked.astype(BF16)
    before = lax.broadcasted_iota(jnp.int32, (128, 128), 0) < lax.broadcasted_iota(jnp.int32, (128, 128), 1)
    inner = bf_dot(ones, jnp.where(before, 1.0, 0.0).astype(BF16), NN)
    sums = bf_dot(ones, jnp.ones((128, 128), BF16), NN).astype(BF16)
    at = lax.broadcasted_iota(jnp.int32, (total, total), 0)
    of = lax.broadcasted_iota(jnp.int32, (total, total), 1)
    lower = (of < at) & (of // rows == at // rows)
    offset = bf_dot(jnp.where(lower, 1.0, 0.0).astype(BF16), sums, NN)
    picked = stacked * (inner + offset)
    rank = picked[0:rows]
    for o in range(1, owner_count):
        rank = rank + picked[o * rows : (o + 1) * rows]
    rank = rank.astype(jnp.int32)
    slot = lax.broadcasted_iota(jnp.int32, (hot.shape[0], 128), 0)
    for r in range(rows):
        hot[:, r * 128 : (r + 1) * 128] = jnp.where(slot == rank[r : r + 1, :], 1.0, 0.0).astype(BF16)


def rank_hot(owners, owner_count, capacity):
    return pl.pallas_call(
        functools.partial(rank_kernel, owner_count),
        out_shape=jax.ShapeDtypeStruct((capacity, owners.size), BF16),
        in_specs=[VMEM],
        out_specs=VMEM,
        compiler_params=params(),
        name="slot_ranks",
    )(owners)


GROUP = 4


def pack_kernel(first, owners, hot, high, low, *refs):
    out, picked = refs[-2:]
    width = high.shape[0]
    base = (first + pl.program_id(0)) * GROUP
    own = owners[...]
    rows = own.shape[0]
    for part, source in enumerate((high, low)):
        for g in range(GROUP):
            mask = jnp.where(own == base + g, 1.0, 0.0)
            for r in range(rows):
                cols = slice(r * 128, (r + 1) * 128)
                keep = jnp.broadcast_to(mask[r : r + 1, :], (width, 128)).astype(BF16)
                picked[part, g * width : (g + 1) * width, cols] = source[:, cols] * keep
    sums = bf_dot(hot[...], picked[0], NT) + bf_dot(hot[...], picked[1], NT)
    for g in range(GROUP):
        out[g] = sums[:, g * width : (g + 1) * width]


def pack(owners, hot, high, low, owner_count, half, slots=None, part=0, parts=1):
    width, cells = high.shape
    capacity = hot.shape[0]
    more = () if slots is None else (slots,)
    groups = owner_count // GROUP // parts
    first = part * groups
    return pl.pallas_call(
        functools.partial(pack_kernel, first),
        grid=(groups,),
        out_shape=jax.ShapeDtypeStruct((owner_count, capacity, 2 * width), F32),
        in_specs=[VMEM] * 4 + [HBM] * len(more),
        out_specs=pl.BlockSpec((GROUP, capacity, width), lambda g: (first + g, 0, half)),
        scratch_shapes=[pltpu.VMEM((2, GROUP * width, cells), BF16)],
        input_output_aliases={4: 0} if more else {},
        compiler_params=params(48),
        cost_estimate=pl.CostEstimate(
            flops=4 * GROUP * groups * capacity * width * cells,
            bytes_accessed=4 * GROUP * groups * capacity * width,
            transcendentals=0,
        ),
        name="pack_slots",
    )(owners, hot, high, low, *more)


BLOCK = 32


def eliminate(work, order):
    row_at = lax.broadcasted_iota(jnp.int32, (BLOCK, 128), 0)
    lane_at = lax.broadcasted_iota(jnp.int32, (BLOCK, 128), 1)
    for first in range(0, order, BLOCK):
        tile, inner = divmod(first, 128)
        tile *= 128
        on_diag = lane_at == row_at + inner
        part = work[first : first + BLOCK, tile : tile + 128]
        unit = jnp.where(on_diag, 1.0, 0.0)
        for k in range(BLOCK):
            column = part[:, inner + k : inner + k + 1]
            factor = jnp.where(row_at > k, column * (1.0 / part[k : k + 1, inner + k : inner + k + 1]), 0.0)
            unit = unit - factor * unit[k : k + 1, :]
            part = part - factor * part[k : k + 1, :]
        pivots = jnp.sum(jnp.where(on_diag, part, 0.0), axis=1, keepdims=True)
        unit = unit / jnp.sqrt(pivots)
        solved = exact_dot(unit, work[tile : tile + 128, :], NN)
        work[first : first + BLOCK, :] = solved
        if first + BLOCK < order:
            change = exact_dot(solved[:, 0:order], solved, TN)
            work[first + BLOCK :, :] = work[first + BLOCK :, :] - change[first + BLOCK :, :]


def identity(order):
    at = lax.broadcasted_iota(jnp.int32, (order, order), 0)
    return jnp.where(at == lax.broadcasted_iota(jnp.int32, (order, order), 1), 1.0, 0.0)


def upper(value):
    at = lax.broadcasted_iota(jnp.int32, value.shape, 0)
    return jnp.where(at <= lax.broadcasted_iota(jnp.int32, value.shape, 1), value, 0.0)


def joined(core, own, other, whole, width):
    half = own.shape[0]
    mine = core[0]
    whole[pl.ds(mine * half, half), 0:width] = own[...]
    whole[pl.ds((1 - mine) * half, half), 0:width] = other[...]


def lead_kernel(core, own, other, r_out, inv_out, work):
    order = 2 * own.shape[0]
    joined(core, own, other, work, order)
    work[:, order:] = identity(order)
    eliminate(work, order)
    r_out[...] = upper(work[:, 0:order])
    inv_out[...] = work[:, order:]


def trail_kernel(core, own_half, other_half, lead, lead_inv, r_out, inv_out, work, gram):
    order = lead.shape[0]
    joined(core, own_half, other_half, gram, 2 * order)
    inverse = lead_inv[...]
    cross = exact_dot(inverse, gram[:, 0:order], NT)
    work[:, 0:order] = gram[:, order:] - exact_dot(cross, cross, TN)
    work[:, order:] = identity(order)
    eliminate(work, order)
    zeros = jnp.zeros((order, order), F32)
    own = work[:, order:]
    r_out[0:order, 0:order] = lead[...]
    r_out[0:order, order:] = cross
    r_out[order:, 0:order] = zeros
    r_out[order:, order:] = upper(work[:, 0:order])
    inv_out[0:order, 0:order] = inverse
    inv_out[0:order, order:] = zeros
    inv_out[order:, 0:order] = -exact_dot(own, exact_dot(cross, inverse, TN), NN)
    inv_out[order:, order:] = own


def factor_lead(core, own, other):
    order = 2 * own.shape[0]
    return pl.pallas_call(
        lead_kernel,
        out_shape=(jax.ShapeDtypeStruct((order, order), F32),) * 2,
        in_specs=[SMEM, VMEM, VMEM],
        out_specs=(VMEM,) * 2,
        scratch_shapes=[pltpu.VMEM((order, 2 * order), F32)],
        compiler_params=params(),
        name="factor_lead",
    )(core, own, other)


def factor_trail(core, own, other, lead, lead_inv):
    order = lead.shape[0]
    return pl.pallas_call(
        trail_kernel,
        out_shape=(jax.ShapeDtypeStruct((2 * order, 2 * order), F32),) * 2,
        in_specs=[SMEM] + [VMEM] * 4,
        out_specs=(VMEM,) * 2,
        scratch_shapes=[pltpu.VMEM((order, 2 * order), F32)] * 2,
        compiler_params=params(),
        name="factor_trail",
    )(core, own, other, lead, lead_inv)


SOURCES = 8


def basis_kernel(inverse, panel, out):
    inv_high, inv_low = split(inverse[...])
    for b in range(SOURCES):
        high, low = split(panel[b])
        rows = high.shape[0]
        out[b * rows : (b + 1) * rows, :] = bf_dot(high, inv_high, NT) + (
            bf_dot(high, inv_low, NT) + bf_dot(low, inv_high, NT)
        )


def basis_of(inverse, panel):
    sources, capacity, order = panel.shape
    return pl.pallas_call(
        basis_kernel,
        grid=(sources // SOURCES,),
        out_shape=jax.ShapeDtypeStruct((sources * capacity, order), F32),
        in_specs=[
            pl.BlockSpec((order, order), lambda b: (0, 0)),
            pl.BlockSpec((SOURCES, capacity, order), lambda b: (b, 0, 0)),
        ],
        out_specs=pl.BlockSpec((SOURCES * capacity, order), lambda b: (b, 0)),
        compiler_params=params(48),
        name="basis_rows",
    )(inverse, panel)


def ring(size, shift):
    return [(i, (i + shift) % size) for i in range(size)]


def swapped(value):
    return lax.ppermute(value, "core", [(0, 1), (1, 0)])


def summed(value, axis, levels):
    size = lax.axis_size(axis)
    for level in levels:
        value = value + lax.ppermute(value, axis, [(i, i ^ 1 << level) for i in range(size)])
    return value


def on_device(state_start, viscosity, forcing, target):
    fields, wide, deep, lanes = state_start.shape
    x_size, pieces = lax.axis_size("x"), lax.axis_size("z")
    owner_count = x_size * pieces
    plane = ("y", "core", "z")
    capacity = 2 * viscosity.size // owner_count
    owners = target.reshape(wide * deep, lanes)

    def swap(value):
        return lax.all_to_all(value, plane, split_axis=0, concat_axis=0, tiled=True)

    x_at = lax.axis_index("x")
    around = jnp.stack([x_at > 0, x_at < x_size - 1]).astype(jnp.int32)
    heights = tuple(SIDE - STEPS * k for k in range(HALF))

    def shared(value, heights):
        last, first = edges_of(value, pieces, heights)
        return lax.ppermute(last, "x", ring(x_size, 1)), lax.ppermute(first, "x", ring(x_size, -1))

    one = swap(opening(viscosity, state_start, forcing, HALF)).reshape(-1, lanes)
    later = jnp.transpose(forcing[HALF:], (1, 0, 2, 3, 4)).astype(F32)
    two = swap(later).reshape(-1, lanes)
    with_visc = (SIDE,) + heights
    low_one, high_one = shared(one, with_visc)
    own_coefs = own_coefs_of(one, pieces, len(with_visc))
    records_one, middle, edge = first_half(around, one, low_one, high_one, own_coefs, pieces, with_visc)
    low_two, high_two = shared(two, heights)
    middle_low = lax.ppermute(middle[-SIDE:], "x", ring(x_size, 1))
    middle_high = lax.ppermute(middle[:SIDE], "x", ring(x_size, -1))
    records_two = second_half(
        two, low_two, high_two, middle, middle_low, middle_high, own_coefs, edge, pieces, heights
    )
    block = (fields, HALF, wide, deep, lanes)
    home_one = swap(records_one.reshape(block))
    home_two = swap(records_two.reshape(block))
    hot = rank_hot(owners, owner_count, capacity)
    core = lax.axis_index("core").astype(jnp.int32).reshape(1)
    both = (0, 1)
    high_a, low_a, keep_a, send_a = prep(core, home_one.reshape(-1, lanes), (), fields, HALF)
    part_a = summed(keep_a + swapped(send_a), "x", both)
    slots = pack(owners, hot, high_a, low_a, owner_count, 0)
    home_two, slots, part_a = lax.optimization_barrier((home_two, slots, part_a))
    high_b, low_b, keep_b, send_b = prep(core, home_two.reshape(-1, lanes), (high_a, low_a), fields, HALF)
    quarters = 4

    def packed(slots, part, *values):
        slots = pack(owners, hot, high_b, low_b, owner_count, 1, slots, part, quarters)
        return lax.optimization_barrier((slots,) + values)

    part_b = summed(keep_b + swapped(send_b), "x", (0,))
    slots, part_b = packed(slots, 0, part_b)
    part_b = summed(part_b, "x", (1,))
    slots, part_b, part_a = packed(slots, 1, part_b, part_a)
    part = summed(jnp.concatenate([part_a, part_b], 1), "z", (0,))
    slots, part = packed(slots, 2, part)
    part = summed(part, "z", (1,))
    slots, part = packed(slots, 3, part)
    panel = lax.all_to_all(slots, ("x", "z"), split_axis=0, concat_axis=0, tiled=True)
    part = summed(part, "y", both)
    other = swapped(part)
    width = fields * HALF
    lead, lead_inv = factor_lead(core, part[:, :width], other[:, :width])
    r_factor, inverse = factor_trail(core, part[:, width:], other[:, width:], lead, lead_inv)
    basis = basis_of(inverse, panel)
    return home_two[:, HALF - 1], r_factor, basis


def solution(mesh):
    slab_size, row_size = mesh.shape["slab"], mesh.shape["row"]
    cores, z_size = 2, 4
    axes = (slab_size // cores, cores, row_size // z_size, z_size)
    cut = Mesh(mesh.devices.reshape(axes), ("y", "core", "x", "z"))
    slab, row = ("y", "core"), ("x", "z")
    placed = (
        P(None, slab, row, None),
        P(slab, row, None),
        P(None, None, slab, row, None),
        P(slab, row, None, None),
    )
    return jax.shard_map(
        on_device,
        mesh=cut,
        in_specs=placed,
        out_specs=(P(None, slab, row, None), P(), P(slab + row, None)),
        check_vma=False,
    )
```

```python
import functools

import jax
import jax.numpy as jnp
from jax import lax
from jax.experimental import pallas as pl
from jax.experimental.pallas import tpu as pltpu
from jax.sharding import Mesh, PartitionSpec as P

SNAPS = 8
STEPS = 2
HALF = SNAPS // 2
ROWS = 8
step_size = 0.08
F32 = jnp.float32
BF16 = jnp.bfloat16
NT = (((1,), (1,)), ((), ()))
NN = (((1,), (0,)), ((), ()))
TN = (((0,), (0,)), ((), ()))


def split(value):
    high = value.astype(BF16)
    return high, (value - high.astype(F32)).astype(BF16)


def exact_dot(left, right, dims):
    return lax.dot_general(
        left, right, dims, precision=lax.Precision.HIGHEST, preferred_element_type=F32
    )


def bf_dot(left, right, dims):
    return lax.dot_general(left, right, dims, preferred_element_type=F32)


SIDE = HALF * STEPS
VMEM = pl.BlockSpec(memory_space=pltpu.VMEM)
SMEM = pl.BlockSpec(memory_space=pltpu.SMEM)
HBM = pl.BlockSpec(memory_space=pltpu.HBM)


def params(size=8):
    return pltpu.CompilerParams(vmem_limit_bytes=size * 1024 * 1024)


def lane_next(value):
    return pltpu.roll(value, value.shape[-1] - 1, value.ndim - 1)


def lane_prev(value):
    return pltpu.roll(value, 1, value.ndim - 1)


def reader(main, low, high, heights, pieces):
    blocks = len(heights)
    rows = sum(heights)
    own = 8 * pieces

    def read(block, y, i):
        y -= SIDE
        if 0 <= y < own:
            z, j = divmod(y, 8)
            start = (z * blocks + block) * 16 + i * 8 + j
            return main[pl.ds(start, 8, stride=pieces * blocks * 16), :]
        first = i * rows + sum(heights[:block])
        if y < 0:
            return low[pl.ds(first + heights[block] + y, 8, stride=2 * rows), :]
        return high[pl.ds(first + y - own, 8, stride=2 * rows), :]

    return read


def row_coefs(visc, y, with_rest, store):
    half = 0.5 * step_size
    slab = lax.broadcasted_iota(jnp.int32, (8, 128), 0)
    here = [visc(y, 0), visc(y, 1)]
    if with_rest:
        pair = half * (here[0] + here[1])
        up = jnp.where(slab < 7, pltpu.roll(here[0], 7, 0), 0.0)
        down = jnp.where(slab > 0, pltpu.roll(here[1], 1, 0), 0.0)
        crosses = (half * (here[0] + down), half * (here[1] + up))
    for i in range(2):
        v, nxt = here[i], visc(y + 1, i)
        inside = v > 0.0
        to_next = half * (v + nxt)
        store(1, y, i, jnp.where(inside & (nxt > 0.0), to_next, 0.0))
        if with_rest:
            z_next = half * (v + lane_next(v))
            z_prev = lane_prev(z_next)
            total = to_next + half * (v + visc(y - 1, i)) + pair + crosses[i] + z_next + z_prev
            wall = slab == (0 if i == 0 else 7)
            store(0, y, i, jnp.where(inside, 1.0 - total, 0.0))
            store(2, y, i, jnp.where(inside, pair, 0.0))
            store(3, y, i, jnp.where(inside & ~wall, crosses[i], 0.0))
            store(4, y, i, jnp.where(inside, z_next, 0.0))
            store(5, y, i, jnp.where(inside, z_prev, 0.0))


def own_coefs_kernel(pieces, blocks, main, coefs):
    own = 8 * pieces
    read = reader(main, None, None, (0,) * blocks, pieces)
    cache = {}

    def visc(y, i):
        if (y, i) not in cache:
            cache[y, i] = read(0, y, i)
        return cache[y, i]

    def store(c, y, i, value):
        coefs[c, y - SIDE, i] = value

    for y in range(SIDE + 1, SIDE + own - 1):
        row_coefs(visc, y, True, store)


def edge_coefs(edge_visc, pieces, edge):
    own = 8 * pieces
    cache = {}

    def visc(y, i):
        if (y, i) not in cache:
            cache[y, i] = edge_visc[y if y <= SIDE + 1 else y - own + 4, i]
        return cache[y, i]

    def store(c, y, i, value):
        edge[c, y if y <= SIDE else y - own + 2, i] = value

    for y in range(0, SIDE + 1):
        row_coefs(visc, y, y > 0, store)
    for y in range(SIDE + own - 1, 2 * SIDE + own - 1):
        row_coefs(visc, y, True, store)


def run_steps(read, blocks, fields, own_coefs, edge, pieces, snaps, records, last):
    own = 8 * pieces
    rows = own + 2 * SIDE

    def coef(c, y, i):
        if SIDE < y < SIDE + own - 1:
            return own_coefs[c, y - SIDE, i]
        return edge[c, y if y <= SIDE else y - own + 2, i]

    def diffuse(source, dest, low, high):
        for base in range(low, high, ROWS):
            top = min(base + ROWS, high)
            u = {(y, i): source[y, i] for y in range(base - 1, top + 1) for i in range(2)}
            face = {(y, i): coef(1, y, i) for y in range(base - 1, top) for i in range(2)}
            for y in range(base, top):
                for i in range(2):
                    mine, other = u[y, i], u[y, 1 - i]
                    cross = pltpu.roll(other, 1 if i == 0 else 7, 0)
                    total = (coef(0, y, i) * mine + coef(2, y, i) * other) + (
                        face[y, i] * u[y + 1, i] + face[y - 1, i] * u[y - 1, i]
                    )
                    total = total + (
                        (coef(4, y, i) * lane_next(mine) + coef(5, y, i) * lane_prev(mine))
                        + coef(3, y, i) * cross
                    )
                    dest[y, i] = total

    done = 0
    for k in range(snaps):
        first = fields[0]
        if k:
            for y in range(done, rows - done):
                for i in range(2):
                    first[y, i] = first[y, i] + read(blocks[k], y, i)
        for step in range(STEPS):
            done += 1
            diffuse(fields[step % 2], fields[(step + 1) % 2], done, rows - done)
        for y in range(own):
            z, j = divmod(y, 8)
            for i in range(2):
                value = first[SIDE + y, i]
                records[pl.ds((z * snaps + k) * 16 + i * 8 + j, 8, stride=pieces * snaps * 16), :] = value
                if last is not None and k == snaps - 1:
                    last[y, i] = value


def first_kernel(
    pieces, heights, around, main, low, high, own_coefs, records, last, edge_visc, buf0, buf1, edge
):
    read = reader(main, low, high, heights, pieces)
    has_low = jnp.where(around[0] > 0, 1.0, 0.0)
    has_high = jnp.where(around[1] > 0, 1.0, 0.0)
    own = 8 * pieces
    for y in range(own + 2 * SIDE):
        for i in range(2):
            buf0[y, i] = read(1, y, i)
    for y in list(range(SIDE + 2)) + list(range(SIDE + own - 2, own + 2 * SIDE)):
        for i in range(2):
            value = read(0, y, i)
            if y < SIDE:
                value = value * has_low
            elif y >= SIDE + own:
                value = value * has_high
            edge_visc[y if y <= SIDE + 1 else y - own + 4, i] = value
    edge_coefs(edge_visc, pieces, edge)
    snaps = len(heights) - 1
    run_steps(read, range(1, snaps + 1), (buf0, buf1), own_coefs, edge, pieces, snaps, records, last)


def second_kernel(pieces, heights, main, low, high, start, start_low, start_high, own_coefs, edge_visc, records, buf0, buf1, edge):
    read = reader(main, low, high, heights, pieces)
    own = 8 * pieces
    for y in range(own + 2 * SIDE):
        for i in range(2):
            if y < SIDE:
                before = start_low[y, i]
            elif y >= SIDE + own:
                before = start_high[y - SIDE - own, i]
            else:
                before = start[y - SIDE, i]
            buf0[y, i] = before + read(0, y, i)
    edge_coefs(edge_visc, pieces, edge)
    snaps = len(heights)
    run_steps(read, range(snaps), (buf0, buf1), own_coefs, edge, pieces, snaps, records, None)


def own_coefs_of(main, pieces, blocks):
    return pl.pallas_call(
        functools.partial(own_coefs_kernel, pieces, blocks),
        out_shape=jax.ShapeDtypeStruct((6, 8 * pieces, 2, 8, 128), F32),
        in_specs=[VMEM],
        out_specs=VMEM,
        compiler_params=params(4),
        name="own_coefficients",
    )(main)


def buffers(pieces):
    return [pltpu.VMEM((8 * pieces + 2 * SIDE, 2, 8, 128), F32)] * 2 + [
        pltpu.VMEM((6, 2 * SIDE + 2, 2, 8, 128), F32),
    ]


def first_half(around, main, low, high, own_coefs, pieces, heights):
    snaps = len(heights) - 1
    return pl.pallas_call(
        functools.partial(first_kernel, pieces, heights),
        out_shape=(
            jax.ShapeDtypeStruct((8 * pieces * snaps * 16, 128), F32),
            jax.ShapeDtypeStruct((8 * pieces, 2, 8, 128), F32),
            jax.ShapeDtypeStruct((2 * SIDE + 4, 2, 8, 128), F32),
        ),
        in_specs=[SMEM] + [VMEM] * 4,
        out_specs=(VMEM,) * 3,
        scratch_shapes=buffers(pieces),
        compiler_params=params(5),
        name="diffuse_first",
    )(around, main, low, high, own_coefs)


def second_half(main, low, high, start, start_low, start_high, own_coefs, edge, pieces, heights):
    snaps = len(heights)
    return pl.pallas_call(
        functools.partial(second_kernel, pieces, heights),
        out_shape=jax.ShapeDtypeStruct((8 * pieces * snaps * 16, 128), F32),
        in_specs=[VMEM] * 8,
        out_specs=VMEM,
        scratch_shapes=buffers(pieces),
        compiler_params=params(5),
        name="diffuse_second",
    )(main, low, high, start, start_low, start_high, own_coefs, edge)


def edge_kernel(pieces, heights, main, last_rows, first_rows):
    blocks, rows = len(heights), sum(heights)
    for a in range(8):
        for i in range(2):
            at = (a * 2 + i) * rows
            for k, height in enumerate(heights):
                first = (a * pieces * blocks + k) * 16 + i * 8
                last = first + (pieces - 1) * blocks * 16
                first_rows[at : at + height, :] = main[first : first + height, :]
                last_rows[at : at + height, :] = main[last + 8 - height : last + 8, :]
                at += height


def edges_of(main, pieces, heights):
    return pl.pallas_call(
        functools.partial(edge_kernel, pieces, heights),
        out_shape=(jax.ShapeDtypeStruct((16 * sum(heights), 128), F32),) * 2,
        in_specs=[VMEM],
        out_specs=(VMEM,) * 2,
        compiler_params=params(4),
        name="edge_rows",
    )(main)


def opening_kernel(visc_from, start_from, forcing_from, out_to, visc, start, forcing, out, in_sems, out_sems):
    snaps, fields = forcing.shape[:2]
    arriving = [
        pltpu.make_async_copy(visc_from, visc, in_sems.at[snaps + 1]),
        pltpu.make_async_copy(start_from, start, in_sems.at[snaps]),
    ]
    arriving += [pltpu.make_async_copy(forcing_from.at[k], forcing.at[k], in_sems.at[k]) for k in range(snaps)]
    for copy in arriving:
        copy.start()
    leaving = [
        pltpu.make_async_copy(out.at[:, k], out_to.at[:, k], out_sems.at[k]) for k in range(snaps + 1)
    ]
    arriving[0].wait()
    value = visc[...]
    for f in range(fields):
        out[f, 0] = value
    leaving[0].start()
    arriving[1].wait()
    for k in range(snaps):
        arriving[2 + k].wait()
        for f in range(fields):
            value = forcing[k, f].astype(F32)
            out[f, k + 1] = value + start[f] if k == 0 else value
        leaving[k + 1].start()
    for copy in leaving:
        copy.wait()


def opening(visc, start, forcing, snaps):
    fields = start.shape[0]
    cells = start.shape[1:]
    return pl.pallas_call(
        opening_kernel,
        out_shape=jax.ShapeDtypeStruct((fields, snaps + 1) + cells, F32),
        in_specs=[HBM] * 3,
        out_specs=HBM,
        scratch_shapes=[
            pltpu.VMEM(cells, F32),
            pltpu.VMEM(start.shape, F32),
            pltpu.VMEM((snaps,) + forcing.shape[1:], forcing.dtype),
            pltpu.VMEM((fields, snaps + 1) + cells, F32),
            pltpu.SemaphoreType.DMA((snaps + 2,)),
            pltpu.SemaphoreType.DMA((snaps + 1,)),
        ],
        compiler_params=params(60),
        name="opening_blocks",
    )(visc, start, forcing)


def prep_kernel(fields, snaps, core, *refs):
    rec, before = refs[0], refs[1:-6]
    whole, high_out, low_out, keep, send, gram = refs[-6:]
    for cell_row in range(16):
        for s in range(snaps):
            for f in range(0, fields, 16):
                parts = [
                    rec[pl.ds(((f + g) * snaps + s) * 16 + cell_row, 8, stride=snaps * 16), :]
                    for g in (0, 8)
                ]
                value = jnp.concatenate(parts, 0)
                high, low = split(value)
                at = (slice(s * fields + f, s * fields + f + 16), slice(cell_row * 128, cell_row * 128 + 128))
                whole[at] = value
                high_out[at] = high
                low_out[at] = low
    width = fields * snaps
    mine = whole[...]
    for c, other in enumerate(before + (whole,)):
        gram[:, c * width : (c + 1) * width] = exact_dot(mine, other[...], NT)
    half = width // 2
    kept = core[0]
    keep[...] = gram[pl.ds(kept * half, half), :]
    send[...] = gram[pl.ds((1 - kept) * half, half), :]


def prep(core, rec, before, fields, snaps):
    width = fields * snaps
    cells = 2048
    columns = width * (len(before) + 1)
    return pl.pallas_call(
        functools.partial(prep_kernel, fields, snaps),
        out_shape=(jax.ShapeDtypeStruct((width, cells), F32),)
        + (jax.ShapeDtypeStruct((width, cells), BF16),) * 2
        + (jax.ShapeDtypeStruct((width // 2, columns), F32),) * 2,
        in_specs=[SMEM] + [VMEM] * (1 + len(before)),
        out_specs=(VMEM,) * 5,
        scratch_shapes=[pltpu.VMEM((width, columns), F32)],
        compiler_params=params(12),
        name="gram_blocks",
    )(core, rec, *before)


def rank_kernel(owner_count, owners, hot):
    own = owners[...]
    rows = own.shape[0]
    total = owner_count * rows
    stacked = jnp.concatenate(
        [jnp.where(own == o, 1.0, 0.0).astype(F32) for o in range(owner_count)], 0
    )
    ones = stacked.astype(BF16)
    before = lax.broadcasted_iota(jnp.int32, (128, 128), 0) < lax.broadcasted_iota(jnp.int32, (128, 128), 1)
    inner = bf_dot(ones, jnp.where(before, 1.0, 0.0).astype(BF16), NN)
    sums = bf_dot(ones, jnp.ones((128, 128), BF16), NN).astype(BF16)
    at = lax.broadcasted_iota(jnp.int32, (total, total), 0)
    of = lax.broadcasted_iota(jnp.int32, (total, total), 1)
    lower = (of < at) & (of // rows == at // rows)
    offset = bf_dot(jnp.where(lower, 1.0, 0.0).astype(BF16), sums, NN)
    picked = stacked * (inner + offset)
    rank = picked[0:rows]
    for o in range(1, owner_count):
        rank = rank + picked[o * rows : (o + 1) * rows]
    rank = rank.astype(jnp.int32)
    slot = lax.broadcasted_iota(jnp.int32, (hot.shape[0], 128), 0)
    for r in range(rows):
        hot[:, r * 128 : (r + 1) * 128] = jnp.where(slot == rank[r : r + 1, :], 1.0, 0.0).astype(BF16)


def rank_hot(owners, owner_count, capacity):
    return pl.pallas_call(
        functools.partial(rank_kernel, owner_count),
        out_shape=jax.ShapeDtypeStruct((capacity, owners.size), BF16),
        in_specs=[VMEM],
        out_specs=VMEM,
        compiler_params=params(),
        name="slot_ranks",
    )(owners)


GROUP = 4


def pack_kernel(first, owners, hot, high, low, *refs):
    out, picked = refs[-2:]
    width = high.shape[0]
    base = (first + pl.program_id(0)) * GROUP
    own = owners[...]
    rows = own.shape[0]
    for part, source in enumerate((high, low)):
        for g in range(GROUP):
            mask = jnp.where(own == base + g, 1.0, 0.0)
            for r in range(rows):
                cols = slice(r * 128, (r + 1) * 128)
                keep = jnp.broadcast_to(mask[r : r + 1, :], (width, 128)).astype(BF16)
                picked[part, g * width : (g + 1) * width, cols] = source[:, cols] * keep
    sums = bf_dot(hot[...], picked[0], NT) + bf_dot(hot[...], picked[1], NT)
    for g in range(GROUP):
        out[g] = sums[:, g * width : (g + 1) * width]


def pack(owners, hot, high, low, owner_count, half, slots=None, part=0, parts=1):
    width, cells = high.shape
    capacity = hot.shape[0]
    more = () if slots is None else (slots,)
    groups = owner_count // GROUP // parts
    first = part * groups
    return pl.pallas_call(
        functools.partial(pack_kernel, first),
        grid=(groups,),
        out_shape=jax.ShapeDtypeStruct((owner_count, capacity, 2 * width), F32),
        in_specs=[VMEM] * 4 + [HBM] * len(more),
        out_specs=pl.BlockSpec((GROUP, capacity, width), lambda g: (first + g, 0, half)),
        scratch_shapes=[pltpu.VMEM((2, GROUP * width, cells), BF16)],
        input_output_aliases={4: 0} if more else {},
        compiler_params=params(48),
        cost_estimate=pl.CostEstimate(
            flops=4 * GROUP * groups * capacity * width * cells,
            bytes_accessed=4 * GROUP * groups * capacity * width,
            transcendentals=0,
        ),
        name="pack_slots",
    )(owners, hot, high, low, *more)


BLOCK = 32


def eliminate(work, order):
    row_at = lax.broadcasted_iota(jnp.int32, (BLOCK, 128), 0)
    lane_at = lax.broadcasted_iota(jnp.int32, (BLOCK, 128), 1)
    for first in range(0, order, BLOCK):
        tile, inner = divmod(first, 128)
        tile *= 128
        on_diag = lane_at == row_at + inner
        part = work[first : first + BLOCK, tile : tile + 128]
        unit = jnp.where(on_diag, 1.0, 0.0)
        for k in range(BLOCK):
            column = part[:, inner + k : inner + k + 1]
            factor = jnp.where(row_at > k, column * (1.0 / part[k : k + 1, inner + k : inner + k + 1]), 0.0)
            unit = unit - factor * unit[k : k + 1, :]
            part = part - factor * part[k : k + 1, :]
        pivots = jnp.sum(jnp.where(on_diag, part, 0.0), axis=1, keepdims=True)
        unit = unit / jnp.sqrt(pivots)
        solved = exact_dot(unit, work[tile : tile + 128, :], NN)
        work[first : first + BLOCK, :] = solved
        if first + BLOCK < order:
            change = exact_dot(solved[:, 0:order], solved, TN)
            work[first + BLOCK :, :] = work[first + BLOCK :, :] - change[first + BLOCK :, :]


def identity(order):
    at = lax.broadcasted_iota(jnp.int32, (order, order), 0)
    return jnp.where(at == lax.broadcasted_iota(jnp.int32, (order, order), 1), 1.0, 0.0)


def upper(value):
    at = lax.broadcasted_iota(jnp.int32, value.shape, 0)
    return jnp.where(at <= lax.broadcasted_iota(jnp.int32, value.shape, 1), value, 0.0)


def joined(core, own, other, whole, width):
    half = own.shape[0]
    mine = core[0]
    whole[pl.ds(mine * half, half), 0:width] = own[...]
    whole[pl.ds((1 - mine) * half, half), 0:width] = other[...]


def lead_kernel(core, own, other, r_out, inv_out, work):
    order = 2 * own.shape[0]
    joined(core, own, other, work, order)
    work[:, order:] = identity(order)
    eliminate(work, order)
    r_out[...] = upper(work[:, 0:order])
    inv_out[...] = work[:, order:]


def trail_kernel(core, own_half, other_half, lead, lead_inv, r_out, inv_out, work, gram):
    order = lead.shape[0]
    joined(core, own_half, other_half, gram, 2 * order)
    inverse = lead_inv[...]
    cross = exact_dot(inverse, gram[:, 0:order], NT)
    work[:, 0:order] = gram[:, order:] - exact_dot(cross, cross, TN)
    work[:, order:] = identity(order)
    eliminate(work, order)
    zeros = jnp.zeros((order, order), F32)
    own = work[:, order:]
    r_out[0:order, 0:order] = lead[...]
    r_out[0:order, order:] = cross
    r_out[order:, 0:order] = zeros
    r_out[order:, order:] = upper(work[:, 0:order])
    inv_out[0:order, 0:order] = inverse
    inv_out[0:order, order:] = zeros
    inv_out[order:, 0:order] = -exact_dot(own, exact_dot(cross, inverse, TN), NN)
    inv_out[order:, order:] = own


def factor_lead(core, own, other):
    order = 2 * own.shape[0]
    return pl.pallas_call(
        lead_kernel,
        out_shape=(jax.ShapeDtypeStruct((order, order), F32),) * 2,
        in_specs=[SMEM, VMEM, VMEM],
        out_specs=(VMEM,) * 2,
        scratch_shapes=[pltpu.VMEM((order, 2 * order), F32)],
        compiler_params=params(),
        name="factor_lead",
    )(core, own, other)


def factor_trail(core, own, other, lead, lead_inv):
    order = lead.shape[0]
    return pl.pallas_call(
        trail_kernel,
        out_shape=(jax.ShapeDtypeStruct((2 * order, 2 * order), F32),) * 2,
        in_specs=[SMEM] + [VMEM] * 4,
        out_specs=(VMEM,) * 2,
        scratch_shapes=[pltpu.VMEM((order, 2 * order), F32)] * 2,
        compiler_params=params(),
        name="factor_trail",
    )(core, own, other, lead, lead_inv)


SOURCES = 8


def basis_kernel(inverse, panel, out):
    inv_high, inv_low = split(inverse[...])
    for b in range(SOURCES):
        high, low = split(panel[b])
        rows = high.shape[0]
        out[b * rows : (b + 1) * rows, :] = bf_dot(high, inv_high, NT) + (
            bf_dot(high, inv_low, NT) + bf_dot(low, inv_high, NT)
        )


def basis_of(inverse, panel):
    sources, capacity, order = panel.shape
    return pl.pallas_call(
        basis_kernel,
        grid=(sources // SOURCES,),
        out_shape=jax.ShapeDtypeStruct((sources * capacity, order), F32),
        in_specs=[
            pl.BlockSpec((order, order), lambda b: (0, 0)),
            pl.BlockSpec((SOURCES, capacity, order), lambda b: (b, 0, 0)),
        ],
        out_specs=pl.BlockSpec((SOURCES * capacity, order), lambda b: (b, 0)),
        compiler_params=params(48),
        name="basis_rows",
    )(inverse, panel)


def ring(size, shift):
    return [(i, (i + shift) % size) for i in range(size)]


def swapped(value):
    return lax.ppermute(value, "core", [(0, 1), (1, 0)])


def summed(value, axis, masks):
    size = lax.axis_size(axis)
    for mask in masks:
        value = value + lax.ppermute(value, axis, [(i, i ^ mask) for i in range(size)])
    return value


def on_device(state_start, viscosity, forcing, target):
    fields, wide, deep, lanes = state_start.shape
    x_size, pieces = lax.axis_size("x"), lax.axis_size("z")
    owner_count = x_size * pieces
    plane = ("y", "core", "z")
    capacity = 2 * viscosity.size // owner_count
    owners = target.reshape(wide * deep, lanes)

    def swap(value):
        return lax.all_to_all(value, plane, split_axis=0, concat_axis=0, tiled=True)

    x_at = lax.axis_index("x")
    around = jnp.stack([x_at > 0, x_at < x_size - 1]).astype(jnp.int32)
    heights = tuple(SIDE - STEPS * k for k in range(HALF))

    def shared(value, heights):
        last, first = edges_of(value, pieces, heights)
        return lax.ppermute(last, "x", ring(x_size, 1)), lax.ppermute(first, "x", ring(x_size, -1))

    one = swap(opening(viscosity, state_start, forcing, HALF)).reshape(-1, lanes)
    later = jnp.transpose(forcing[HALF:], (1, 0, 2, 3, 4)).astype(F32)
    two = swap(later).reshape(-1, lanes)
    with_visc = (SIDE,) + heights
    low_one, high_one = shared(one, with_visc)
    own_coefs = own_coefs_of(one, pieces, len(with_visc))
    records_one, middle, edge = first_half(around, one, low_one, high_one, own_coefs, pieces, with_visc)
    low_two, high_two = shared(two, heights)
    middle_low = lax.ppermute(middle[-SIDE:], "x", ring(x_size, 1))
    middle_high = lax.ppermute(middle[:SIDE], "x", ring(x_size, -1))
    records_two = second_half(
        two, low_two, high_two, middle, middle_low, middle_high, own_coefs, edge, pieces, heights
    )
    block = (fields, HALF, wide, deep, lanes)
    home_one = swap(records_one.reshape(block))
    home_two = swap(records_two.reshape(block))
    hot = rank_hot(owners, owner_count, capacity)
    core = lax.axis_index("core").astype(jnp.int32).reshape(1)
    both = (1, 3)
    whole_a, high_a, low_a, keep_a, send_a = prep(core, home_one.reshape(-1, lanes), (), fields, HALF)
    part_a = summed(keep_a + swapped(send_a), "x", both)
    slots = pack(owners, hot, high_a, low_a, owner_count, 0)
    home_two, slots, part_a = lax.optimization_barrier((home_two, slots, part_a))
    _, high_b, low_b, keep_b, send_b = prep(core, home_two.reshape(-1, lanes), (whole_a,), fields, HALF)
    quarters = 4

    def packed(slots, part, *values):
        slots = pack(owners, hot, high_b, low_b, owner_count, 1, slots, part, quarters)
        return lax.optimization_barrier((slots,) + values)

    part_b = summed(keep_b + swapped(send_b), "x", (1,))
    slots, part_b = packed(slots, 0, part_b)
    part_b = summed(part_b, "x", (3,))
    slots, part_b, part_a = packed(slots, 1, part_b, part_a)
    part = summed(jnp.concatenate([part_a, part_b], 1), "z", (1,))
    slots, part = packed(slots, 2, part)
    part = summed(part, "z", (3,))
    slots, part = packed(slots, 3, part)
    panel = lax.all_to_all(slots, ("x", "z"), split_axis=0, concat_axis=0, tiled=True)
    part = summed(part, "y", both)
    other = swapped(part)
    width = fields * HALF
    lead, lead_inv = factor_lead(core, part[:, :width], other[:, :width])
    r_factor, inverse = factor_trail(core, part[:, width:], other[:, width:], lead, lead_inv)
    basis = basis_of(inverse, panel)
    return home_two[:, HALF - 1], r_factor, basis


def solution(mesh):
    slab_size, row_size = mesh.shape["slab"], mesh.shape["row"]
    cores, z_size = 2, 4
    axes = (slab_size // cores, cores, row_size // z_size, z_size)
    cut = Mesh(mesh.devices.reshape(axes), ("y", "core", "x", "z"))
    slab, row = ("y", "core"), ("x", "z")
    placed = (
        P(None, slab, row, None),
        P(slab, row, None),
        P(None, None, slab, row, None),
        P(slab, row, None, None),
    )
    return jax.shard_map(
        on_device,
        mesh=cut,
        in_specs=placed,
        out_specs=(P(None, slab, row, None), P(), P(slab + row, None)),
        check_vma=False,
    )
```

```python
import functools

import jax
import jax.numpy as jnp
from jax import lax
from jax.experimental import pallas as pl
from jax.experimental.pallas import tpu as pltpu
from jax.sharding import Mesh, PartitionSpec as P

SNAPS = 8
STEPS = 2
HALF = SNAPS // 2
ROWS = 8
step_size = 0.08
F32 = jnp.float32
BF16 = jnp.bfloat16
NT = (((1,), (1,)), ((), ()))
NN = (((1,), (0,)), ((), ()))
TN = (((0,), (0,)), ((), ()))


def split(value):
    high = value.astype(BF16)
    return high, (value - high.astype(F32)).astype(BF16)


def exact_dot(left, right, dims):
    return lax.dot_general(
        left, right, dims, precision=lax.Precision.HIGHEST, preferred_element_type=F32
    )


def bf_dot(left, right, dims):
    return lax.dot_general(left, right, dims, preferred_element_type=F32)


SIDE = HALF * STEPS
VMEM = pl.BlockSpec(memory_space=pltpu.VMEM)
SMEM = pl.BlockSpec(memory_space=pltpu.SMEM)
HBM = pl.BlockSpec(memory_space=pltpu.HBM)


def params(size=8):
    return pltpu.CompilerParams(vmem_limit_bytes=size * 1024 * 1024)


def lane_next(value):
    return pltpu.roll(value, value.shape[-1] - 1, value.ndim - 1)


def lane_prev(value):
    return pltpu.roll(value, 1, value.ndim - 1)


def reader(main, low, high, heights, pieces):
    blocks = len(heights)
    rows = sum(heights)
    own = 8 * pieces

    def read(block, y, i):
        y -= SIDE
        if 0 <= y < own:
            z, j = divmod(y, 8)
            start = (z * blocks + block) * 16 + i * 8 + j
            return main[pl.ds(start, 8, stride=pieces * blocks * 16), :]
        first = i * rows + sum(heights[:block])
        if y < 0:
            return low[pl.ds(first + heights[block] + y, 8, stride=2 * rows), :]
        return high[pl.ds(first + y - own, 8, stride=2 * rows), :]

    return read


def row_coefs(visc, y, with_rest, store):
    half = 0.5 * step_size
    slab = lax.broadcasted_iota(jnp.int32, (8, 128), 0)
    here = [visc(y, 0), visc(y, 1)]
    if with_rest:
        pair = half * (here[0] + here[1])
        up = jnp.where(slab < 7, pltpu.roll(here[0], 7, 0), 0.0)
        down = jnp.where(slab > 0, pltpu.roll(here[1], 1, 0), 0.0)
        crosses = (half * (here[0] + down), half * (here[1] + up))
    for i in range(2):
        v, nxt = here[i], visc(y + 1, i)
        inside = v > 0.0
        to_next = half * (v + nxt)
        store(1, y, i, jnp.where(inside & (nxt > 0.0), to_next, 0.0))
        if with_rest:
            z_next = half * (v + lane_next(v))
            z_prev = lane_prev(z_next)
            total = to_next + half * (v + visc(y - 1, i)) + pair + crosses[i] + z_next + z_prev
            wall = slab == (0 if i == 0 else 7)
            store(0, y, i, jnp.where(inside, 1.0 - total, 0.0))
            store(2, y, i, jnp.where(inside, pair, 0.0))
            store(3, y, i, jnp.where(inside & ~wall, crosses[i], 0.0))
            store(4, y, i, jnp.where(inside, z_next, 0.0))
            store(5, y, i, jnp.where(inside, z_prev, 0.0))


def own_coefs_kernel(pieces, blocks, main, coefs):
    own = 8 * pieces
    read = reader(main, None, None, (0,) * blocks, pieces)
    cache = {}

    def visc(y, i):
        if (y, i) not in cache:
            cache[y, i] = read(0, y, i)
        return cache[y, i]

    def store(c, y, i, value):
        coefs[c, y - SIDE, i] = value

    for y in range(SIDE + 1, SIDE + own - 1):
        row_coefs(visc, y, True, store)


def edge_coefs(edge_visc, pieces, edge):
    own = 8 * pieces
    cache = {}

    def visc(y, i):
        if (y, i) not in cache:
            cache[y, i] = edge_visc[y if y <= SIDE + 1 else y - own + 4, i]
        return cache[y, i]

    def store(c, y, i, value):
        edge[c, y if y <= SIDE else y - own + 2, i] = value

    for y in range(0, SIDE + 1):
        row_coefs(visc, y, y > 0, store)
    for y in range(SIDE + own - 1, 2 * SIDE + own - 1):
        row_coefs(visc, y, True, store)


def run_steps(read, blocks, fields, own_coefs, edge, pieces, snaps, records, last):
    own = 8 * pieces
    rows = own + 2 * SIDE

    def coef(c, y, i):
        if SIDE < y < SIDE + own - 1:
            return own_coefs[c, y - SIDE, i]
        return edge[c, y if y <= SIDE else y - own + 2, i]

    def diffuse(source, dest, low, high):
        for base in range(low, high, ROWS):
            top = min(base + ROWS, high)
            u = {(y, i): source[y, i] for y in range(base - 1, top + 1) for i in range(2)}
            face = {(y, i): coef(1, y, i) for y in range(base - 1, top) for i in range(2)}
            for y in range(base, top):
                for i in range(2):
                    mine, other = u[y, i], u[y, 1 - i]
                    cross = pltpu.roll(other, 1 if i == 0 else 7, 0)
                    total = (coef(0, y, i) * mine + coef(2, y, i) * other) + (
                        face[y, i] * u[y + 1, i] + face[y - 1, i] * u[y - 1, i]
                    )
                    total = total + (
                        (coef(4, y, i) * lane_next(mine) + coef(5, y, i) * lane_prev(mine))
                        + coef(3, y, i) * cross
                    )
                    dest[y, i] = total

    done = 0
    for k in range(snaps):
        first = fields[0]
        if k:
            for y in range(done, rows - done):
                for i in range(2):
                    first[y, i] = first[y, i] + read(blocks[k], y, i)
        for step in range(STEPS):
            done += 1
            diffuse(fields[step % 2], fields[(step + 1) % 2], done, rows - done)
        for y in range(own):
            z, j = divmod(y, 8)
            for i in range(2):
                value = first[SIDE + y, i]
                records[pl.ds((z * snaps + k) * 16 + i * 8 + j, 8, stride=pieces * snaps * 16), :] = value
                if last is not None and k == snaps - 1:
                    last[y, i] = value


def first_kernel(
    pieces, heights, around, main, low, high, own_coefs, records, last, edge_visc, buf0, buf1, edge
):
    read = reader(main, low, high, heights, pieces)
    has_low = jnp.where(around[0] > 0, 1.0, 0.0)
    has_high = jnp.where(around[1] > 0, 1.0, 0.0)
    own = 8 * pieces
    for y in range(own + 2 * SIDE):
        for i in range(2):
            buf0[y, i] = read(1, y, i)
    for y in list(range(SIDE + 2)) + list(range(SIDE + own - 2, own + 2 * SIDE)):
        for i in range(2):
            value = read(0, y, i)
            if y < SIDE:
                value = value * has_low
            elif y >= SIDE + own:
                value = value * has_high
            edge_visc[y if y <= SIDE + 1 else y - own + 4, i] = value
    edge_coefs(edge_visc, pieces, edge)
    snaps = len(heights) - 1
    run_steps(read, range(1, snaps + 1), (buf0, buf1), own_coefs, edge, pieces, snaps, records, last)


def second_kernel(pieces, heights, main, low, high, start, start_low, start_high, own_coefs, edge_visc, records, buf0, buf1, edge):
    read = reader(main, low, high, heights, pieces)
    own = 8 * pieces
    for y in range(own + 2 * SIDE):
        for i in range(2):
            if y < SIDE:
                before = start_low[y, i]
            elif y >= SIDE + own:
                before = start_high[y - SIDE - own, i]
            else:
                before = start[y - SIDE, i]
            buf0[y, i] = before + read(0, y, i)
    edge_coefs(edge_visc, pieces, edge)
    snaps = len(heights)
    run_steps(read, range(snaps), (buf0, buf1), own_coefs, edge, pieces, snaps, records, None)


def own_coefs_of(main, pieces, blocks):
    return pl.pallas_call(
        functools.partial(own_coefs_kernel, pieces, blocks),
        out_shape=jax.ShapeDtypeStruct((6, 8 * pieces, 2, 8, 128), F32),
        in_specs=[VMEM],
        out_specs=VMEM,
        compiler_params=params(4),
        name="own_coefficients",
    )(main)


def buffers(pieces):
    return [pltpu.VMEM((8 * pieces + 2 * SIDE, 2, 8, 128), F32)] * 2 + [
        pltpu.VMEM((6, 2 * SIDE + 2, 2, 8, 128), F32),
    ]


def first_half(around, main, low, high, own_coefs, pieces, heights):
    snaps = len(heights) - 1
    return pl.pallas_call(
        functools.partial(first_kernel, pieces, heights),
        out_shape=(
            jax.ShapeDtypeStruct((8 * pieces * snaps * 16, 128), F32),
            jax.ShapeDtypeStruct((8 * pieces, 2, 8, 128), F32),
            jax.ShapeDtypeStruct((2 * SIDE + 4, 2, 8, 128), F32),
        ),
        in_specs=[SMEM] + [VMEM] * 4,
        out_specs=(VMEM,) * 3,
        scratch_shapes=buffers(pieces),
        compiler_params=params(5),
        name="diffuse_first",
    )(around, main, low, high, own_coefs)


def second_half(main, low, high, start, start_low, start_high, own_coefs, edge, pieces, heights):
    snaps = len(heights)
    return pl.pallas_call(
        functools.partial(second_kernel, pieces, heights),
        out_shape=jax.ShapeDtypeStruct((8 * pieces * snaps * 16, 128), F32),
        in_specs=[VMEM] * 8,
        out_specs=VMEM,
        scratch_shapes=buffers(pieces),
        compiler_params=params(5),
        name="diffuse_second",
    )(main, low, high, start, start_low, start_high, own_coefs, edge)


def edge_kernel(pieces, heights, main, last_rows, first_rows):
    blocks, rows = len(heights), sum(heights)
    for a in range(8):
        for i in range(2):
            at = (a * 2 + i) * rows
            for k, height in enumerate(heights):
                first = (a * pieces * blocks + k) * 16 + i * 8
                last = first + (pieces - 1) * blocks * 16
                first_rows[at : at + height, :] = main[first : first + height, :]
                last_rows[at : at + height, :] = main[last + 8 - height : last + 8, :]
                at += height


def edges_of(main, pieces, heights):
    return pl.pallas_call(
        functools.partial(edge_kernel, pieces, heights),
        out_shape=(jax.ShapeDtypeStruct((16 * sum(heights), 128), F32),) * 2,
        in_specs=[VMEM],
        out_specs=(VMEM,) * 2,
        compiler_params=params(4),
        name="edge_rows",
    )(main)


def opening_kernel(visc_from, start_from, forcing_from, out_to, visc, start, forcing, out, in_sems, out_sems):
    snaps, fields = forcing.shape[:2]
    arriving = [
        pltpu.make_async_copy(visc_from, visc, in_sems.at[snaps + 1]),
        pltpu.make_async_copy(start_from, start, in_sems.at[snaps]),
    ]
    arriving += [pltpu.make_async_copy(forcing_from.at[k], forcing.at[k], in_sems.at[k]) for k in range(snaps)]
    for copy in arriving:
        copy.start()
    leaving = [
        pltpu.make_async_copy(out.at[:, k], out_to.at[:, k], out_sems.at[k]) for k in range(snaps + 1)
    ]
    arriving[0].wait()
    value = visc[...]
    for f in range(fields):
        out[f, 0] = value
    leaving[0].start()
    arriving[1].wait()
    for k in range(snaps):
        arriving[2 + k].wait()
        for f in range(fields):
            value = forcing[k, f].astype(F32)
            out[f, k + 1] = value + start[f] if k == 0 else value
        leaving[k + 1].start()
    for copy in leaving:
        copy.wait()


def opening(visc, start, forcing, snaps):
    fields = start.shape[0]
    cells = start.shape[1:]
    return pl.pallas_call(
        opening_kernel,
        out_shape=jax.ShapeDtypeStruct((fields, snaps + 1) + cells, F32),
        in_specs=[HBM] * 3,
        out_specs=HBM,
        scratch_shapes=[
            pltpu.VMEM(cells, F32),
            pltpu.VMEM(start.shape, F32),
            pltpu.VMEM((snaps,) + forcing.shape[1:], forcing.dtype),
            pltpu.VMEM((fields, snaps + 1) + cells, F32),
            pltpu.SemaphoreType.DMA((snaps + 2,)),
            pltpu.SemaphoreType.DMA((snaps + 1,)),
        ],
        compiler_params=params(60),
        name="opening_blocks",
    )(visc, start, forcing)


def gram_kernel(fields, snaps, core, *refs):
    rec, before = refs[0], refs[1:-4]
    whole, keep, send, gram = refs[-4:]
    for cell_row in range(16):
        for s in range(snaps):
            for f in range(0, fields, 8):
                value = rec[pl.ds((f * snaps + s) * 16 + cell_row, 8, stride=snaps * 16), :]
                at = (slice(s * fields + f, s * fields + f + 8), slice(cell_row * 128, cell_row * 128 + 128))
                whole[at] = value
    width = fields * snaps
    mine = whole[...]
    for c, other in enumerate(before + (whole,)):
        gram[:, c * width : (c + 1) * width] = exact_dot(mine, other[...], NT)
    half = width // 2
    kept = core[0]
    keep[...] = gram[pl.ds(kept * half, half), :]
    send[...] = gram[pl.ds((1 - kept) * half, half), :]


def gram_of(core, rec, before, fields, snaps):
    width = fields * snaps
    cells = 2048
    columns = width * (len(before) + 1)
    return pl.pallas_call(
        functools.partial(gram_kernel, fields, snaps),
        out_shape=(jax.ShapeDtypeStruct((width, cells), F32),)
        + (jax.ShapeDtypeStruct((width // 2, columns), F32),) * 2,
        in_specs=[SMEM] + [VMEM] * (1 + len(before)),
        out_specs=(VMEM,) * 3,
        scratch_shapes=[pltpu.VMEM((width, columns), F32)],
        compiler_params=params(12),
        name="gram_blocks",
    )(core, rec, *before)


def terms_kernel(whole, high_out, low_out):
    high, low = split(whole[...])
    high_out[...] = high
    low_out[...] = low


def terms_of(whole):
    return pl.pallas_call(
        terms_kernel,
        out_shape=(jax.ShapeDtypeStruct(whole.shape, BF16),) * 2,
        in_specs=[VMEM],
        out_specs=(VMEM,) * 2,
        compiler_params=params(),
        name="two_terms",
    )(whole)


def rank_kernel(owner_count, owners, hot):
    own = owners[...]
    rows = own.shape[0]
    total = owner_count * rows
    stacked = jnp.concatenate(
        [jnp.where(own == o, 1.0, 0.0).astype(F32) for o in range(owner_count)], 0
    )
    ones = stacked.astype(BF16)
    before = lax.broadcasted_iota(jnp.int32, (128, 128), 0) < lax.broadcasted_iota(jnp.int32, (128, 128), 1)
    inner = bf_dot(ones, jnp.where(before, 1.0, 0.0).astype(BF16), NN)
    sums = bf_dot(ones, jnp.ones((128, 128), BF16), NN).astype(BF16)
    at = lax.broadcasted_iota(jnp.int32, (total, total), 0)
    of = lax.broadcasted_iota(jnp.int32, (total, total), 1)
    lower = (of < at) & (of // rows == at // rows)
    offset = bf_dot(jnp.where(lower, 1.0, 0.0).astype(BF16), sums, NN)
    picked = stacked * (inner + offset)
    rank = picked[0:rows]
    for o in range(1, owner_count):
        rank = rank + picked[o * rows : (o + 1) * rows]
    rank = rank.astype(jnp.int32)
    slot = lax.broadcasted_iota(jnp.int32, (hot.shape[0], 128), 0)
    for r in range(rows):
        hot[:, r * 128 : (r + 1) * 128] = jnp.where(slot == rank[r : r + 1, :], 1.0, 0.0).astype(BF16)


def rank_hot(owners, owner_count, capacity):
    return pl.pallas_call(
        functools.partial(rank_kernel, owner_count),
        out_shape=jax.ShapeDtypeStruct((capacity, owners.size), BF16),
        in_specs=[VMEM],
        out_specs=VMEM,
        compiler_params=params(),
        name="slot_ranks",
    )(owners)


GROUP = 4


def pack_kernel(first, owners, hot, high, low, *refs):
    out, picked = refs[-2:]
    width = high.shape[0]
    base = (first + pl.program_id(0)) * GROUP
    own = owners[...]
    rows = own.shape[0]
    for part, source in enumerate((high, low)):
        for g in range(GROUP):
            mask = jnp.where(own == base + g, 1.0, 0.0)
            for r in range(rows):
                cols = slice(r * 128, (r + 1) * 128)
                keep = jnp.broadcast_to(mask[r : r + 1, :], (width, 128)).astype(BF16)
                picked[part, g * width : (g + 1) * width, cols] = source[:, cols] * keep
    sums = bf_dot(hot[...], picked[0], NT) + bf_dot(hot[...], picked[1], NT)
    for g in range(GROUP):
        out[g] = sums[:, g * width : (g + 1) * width]


def pack(owners, hot, high, low, owner_count, half, slots=None, part=0, parts=1):
    width, cells = high.shape
    capacity = hot.shape[0]
    more = () if slots is None else (slots,)
    groups = owner_count // GROUP // parts
    first = part * groups
    return pl.pallas_call(
        functools.partial(pack_kernel, first),
        grid=(groups,),
        out_shape=jax.ShapeDtypeStruct((owner_count, capacity, 2 * width), F32),
        in_specs=[VMEM] * 4 + [HBM] * len(more),
        out_specs=pl.BlockSpec((GROUP, capacity, width), lambda g: (first + g, 0, half)),
        scratch_shapes=[pltpu.VMEM((2, GROUP * width, cells), BF16)],
        input_output_aliases={4: 0} if more else {},
        compiler_params=params(48),
        cost_estimate=pl.CostEstimate(
            flops=4 * GROUP * groups * capacity * width * cells,
            bytes_accessed=4 * GROUP * groups * capacity * width,
            transcendentals=0,
        ),
        name="pack_slots",
    )(owners, hot, high, low, *more)


BLOCK = 32


def eliminate(work, order):
    row_at = lax.broadcasted_iota(jnp.int32, (BLOCK, 128), 0)
    lane_at = lax.broadcasted_iota(jnp.int32, (BLOCK, 128), 1)
    for first in range(0, order, BLOCK):
        tile, inner = divmod(first, 128)
        tile *= 128
        on_diag = lane_at == row_at + inner
        part = work[first : first + BLOCK, tile : tile + 128]
        unit = jnp.where(on_diag, 1.0, 0.0)
        for k in range(BLOCK):
            column = part[:, inner + k : inner + k + 1]
            factor = jnp.where(row_at > k, column * (1.0 / part[k : k + 1, inner + k : inner + k + 1]), 0.0)
            unit = unit - factor * unit[k : k + 1, :]
            part = part - factor * part[k : k + 1, :]
        pivots = jnp.sum(jnp.where(on_diag, part, 0.0), axis=1, keepdims=True)
        unit = unit / jnp.sqrt(pivots)
        solved = exact_dot(unit, work[tile : tile + 128, :], NN)
        work[first : first + BLOCK, :] = solved
        if first + BLOCK < order:
            change = exact_dot(solved[:, 0:order], solved, TN)
            work[first + BLOCK :, :] = work[first + BLOCK :, :] - change[first + BLOCK :, :]


def identity(order):
    at = lax.broadcasted_iota(jnp.int32, (order, order), 0)
    return jnp.where(at == lax.broadcasted_iota(jnp.int32, (order, order), 1), 1.0, 0.0)


def upper(value):
    at = lax.broadcasted_iota(jnp.int32, value.shape, 0)
    return jnp.where(at <= lax.broadcasted_iota(jnp.int32, value.shape, 1), value, 0.0)


def joined(core, own, other, whole, width):
    half = own.shape[0]
    mine = core[0]
    whole[pl.ds(mine * half, half), 0:width] = own[...]
    whole[pl.ds((1 - mine) * half, half), 0:width] = other[...]


def lead_kernel(core, own, other, r_out, inv_out, work):
    order = 2 * own.shape[0]
    joined(core, own, other, work, order)
    work[:, order:] = identity(order)
    eliminate(work, order)
    r_out[...] = upper(work[:, 0:order])
    inv_out[...] = work[:, order:]


def trail_kernel(core, own_half, other_half, lead, lead_inv, r_out, inv_out, work, gram):
    order = lead.shape[0]
    joined(core, own_half, other_half, gram, 2 * order)
    inverse = lead_inv[...]
    cross = exact_dot(inverse, gram[:, 0:order], NT)
    work[:, 0:order] = gram[:, order:] - exact_dot(cross, cross, TN)
    work[:, order:] = identity(order)
    eliminate(work, order)
    zeros = jnp.zeros((order, order), F32)
    own = work[:, order:]
    r_out[0:order, 0:order] = lead[...]
    r_out[0:order, order:] = cross
    r_out[order:, 0:order] = zeros
    r_out[order:, order:] = upper(work[:, 0:order])
    inv_out[0:order, 0:order] = inverse
    inv_out[0:order, order:] = zeros
    inv_out[order:, 0:order] = -exact_dot(own, exact_dot(cross, inverse, TN), NN)
    inv_out[order:, order:] = own


def factor_lead(core, own, other):
    order = 2 * own.shape[0]
    return pl.pallas_call(
        lead_kernel,
        out_shape=(jax.ShapeDtypeStruct((order, order), F32),) * 2,
        in_specs=[SMEM, VMEM, VMEM],
        out_specs=(VMEM,) * 2,
        scratch_shapes=[pltpu.VMEM((order, 2 * order), F32)],
        compiler_params=params(),
        name="factor_lead",
    )(core, own, other)


def factor_trail(core, own, other, lead, lead_inv):
    order = lead.shape[0]
    return pl.pallas_call(
        trail_kernel,
        out_shape=(jax.ShapeDtypeStruct((2 * order, 2 * order), F32),) * 2,
        in_specs=[SMEM] + [VMEM] * 4,
        out_specs=(VMEM,) * 2,
        scratch_shapes=[pltpu.VMEM((order, 2 * order), F32)] * 2,
        compiler_params=params(),
        name="factor_trail",
    )(core, own, other, lead, lead_inv)


SOURCES = 8


def basis_kernel(inverse, panel, out):
    inv_high, inv_low = split(inverse[...])
    for b in range(SOURCES):
        high, low = split(panel[b])
        rows = high.shape[0]
        out[b * rows : (b + 1) * rows, :] = bf_dot(high, inv_high, NT) + (
            bf_dot(high, inv_low, NT) + bf_dot(low, inv_high, NT)
        )


def basis_of(inverse, panel):
    sources, capacity, order = panel.shape
    return pl.pallas_call(
        basis_kernel,
        grid=(sources // SOURCES,),
        out_shape=jax.ShapeDtypeStruct((sources * capacity, order), F32),
        in_specs=[
            pl.BlockSpec((order, order), lambda b: (0, 0)),
            pl.BlockSpec((SOURCES, capacity, order), lambda b: (b, 0, 0)),
        ],
        out_specs=pl.BlockSpec((SOURCES * capacity, order), lambda b: (b, 0)),
        compiler_params=params(48),
        name="basis_rows",
    )(inverse, panel)


def ring(size, shift):
    return [(i, (i + shift) % size) for i in range(size)]


def swapped(value):
    return lax.ppermute(value, "core", [(0, 1), (1, 0)])


def summed(value, axis, masks):
    size = lax.axis_size(axis)
    for mask in masks:
        value = value + lax.ppermute(value, axis, [(i, i ^ mask) for i in range(size)])
    return value


def on_device(state_start, viscosity, forcing, target):
    fields, wide, deep, lanes = state_start.shape
    x_size, pieces = lax.axis_size("x"), lax.axis_size("z")
    owner_count = x_size * pieces
    plane = ("y", "core", "z")
    capacity = 2 * viscosity.size // owner_count
    owners = target.reshape(wide * deep, lanes)

    def swap(value):
        return lax.all_to_all(value, plane, split_axis=0, concat_axis=0, tiled=True)

    x_at = lax.axis_index("x")
    around = jnp.stack([x_at > 0, x_at < x_size - 1]).astype(jnp.int32)
    heights = tuple(SIDE - STEPS * k for k in range(HALF))

    def shared(value, heights):
        last, first = edges_of(value, pieces, heights)
        return lax.ppermute(last, "x", ring(x_size, 1)), lax.ppermute(first, "x", ring(x_size, -1))

    one = swap(opening(viscosity, state_start, forcing, HALF)).reshape(-1, lanes)
    later = jnp.transpose(forcing[HALF:], (1, 0, 2, 3, 4)).astype(F32)
    two = swap(later).reshape(-1, lanes)
    with_visc = (SIDE,) + heights
    low_one, high_one = shared(one, with_visc)
    own_coefs = own_coefs_of(one, pieces, len(with_visc))
    records_one, middle, edge = first_half(around, one, low_one, high_one, own_coefs, pieces, with_visc)
    low_two, high_two = shared(two, heights)
    middle_low = lax.ppermute(middle[-SIDE:], "x", ring(x_size, 1))
    middle_high = lax.ppermute(middle[:SIDE], "x", ring(x_size, -1))
    records_two = second_half(
        two, low_two, high_two, middle, middle_low, middle_high, own_coefs, edge, pieces, heights
    )
    block = (fields, HALF, wide, deep, lanes)
    home_one = swap(records_one.reshape(block))
    home_two = swap(records_two.reshape(block))
    hot = rank_hot(owners, owner_count, capacity)
    core = lax.axis_index("core").astype(jnp.int32).reshape(1)
    both = (1, 3)
    whole_a, keep_a, send_a = gram_of(core, home_one.reshape(-1, lanes), (), fields, HALF)
    high_a, low_a = terms_of(whole_a)
    part_a = summed(keep_a + swapped(send_a), "x", both)
    slots = pack(owners, hot, high_a, low_a, owner_count, 0)
    home_two, slots, part_a = lax.optimization_barrier((home_two, slots, part_a))
    whole_b, keep_b, send_b = gram_of(core, home_two.reshape(-1, lanes), (whole_a,), fields, HALF)
    high_b, low_b = terms_of(whole_b)
    quarters = 4

    def packed(slots, part, *values):
        slots = pack(owners, hot, high_b, low_b, owner_count, 1, slots, part, quarters)
        return lax.optimization_barrier((slots,) + values)

    part_b = summed(keep_b + swapped(send_b), "x", (1,))
    slots, part_a, part_b = packed(slots, 0, part_a, part_b)
    part = summed(jnp.concatenate([part_a, part_b], 1), "z", (1,))
    slots, part = packed(slots, 1, part)
    width = fields * HALF
    part_a, part_b = part[:, :width], summed(part[:, width:], "x", (3,))
    slots, part_a, part_b = packed(slots, 2, part_a, part_b)
    part = summed(jnp.concatenate([part_a, part_b], 1), "z", (3,))
    slots, part = packed(slots, 3, part)
    panel = lax.all_to_all(slots, ("x", "z"), split_axis=0, concat_axis=0, tiled=True)
    part = summed(part, "y", both)
    other = swapped(part)
    lead, lead_inv = factor_lead(core, part[:, :width], other[:, :width])
    r_factor, inverse = factor_trail(core, part[:, width:], other[:, width:], lead, lead_inv)
    basis = basis_of(inverse, panel)
    return home_two[:, HALF - 1], r_factor, basis


def solution(mesh):
    slab_size, row_size = mesh.shape["slab"], mesh.shape["row"]
    cores, z_size = 2, 4
    axes = (slab_size // cores, cores, row_size // z_size, z_size)
    cut = Mesh(mesh.devices.reshape(axes), ("y", "core", "x", "z"))
    slab, row = ("y", "core"), ("x", "z")
    placed = (
        P(None, slab, row, None),
        P(slab, row, None),
        P(None, None, slab, row, None),
        P(slab, row, None, None),
    )
    return jax.shard_map(
        on_device,
        mesh=cut,
        in_specs=placed,
        out_specs=(P(None, slab, row, None), P(), P(slab + row, None)),
        check_vma=False,
    )
```

```python
import functools

import jax
import jax.numpy as jnp
from jax import lax
from jax.experimental import pallas as pl
from jax.experimental.pallas import tpu as pltpu
from jax.sharding import Mesh, PartitionSpec as P

SNAPS = 8
STEPS = 2
HALF = SNAPS // 2
ROWS = 8
step_size = 0.08
F32 = jnp.float32
BF16 = jnp.bfloat16
NT = (((1,), (1,)), ((), ()))
NN = (((1,), (0,)), ((), ()))
TN = (((0,), (0,)), ((), ()))


def split(value):
    high = value.astype(BF16)
    return high, (value - high.astype(F32)).astype(BF16)


def exact_dot(left, right, dims):
    return lax.dot_general(
        left, right, dims, precision=lax.Precision.HIGHEST, preferred_element_type=F32
    )


def bf_dot(left, right, dims):
    return lax.dot_general(left, right, dims, preferred_element_type=F32)


SIDE = HALF * STEPS
VMEM = pl.BlockSpec(memory_space=pltpu.VMEM)
SMEM = pl.BlockSpec(memory_space=pltpu.SMEM)
HBM = pl.BlockSpec(memory_space=pltpu.HBM)


def params(size=8):
    return pltpu.CompilerParams(vmem_limit_bytes=size * 1024 * 1024)


def lane_next(value):
    return pltpu.roll(value, value.shape[-1] - 1, value.ndim - 1)


def lane_prev(value):
    return pltpu.roll(value, 1, value.ndim - 1)


def reader(main, low, high, heights, pieces):
    blocks = len(heights)
    rows = sum(heights)
    own = 8 * pieces

    def read(block, y, i):
        y -= SIDE
        if 0 <= y < own:
            z, j = divmod(y, 8)
            start = (z * blocks + block) * 16 + i * 8 + j
            return main[pl.ds(start, 8, stride=pieces * blocks * 16), :]
        first = i * rows + sum(heights[:block])
        if y < 0:
            return low[pl.ds(first + heights[block] + y, 8, stride=2 * rows), :]
        return high[pl.ds(first + y - own, 8, stride=2 * rows), :]

    return read


def row_coefs(visc, y, with_rest, store):
    half = 0.5 * step_size
    slab = lax.broadcasted_iota(jnp.int32, (8, 128), 0)
    here = [visc(y, 0), visc(y, 1)]
    if with_rest:
        pair = half * (here[0] + here[1])
        up = jnp.where(slab < 7, pltpu.roll(here[0], 7, 0), 0.0)
        down = jnp.where(slab > 0, pltpu.roll(here[1], 1, 0), 0.0)
        crosses = (half * (here[0] + down), half * (here[1] + up))
    for i in range(2):
        v, nxt = here[i], visc(y + 1, i)
        inside = v > 0.0
        to_next = half * (v + nxt)
        store(1, y, i, jnp.where(inside & (nxt > 0.0), to_next, 0.0))
        if with_rest:
            z_next = half * (v + lane_next(v))
            z_prev = lane_prev(z_next)
            total = to_next + half * (v + visc(y - 1, i)) + pair + crosses[i] + z_next + z_prev
            wall = slab == (0 if i == 0 else 7)
            store(0, y, i, jnp.where(inside, 1.0 - total, 0.0))
            store(2, y, i, jnp.where(inside, pair, 0.0))
            store(3, y, i, jnp.where(inside & ~wall, crosses[i], 0.0))
            store(4, y, i, jnp.where(inside, z_next, 0.0))
            store(5, y, i, jnp.where(inside, z_prev, 0.0))


def own_coefs_kernel(pieces, blocks, main, coefs):
    own = 8 * pieces
    read = reader(main, None, None, (0,) * blocks, pieces)
    cache = {}

    def visc(y, i):
        if (y, i) not in cache:
            cache[y, i] = read(0, y, i)
        return cache[y, i]

    def store(c, y, i, value):
        coefs[c, y - SIDE, i] = value

    for y in range(SIDE + 1, SIDE + own - 1):
        row_coefs(visc, y, True, store)


def edge_coefs(edge_visc, pieces, edge):
    own = 8 * pieces
    cache = {}

    def visc(y, i):
        if (y, i) not in cache:
            cache[y, i] = edge_visc[y if y <= SIDE + 1 else y - own + 4, i]
        return cache[y, i]

    def store(c, y, i, value):
        edge[c, y if y <= SIDE else y - own + 2, i] = value

    for y in range(0, SIDE + 1):
        row_coefs(visc, y, y > 0, store)
    for y in range(SIDE + own - 1, 2 * SIDE + own - 1):
        row_coefs(visc, y, True, store)


def run_steps(read, blocks, fields, own_coefs, edge, pieces, snaps, records, last):
    own = 8 * pieces
    rows = own + 2 * SIDE

    def coef(c, y, i):
        if SIDE < y < SIDE + own - 1:
            return own_coefs[c, y - SIDE, i]
        return edge[c, y if y <= SIDE else y - own + 2, i]

    def diffuse(source, dest, low, high):
        for base in range(low, high, ROWS):
            top = min(base + ROWS, high)
            u = {(y, i): source[y, i] for y in range(base - 1, top + 1) for i in range(2)}
            face = {(y, i): coef(1, y, i) for y in range(base - 1, top) for i in range(2)}
            for y in range(base, top):
                for i in range(2):
                    mine, other = u[y, i], u[y, 1 - i]
                    cross = pltpu.roll(other, 1 if i == 0 else 7, 0)
                    total = (coef(0, y, i) * mine + coef(2, y, i) * other) + (
                        face[y, i] * u[y + 1, i] + face[y - 1, i] * u[y - 1, i]
                    )
                    total = total + (
                        (coef(4, y, i) * lane_next(mine) + coef(5, y, i) * lane_prev(mine))
                        + coef(3, y, i) * cross
                    )
                    dest[y, i] = total

    done = 0
    for k in range(snaps):
        first = fields[0]
        if k:
            for y in range(done, rows - done):
                for i in range(2):
                    first[y, i] = first[y, i] + read(blocks[k], y, i)
        for step in range(STEPS):
            done += 1
            diffuse(fields[step % 2], fields[(step + 1) % 2], done, rows - done)
        for y in range(own):
            z, j = divmod(y, 8)
            for i in range(2):
                value = first[SIDE + y, i]
                records[pl.ds((z * snaps + k) * 16 + i * 8 + j, 8, stride=pieces * snaps * 16), :] = value
                if last is not None and k == snaps - 1:
                    last[y, i] = value


def first_kernel(
    pieces, heights, around, main, low, high, own_coefs, records, last, edge_visc, buf0, buf1, edge
):
    read = reader(main, low, high, heights, pieces)
    has_low = jnp.where(around[0] > 0, 1.0, 0.0)
    has_high = jnp.where(around[1] > 0, 1.0, 0.0)
    own = 8 * pieces
    for y in range(own + 2 * SIDE):
        for i in range(2):
            buf0[y, i] = read(1, y, i)
    for y in list(range(SIDE + 2)) + list(range(SIDE + own - 2, own + 2 * SIDE)):
        for i in range(2):
            value = read(0, y, i)
            if y < SIDE:
                value = value * has_low
            elif y >= SIDE + own:
                value = value * has_high
            edge_visc[y if y <= SIDE + 1 else y - own + 4, i] = value
    edge_coefs(edge_visc, pieces, edge)
    snaps = len(heights) - 1
    run_steps(read, range(1, snaps + 1), (buf0, buf1), own_coefs, edge, pieces, snaps, records, last)


def second_kernel(pieces, heights, main, low, high, start, start_low, start_high, own_coefs, edge_visc, records, buf0, buf1, edge):
    read = reader(main, low, high, heights, pieces)
    own = 8 * pieces
    for y in range(own + 2 * SIDE):
        for i in range(2):
            if y < SIDE:
                before = start_low[y, i]
            elif y >= SIDE + own:
                before = start_high[y - SIDE - own, i]
            else:
                before = start[y - SIDE, i]
            buf0[y, i] = before + read(0, y, i)
    edge_coefs(edge_visc, pieces, edge)
    snaps = len(heights)
    run_steps(read, range(snaps), (buf0, buf1), own_coefs, edge, pieces, snaps, records, None)


def own_coefs_of(main, pieces, blocks):
    return pl.pallas_call(
        functools.partial(own_coefs_kernel, pieces, blocks),
        out_shape=jax.ShapeDtypeStruct((6, 8 * pieces, 2, 8, 128), F32),
        in_specs=[VMEM],
        out_specs=VMEM,
        compiler_params=params(4),
        name="own_coefficients",
    )(main)


def buffers(pieces):
    return [pltpu.VMEM((8 * pieces + 2 * SIDE, 2, 8, 128), F32)] * 2 + [
        pltpu.VMEM((6, 2 * SIDE + 2, 2, 8, 128), F32),
    ]


def first_half(around, main, low, high, own_coefs, pieces, heights):
    snaps = len(heights) - 1
    return pl.pallas_call(
        functools.partial(first_kernel, pieces, heights),
        out_shape=(
            jax.ShapeDtypeStruct((8 * pieces * snaps * 16, 128), F32),
            jax.ShapeDtypeStruct((8 * pieces, 2, 8, 128), F32),
            jax.ShapeDtypeStruct((2 * SIDE + 4, 2, 8, 128), F32),
        ),
        in_specs=[SMEM] + [VMEM] * 4,
        out_specs=(VMEM,) * 3,
        scratch_shapes=buffers(pieces),
        compiler_params=params(5),
        name="diffuse_first",
    )(around, main, low, high, own_coefs)


def second_half(main, low, high, start, start_low, start_high, own_coefs, edge, pieces, heights):
    snaps = len(heights)
    return pl.pallas_call(
        functools.partial(second_kernel, pieces, heights),
        out_shape=jax.ShapeDtypeStruct((8 * pieces * snaps * 16, 128), F32),
        in_specs=[VMEM] * 8,
        out_specs=VMEM,
        scratch_shapes=buffers(pieces),
        compiler_params=params(5),
        name="diffuse_second",
    )(main, low, high, start, start_low, start_high, own_coefs, edge)


def edge_kernel(pieces, heights, main, last_rows, first_rows):
    blocks, rows = len(heights), sum(heights)
    for a in range(8):
        for i in range(2):
            at = (a * 2 + i) * rows
            for k, height in enumerate(heights):
                first = (a * pieces * blocks + k) * 16 + i * 8
                last = first + (pieces - 1) * blocks * 16
                first_rows[at : at + height, :] = main[first : first + height, :]
                last_rows[at : at + height, :] = main[last + 8 - height : last + 8, :]
                at += height


def edges_of(main, pieces, heights):
    return pl.pallas_call(
        functools.partial(edge_kernel, pieces, heights),
        out_shape=(jax.ShapeDtypeStruct((16 * sum(heights), 128), F32),) * 2,
        in_specs=[VMEM],
        out_specs=(VMEM,) * 2,
        compiler_params=params(4),
        name="edge_rows",
    )(main)


def opening_kernel(visc_from, start_from, forcing_from, out_to, visc, start, forcing, out, in_sems, out_sems):
    snaps, fields = forcing.shape[:2]
    arriving = [
        pltpu.make_async_copy(visc_from, visc, in_sems.at[snaps + 1]),
        pltpu.make_async_copy(start_from, start, in_sems.at[snaps]),
    ]
    arriving += [pltpu.make_async_copy(forcing_from.at[k], forcing.at[k], in_sems.at[k]) for k in range(snaps)]
    for copy in arriving:
        copy.start()
    leaving = [
        pltpu.make_async_copy(out.at[:, k], out_to.at[:, k], out_sems.at[k]) for k in range(snaps + 1)
    ]
    arriving[0].wait()
    value = visc[...]
    for f in range(fields):
        out[f, 0] = value
    leaving[0].start()
    arriving[1].wait()
    for k in range(snaps):
        arriving[2 + k].wait()
        for f in range(fields):
            value = forcing[k, f].astype(F32)
            out[f, k + 1] = value + start[f] if k == 0 else value
        leaving[k + 1].start()
    for copy in leaving:
        copy.wait()


def opening(visc, start, forcing, snaps):
    fields = start.shape[0]
    cells = start.shape[1:]
    return pl.pallas_call(
        opening_kernel,
        out_shape=jax.ShapeDtypeStruct((fields, snaps + 1) + cells, F32),
        in_specs=[HBM] * 3,
        out_specs=HBM,
        scratch_shapes=[
            pltpu.VMEM(cells, F32),
            pltpu.VMEM(start.shape, F32),
            pltpu.VMEM((snaps,) + forcing.shape[1:], forcing.dtype),
            pltpu.VMEM((fields, snaps + 1) + cells, F32),
            pltpu.SemaphoreType.DMA((snaps + 2,)),
            pltpu.SemaphoreType.DMA((snaps + 1,)),
        ],
        compiler_params=params(60),
        name="opening_blocks",
    )(visc, start, forcing)


def gram_kernel(fields, snaps, core, *refs):
    rec, before = refs[0], refs[1:-6]
    mine = refs[-6:-3]
    keep, send, gram = refs[-3:]
    for cell_row in range(16):
        for s in range(snaps):
            for f in range(0, fields, 16):
                parts = [
                    rec[pl.ds(((f + g) * snaps + s) * 16 + cell_row, 8, stride=snaps * 16), :]
                    for g in (0, 8)
                ]
                rest = jnp.concatenate(parts, 0)
                at = (slice(s * fields + f, s * fields + f + 16), slice(cell_row * 128, cell_row * 128 + 128))
                for term in mine:
                    piece = rest.astype(BF16)
                    term[at] = piece
                    rest = rest - piece.astype(F32)
    width = fields * snaps
    high, middle, low = (ref[...] for ref in mine)
    others = (before, mine) if before else (mine,)
    high_of, middle_of, low_of = (jnp.concatenate([group[t][...] for group in others], 0) for t in range(3))
    by_high = bf_dot(jnp.concatenate([high, middle, low], 0), high_of, NT)
    by_middle = bf_dot(jnp.concatenate([high, middle], 0), middle_of, NT)
    small = by_high[2 * width :] + by_middle[width:] + bf_dot(high, low_of, NT)
    gram[...] = by_high[:width] + (by_high[width : 2 * width] + by_middle[:width] + small)
    half = width // 2
    kept = core[0]
    keep[...] = gram[pl.ds(kept * half, half), :]
    send[...] = gram[pl.ds((1 - kept) * half, half), :]


def gram_of(core, rec, before, fields, snaps):
    width = fields * snaps
    cells = 2048
    columns = width * (2 if before else 1)
    return pl.pallas_call(
        functools.partial(gram_kernel, fields, snaps),
        out_shape=(jax.ShapeDtypeStruct((width, cells), BF16),) * 3
        + (jax.ShapeDtypeStruct((width // 2, columns), F32),) * 2,
        in_specs=[SMEM] + [VMEM] * (1 + len(before)),
        out_specs=(VMEM,) * 5,
        scratch_shapes=[pltpu.VMEM((width, columns), F32)],
        compiler_params=params(16),
        name="gram_blocks",
    )(core, rec, *before)


def rank_kernel(owner_count, owners, hot):
    own = owners[...]
    rows = own.shape[0]
    total = owner_count * rows
    stacked = jnp.concatenate(
        [jnp.where(own == o, 1.0, 0.0).astype(F32) for o in range(owner_count)], 0
    )
    ones = stacked.astype(BF16)
    before = lax.broadcasted_iota(jnp.int32, (128, 128), 0) < lax.broadcasted_iota(jnp.int32, (128, 128), 1)
    inner = bf_dot(ones, jnp.where(before, 1.0, 0.0).astype(BF16), NN)
    sums = bf_dot(ones, jnp.ones((128, 128), BF16), NN).astype(BF16)
    at = lax.broadcasted_iota(jnp.int32, (total, total), 0)
    of = lax.broadcasted_iota(jnp.int32, (total, total), 1)
    lower = (of < at) & (of // rows == at // rows)
    offset = bf_dot(jnp.where(lower, 1.0, 0.0).astype(BF16), sums, NN)
    picked = stacked * (inner + offset)
    rank = picked[0:rows]
    for o in range(1, owner_count):
        rank = rank + picked[o * rows : (o + 1) * rows]
    rank = rank.astype(jnp.int32)
    slot = lax.broadcasted_iota(jnp.int32, (hot.shape[0], 128), 0)
    for r in range(rows):
        hot[:, r * 128 : (r + 1) * 128] = jnp.where(slot == rank[r : r + 1, :], 1.0, 0.0).astype(BF16)


def rank_hot(owners, owner_count, capacity):
    return pl.pallas_call(
        functools.partial(rank_kernel, owner_count),
        out_shape=jax.ShapeDtypeStruct((capacity, owners.size), BF16),
        in_specs=[VMEM],
        out_specs=VMEM,
        compiler_params=params(),
        name="slot_ranks",
    )(owners)


GROUP = 4


def pack_kernel(first, owners, hot, high, low, *refs):
    out, picked = refs[-2:]
    width = high.shape[0]
    base = (first + pl.program_id(0)) * GROUP
    own = owners[...]
    rows = own.shape[0]
    for part, source in enumerate((high, low)):
        for g in range(GROUP):
            mask = jnp.where(own == base + g, 1.0, 0.0)
            for r in range(rows):
                cols = slice(r * 128, (r + 1) * 128)
                keep = jnp.broadcast_to(mask[r : r + 1, :], (width, 128)).astype(BF16)
                picked[part, g * width : (g + 1) * width, cols] = source[:, cols] * keep
    sums = bf_dot(hot[...], picked[0], NT) + bf_dot(hot[...], picked[1], NT)
    for g in range(GROUP):
        out[g] = sums[:, g * width : (g + 1) * width]


def pack(owners, hot, high, low, owner_count, half, slots=None, part=0, parts=1):
    width, cells = high.shape
    capacity = hot.shape[0]
    more = () if slots is None else (slots,)
    groups = owner_count // GROUP // parts
    first = part * groups
    return pl.pallas_call(
        functools.partial(pack_kernel, first),
        grid=(groups,),
        out_shape=jax.ShapeDtypeStruct((owner_count, capacity, 2 * width), F32),
        in_specs=[VMEM] * 4 + [HBM] * len(more),
        out_specs=pl.BlockSpec((GROUP, capacity, width), lambda g: (first + g, 0, half)),
        scratch_shapes=[pltpu.VMEM((2, GROUP * width, cells), BF16)],
        input_output_aliases={4: 0} if more else {},
        compiler_params=params(48),
        cost_estimate=pl.CostEstimate(
            flops=4 * GROUP * groups * capacity * width * cells,
            bytes_accessed=4 * GROUP * groups * capacity * width,
            transcendentals=0,
        ),
        name="pack_slots",
    )(owners, hot, high, low, *more)


BLOCK = 32


def eliminate(work, order):
    row_at = lax.broadcasted_iota(jnp.int32, (BLOCK, 128), 0)
    lane_at = lax.broadcasted_iota(jnp.int32, (BLOCK, 128), 1)
    for first in range(0, order, BLOCK):
        tile, inner = divmod(first, 128)
        tile *= 128
        on_diag = lane_at == row_at + inner
        part = work[first : first + BLOCK, tile : tile + 128]
        unit = jnp.where(on_diag, 1.0, 0.0)
        for k in range(BLOCK):
            column = part[:, inner + k : inner + k + 1]
            factor = jnp.where(row_at > k, column * (1.0 / part[k : k + 1, inner + k : inner + k + 1]), 0.0)
            unit = unit - factor * unit[k : k + 1, :]
            part = part - factor * part[k : k + 1, :]
        pivots = jnp.sum(jnp.where(on_diag, part, 0.0), axis=1, keepdims=True)
        unit = unit / jnp.sqrt(pivots)
        solved = exact_dot(unit, work[tile : tile + 128, :], NN)
        work[first : first + BLOCK, :] = solved
        if first + BLOCK < order:
            change = exact_dot(solved[:, 0:order], solved, TN)
            work[first + BLOCK :, :] = work[first + BLOCK :, :] - change[first + BLOCK :, :]


def identity(order):
    at = lax.broadcasted_iota(jnp.int32, (order, order), 0)
    return jnp.where(at == lax.broadcasted_iota(jnp.int32, (order, order), 1), 1.0, 0.0)


def upper(value):
    at = lax.broadcasted_iota(jnp.int32, value.shape, 0)
    return jnp.where(at <= lax.broadcasted_iota(jnp.int32, value.shape, 1), value, 0.0)


def joined(core, own, other, whole, width):
    half = own.shape[0]
    mine = core[0]
    whole[pl.ds(mine * half, half), 0:width] = own[...]
    whole[pl.ds((1 - mine) * half, half), 0:width] = other[...]


def lead_kernel(core, own, other, r_out, inv_out, work):
    order = 2 * own.shape[0]
    joined(core, own, other, work, order)
    work[:, order:] = identity(order)
    eliminate(work, order)
    r_out[...] = upper(work[:, 0:order])
    inv_out[...] = work[:, order:]


def trail_kernel(core, own_half, other_half, lead, lead_inv, r_out, inv_out, work, gram):
    order = lead.shape[0]
    joined(core, own_half, other_half, gram, 2 * order)
    inverse = lead_inv[...]
    cross = exact_dot(inverse, gram[:, 0:order], NT)
    work[:, 0:order] = gram[:, order:] - exact_dot(cross, cross, TN)
    work[:, order:] = identity(order)
    eliminate(work, order)
    zeros = jnp.zeros((order, order), F32)
    own = work[:, order:]
    r_out[0:order, 0:order] = lead[...]
    r_out[0:order, order:] = cross
    r_out[order:, 0:order] = zeros
    r_out[order:, order:] = upper(work[:, 0:order])
    inv_out[0:order, 0:order] = inverse
    inv_out[0:order, order:] = zeros
    inv_out[order:, 0:order] = -exact_dot(own, exact_dot(cross, inverse, TN), NN)
    inv_out[order:, order:] = own


def factor_lead(core, own, other):
    order = 2 * own.shape[0]
    return pl.pallas_call(
        lead_kernel,
        out_shape=(jax.ShapeDtypeStruct((order, order), F32),) * 2,
        in_specs=[SMEM, VMEM, VMEM],
        out_specs=(VMEM,) * 2,
        scratch_shapes=[pltpu.VMEM((order, 2 * order), F32)],
        compiler_params=params(),
        name="factor_lead",
    )(core, own, other)


def factor_trail(core, own, other, lead, lead_inv):
    order = lead.shape[0]
    return pl.pallas_call(
        trail_kernel,
        out_shape=(jax.ShapeDtypeStruct((2 * order, 2 * order), F32),) * 2,
        in_specs=[SMEM] + [VMEM] * 4,
        out_specs=(VMEM,) * 2,
        scratch_shapes=[pltpu.VMEM((order, 2 * order), F32)] * 2,
        compiler_params=params(),
        name="factor_trail",
    )(core, own, other, lead, lead_inv)


SOURCES = 8


def basis_kernel(inverse, panel, out):
    inv_high, inv_low = split(inverse[...])
    for b in range(SOURCES):
        high, low = split(panel[b])
        rows = high.shape[0]
        out[b * rows : (b + 1) * rows, :] = bf_dot(high, inv_high, NT) + (
            bf_dot(high, inv_low, NT) + bf_dot(low, inv_high, NT)
        )


def basis_of(inverse, panel):
    sources, capacity, order = panel.shape
    return pl.pallas_call(
        basis_kernel,
        grid=(sources // SOURCES,),
        out_shape=jax.ShapeDtypeStruct((sources * capacity, order), F32),
        in_specs=[
            pl.BlockSpec((order, order), lambda b: (0, 0)),
            pl.BlockSpec((SOURCES, capacity, order), lambda b: (b, 0, 0)),
        ],
        out_specs=pl.BlockSpec((SOURCES * capacity, order), lambda b: (b, 0)),
        compiler_params=params(48),
        name="basis_rows",
    )(inverse, panel)


def ring(size, shift):
    return [(i, (i + shift) % size) for i in range(size)]


def swapped(value):
    return lax.ppermute(value, "core", [(0, 1), (1, 0)])


def summed(value, axis, masks):
    size = lax.axis_size(axis)
    for mask in masks:
        value = value + lax.ppermute(value, axis, [(i, i ^ mask) for i in range(size)])
    return value


def on_device(state_start, viscosity, forcing, target):
    fields, wide, deep, lanes = state_start.shape
    x_size, pieces = lax.axis_size("x"), lax.axis_size("z")
    owner_count = x_size * pieces
    plane = ("y", "core", "z")
    capacity = 2 * viscosity.size // owner_count
    owners = target.reshape(wide * deep, lanes)

    def swap(value):
        return lax.all_to_all(value, plane, split_axis=0, concat_axis=0, tiled=True)

    x_at = lax.axis_index("x")
    around = jnp.stack([x_at > 0, x_at < x_size - 1]).astype(jnp.int32)
    heights = tuple(SIDE - STEPS * k for k in range(HALF))

    def shared(value, heights):
        last, first = edges_of(value, pieces, heights)
        return lax.ppermute(last, "x", ring(x_size, 1)), lax.ppermute(first, "x", ring(x_size, -1))

    one = swap(opening(viscosity, state_start, forcing, HALF)).reshape(-1, lanes)
    later = jnp.transpose(forcing[HALF:], (1, 0, 2, 3, 4)).astype(F32)
    two = swap(later).reshape(-1, lanes)
    with_visc = (SIDE,) + heights
    low_one, high_one = shared(one, with_visc)
    own_coefs = own_coefs_of(one, pieces, len(with_visc))
    records_one, middle, edge = first_half(around, one, low_one, high_one, own_coefs, pieces, with_visc)
    low_two, high_two = shared(two, heights)
    middle_low = lax.ppermute(middle[-SIDE:], "x", ring(x_size, 1))
    middle_high = lax.ppermute(middle[:SIDE], "x", ring(x_size, -1))
    records_two = second_half(
        two, low_two, high_two, middle, middle_low, middle_high, own_coefs, edge, pieces, heights
    )
    block = (fields, HALF, wide, deep, lanes)
    home_one = swap(records_one.reshape(block))
    home_two = swap(records_two.reshape(block))
    hot = rank_hot(owners, owner_count, capacity)
    core = lax.axis_index("core").astype(jnp.int32).reshape(1)
    both = (1, 3)
    *terms_a, keep_a, send_a = gram_of(core, home_one.reshape(-1, lanes), (), fields, HALF)
    high_a, low_a = terms_a[:2]
    part_a = summed(keep_a + swapped(send_a), "x", both)
    slots = pack(owners, hot, high_a, low_a, owner_count, 0)
    home_two, slots, part_a = lax.optimization_barrier((home_two, slots, part_a))
    high_b, low_b, _, keep_b, send_b = gram_of(core, home_two.reshape(-1, lanes), terms_a, fields, HALF)
    quarters = 4

    def packed(slots, part, *values):
        slots = pack(owners, hot, high_b, low_b, owner_count, 1, slots, part, quarters)
        return lax.optimization_barrier((slots,) + values)

    part_b = summed(keep_b + swapped(send_b), "x", (1,))
    slots, part_a, part_b = packed(slots, 0, part_a, part_b)
    part = summed(jnp.concatenate([part_a, part_b], 1), "z", (1,))
    slots, part = packed(slots, 1, part)
    width = fields * HALF
    part_a, part_b = part[:, :width], summed(part[:, width:], "x", (3,))
    slots, part_a, part_b = packed(slots, 2, part_a, part_b)
    part = summed(jnp.concatenate([part_a, part_b], 1), "z", (3,))
    slots, part = packed(slots, 3, part)
    panel = lax.all_to_all(slots, ("x", "z"), split_axis=0, concat_axis=0, tiled=True)
    part = summed(part, "y", both)
    other = swapped(part)
    lead, lead_inv = factor_lead(core, part[:, :width], other[:, :width])
    r_factor, inverse = factor_trail(core, part[:, width:], other[:, width:], lead, lead_inv)
    basis = basis_of(inverse, panel)
    return home_two[:, HALF - 1], r_factor, basis


def solution(mesh):
    slab_size, row_size = mesh.shape["slab"], mesh.shape["row"]
    cores, z_size = 2, 4
    axes = (slab_size // cores, cores, row_size // z_size, z_size)
    cut = Mesh(mesh.devices.reshape(axes), ("y", "core", "x", "z"))
    slab, row = ("y", "core"), ("x", "z")
    placed = (
        P(None, slab, row, None),
        P(slab, row, None),
        P(None, None, slab, row, None),
        P(slab, row, None, None),
    )
    return jax.shard_map(
        on_device,
        mesh=cut,
        in_specs=placed,
        out_specs=(P(None, slab, row, None), P(), P(slab + row, None)),
        check_vma=False,
    )
```
